256 devices in a mesh: dp: 4 (over z_hi, core), tm: 4 (over z_lo), height: 16 (over x, y).
Axes of the slice: x: 4, y: 4, z: 8 (z_hi: 2, z_lo: 4; z = z_hi * 4 + z_lo), core: 2. Of those that a mesh axis runs over, the one named last changes fastest.
Arguments:
- vit_cot: bfloat16 [4, 64, 256, 1280], P('dp', ('tm', 'height')), may hold values from -6 to 6
- vit_pre: bfloat16 [4, 64, 256, 1280], P('dp', ('tm', 'height')), may hold values from -6 to 6
- ln_gain: bfloat16 [1280], replicated, may hold values from 0.099609375 to 1.8984375
- patch_w: bfloat16 [588, 1280], replicated, may hold values from -0.25 to 0.25
- frame_owner: int32 [64], replicated, may hold values from 0 to 15, as said below
- conv_w: bfloat16 [81, 128], replicated, may hold values from -0.625 to 0.625
- join_w: bfloat16 [512, 3072], replicated, may hold values from -0.25 to 0.25
- token_order: int32 [16, 256], P('height', 'tm'), may hold values from 0 to 63, as said below
- queries: bfloat16 [4, 4096, 1536], P('dp', 'height', 'tm'), may hold values from -28 to 28
- keys: bfloat16 [4, 4096, 1536], P('dp', 'height', 'tm'), may hold values from -13 to 13
- values: bfloat16 [4, 4096, 1536], P('dp', 'height', 'tm'), may hold values from -6 to 6
- attn_out: bfloat16 [4, 4096, 1536], P('dp', 'height', 'tm'), may hold values from -6 to 6
- out_w: bfloat16 [1536, 3072], P('tm'), may hold values from -0.15625 to 0.15625
Outputs:
- query_grad: bfloat16 [4, 4096, 1536], P('dp', 'height', 'tm')
- key_grad: bfloat16 [4, 4096, 1536], P('dp', 'height', 'tm')
- value_grad: bfloat16 [4, 4096, 1536], P('dp', 'height', 'tm')
- weight_grad: float32 [3072, 1536], P(('dp', 'height'), 'tm')
The draws below stay inside these ranges and needn't reach their ends.
Inputs may be any that keep to these rules, and one draw needn't show every extreme that they name: `frame_owner`: each aligned block of 16 entries holds every number of 0 to 15 once. `token_order`: each aligned block of 64 entries of a row holds every number of 0 to 63 once.
All inputs are finite; a program needn't handle non-finite values.
Results may differ from the reference program's by a relative error of at most 0.022.
Values may be sent and summed in bfloat16 or wider, within the bound.
No kernel may reach another device: no remote copies, remote signals or barrier semaphores. Data moves between devices by JAX's collectives and lax.ppermute only.
A program may use at most 128 MiB of HBM per device.

```python
import math
import jax
import jax.numpy as jnp
from jax import lax

D = 3072
HEADS = 12
HDIM = 128
VW = 1280
CH = 128
IMG = 224
PATCH = 14
PW = 56
CLIPS = 4
SLAB_FRAMES = 16
FRAMES = 64
ROWS = 14
NP = 256
TOK_DEV = 64
TOKENS = 4096
HD = 1536
N_TM = 4
N_HEIGHT = 16


def block_permutation(key, block_count, width):
    scores = jax.random.randint(key, (block_count, width), 0, 1 << 20) * width + jnp.arange(width, dtype=jnp.int32)[None, :]
    return jnp.argsort(scores, axis=1).astype(jnp.int32).reshape(-1)


def draw_frame_owner(key, part):
    key = jax.random.fold_in(key, 2)
    return block_permutation(key, FRAMES // SLAB_FRAMES, SLAB_FRAMES)


def draw_token_order(key, part):
    key = jax.random.fold_in(key, 3)
    return block_permutation(key, TOKENS // TOK_DEV, TOK_DEV).reshape(N_HEIGHT, N_TM * TOK_DEV)


def draw_keys(key, part):
    key = jax.random.fold_in(key, 4)
    own = jnp.clip(jax.random.normal(key, (CLIPS, TOKENS, HD), jnp.float32), -4.0, 4.0)
    return own.astype(jnp.bfloat16)


def draw_queries(key, part):
    key = jax.random.fold_in(key, 5)
    own = jnp.clip(jax.random.normal(key, (CLIPS, TOKENS, HD), jnp.float32), -4.0, 4.0)
    return own.astype(jnp.bfloat16)


def block_scale(key, dims, split, least, top_value):
    level, own = 1.0, jax.random.fold_in(key, 6)
    for axis_at, parts in split:
        heights = jnp.exp(jax.random.uniform(jax.random.fold_in(own, axis_at), (parts,), jnp.float32, least / len(split), top_value / len(split)))
        level = level * jnp.repeat(heights, dims[axis_at] // parts).reshape([-1 if axis == axis_at else 1 for axis in range(len(dims))])
    return level


def gaussian(own_key, shape, scale, limit, cuts=(), kind=jnp.bfloat16):
    values = jax.random.normal(own_key, shape, jnp.float32) * scale
    if len(cuts) > 0:
        values = block_scale(own_key, shape, cuts, -0.22, 0.18) * values
    return jnp.clip(values, min=-limit, max=limit).astype(kind)


def setup_inputs(seed: int = 0) -> dict:
    arg_keys = jax.random.split(jax.random.key(seed), 14)
    vit_cot = gaussian(arg_keys[0], (CLIPS, FRAMES, NP, VW), 1.0, 6.0, ((0, 4), (1, 64)))
    vit_pre = gaussian(arg_keys[1], (CLIPS, FRAMES, NP, VW), 1.0, 6.0, ((0, 4), (1, 64)))
    ln_gain = jnp.clip(1.0 + 0.18 * jax.random.normal(arg_keys[2], (VW,), jnp.float32), 0.099609375, 1.8984375).astype(jnp.bfloat16)
    patch_w = gaussian(arg_keys[3], (3 * PATCH * PATCH, VW), (3 * PATCH * PATCH) ** -0.5, 0.25)
    frame_owner = draw_frame_owner(jax.random.fold_in(arg_keys[13], 71), 0)
    conv_w = gaussian(arg_keys[5], (81, CH), 81 ** -0.5, 0.625)
    join_w = gaussian(arg_keys[6], (4 * CH, D), (4 * CH) ** -0.5, 0.25)
    token_order = draw_token_order(jax.random.fold_in(arg_keys[13], 71), 0)
    queries = draw_queries(jax.random.fold_in(arg_keys[13], 71), 0)
    keys = draw_keys(jax.random.fold_in(arg_keys[13], 71), 0)
    values = gaussian(arg_keys[10], (CLIPS, TOKENS, HD), 1.0, 6.0, ((0, 4), (1, 16), (2, 4)))
    attn_out = gaussian(arg_keys[11], (CLIPS, TOKENS, HD), 1.0, 6.0, ((0, 4), (1, 16), (2, 4)))
    out_w = gaussian(arg_keys[12], (HD, D), HD ** -0.5, 0.15625, ((0, 4),))
    return dict(vit_cot=vit_cot, vit_pre=vit_pre, ln_gain=ln_gain, patch_w=patch_w, frame_owner=frame_owner, conv_w=conv_w, join_w=join_w, token_order=token_order, queries=queries, keys=keys, values=values, attn_out=attn_out, out_w=out_w)


epsilon = 1e-05
pixel_std = (0.26862954, 0.26130258, 0.27577711)

def norm_backward(cotangent, inputs, gain):
    values32 = inputs.astype(jnp.float32)
    centered = values32 - lax.optimization_barrier(jnp.mean(values32, axis=-1, keepdims=True))
    inverse = lax.rsqrt(lax.optimization_barrier(jnp.mean(centered * centered, axis=-1, keepdims=True)) + epsilon)
    normed = centered * inverse
    scaled = cotangent.astype(jnp.float32) * gain.astype(jnp.float32)
    return inverse * (scaled - lax.optimization_barrier(jnp.mean(scaled, axis=-1, keepdims=True)) - normed * lax.optimization_barrier(jnp.mean(scaled * normed, axis=-1, keepdims=True)))

def patch_pixels(grad_rows, patch_w):
    flattened = jnp.dot(grad_rows, patch_w.T, preferred_element_type=jnp.float32)
    patches = flattened.reshape(flattened.shape[0], 3, PATCH, PATCH)
    deviation = jnp.array(pixel_std, dtype=jnp.float32)
    return patches / deviation[None, :, None, None]

def frame_image(cotangent, inputs, gain, patch_w):
    grad_rows = norm_backward(cotangent, inputs, gain).astype(jnp.bfloat16)
    patches = patch_pixels(grad_rows, patch_w)
    side_count = IMG // PATCH
    picture = patches.reshape(side_count, side_count, 3, PATCH, PATCH).transpose(2, 0, 3, 1, 4)
    return picture.reshape(3, IMG, IMG).astype(jnp.bfloat16)

def conv_adjoint(padded, conv_w, frame_count, row_count, col_count):
    shifted = [padded[:, shift_t:shift_t + frame_count, shift_r:shift_r + row_count, shift_c:shift_c + col_count] for shift_t in range(3) for shift_r in range(3) for shift_c in range(3)]
    stacked = jnp.stack(shifted, axis=0).reshape(81, frame_count * row_count * col_count)
    return lax.dot_general(stacked, conv_w, (((0,), (0,)), ((), ())), preferred_element_type=jnp.float32)

def pool_tokens(cell_grads, frame_count, row_count, col_count):
    channels = cell_grads.shape[-1]
    pooled_grid = cell_grads.reshape(frame_count, row_count // PATCH, 2, PATCH // 2, col_count // PW, 2, PW // 2, channels)
    quarter_means = lax.optimization_barrier(jnp.mean(pooled_grid, axis=(3, 6)))
    ordered = quarter_means.transpose(0, 1, 3, 2, 4, 5)
    return ordered.reshape(frame_count * (row_count // PATCH) * (col_count // PW), 4 * channels).astype(jnp.bfloat16)

def head_grads(operands):
    query_rows, key_rows, value_rows, output_rows, grad_rows = operands
    score_scale = HDIM ** (-0.5)
    scores = jnp.dot(query_rows, key_rows.T, preferred_element_type=jnp.float32) * score_scale
    log_totals = jax.nn.logsumexp(scores, axis=-1)
    weights = jnp.exp(scores - log_totals[:, None])
    mixed_grads = jnp.dot(grad_rows, value_rows.T, preferred_element_type=jnp.float32)
    row_dots = lax.optimization_barrier(jnp.sum(grad_rows.astype(jnp.float32) * output_rows.astype(jnp.float32), axis=-1))
    dscore = (weights * (mixed_grads - row_dots[:, None])).astype(jnp.bfloat16)
    query_acc = jnp.dot(dscore, key_rows, preferred_element_type=jnp.float32) * score_scale
    key_acc = jnp.dot(dscore.T, query_rows, preferred_element_type=jnp.float32) * score_scale
    value_acc = jnp.dot(weights.astype(jnp.bfloat16).T, grad_rows, preferred_element_type=jnp.float32)
    return (query_acc, key_acc, value_acc)

def split_heads(matrix):
    return matrix.reshape(TOKENS, HEADS, HDIM).transpose(1, 0, 2)

def reference(vit_cot, vit_pre, ln_gain, patch_w, frame_owner, conv_w, join_w, token_order, queries, keys, values, attn_out, out_w):
    slot_index = jnp.arange(FRAMES, dtype=jnp.int32) // SLAB_FRAMES * SLAB_FRAMES + frame_owner.astype(jnp.int32)
    order_flat = token_order.reshape(TOKENS).astype(jnp.int32)
    token_index = jnp.arange(TOKENS, dtype=jnp.int32) // TOK_DEV * TOK_DEV + order_flat
    patch_rows = ROWS // PATCH
    patch_cols = IMG // PW
    root = math.sqrt(TOKENS)
    weight_grad = jnp.zeros((D, HD), jnp.float32)
    query_list = []
    key_list = []
    value_list = []

    def merge_heads(grads):
        return (grads * root).transpose(1, 0, 2).reshape(TOKENS, HD).astype(jnp.bfloat16)
    for clip_index in range(CLIPS):

        def one_image(operands):
            return frame_image(operands[0], operands[1], ln_gain, patch_w)
        images = lax.map(one_image, (vit_cot[clip_index], vit_pre[clip_index]))
        pixels = jnp.take(images, slot_index, axis=0).transpose(1, 0, 2, 3)
        padded = jnp.pad(pixels, ((0, 0), (1, 1), (1, 1), (1, 1)))

        def frame_tokens(frame):
            window = lax.dynamic_slice_in_dim(padded, frame, 3, 1)
            return pool_tokens(conv_adjoint(window, conv_w, 1, IMG, IMG), 1, IMG, IMG)
        pooled = lax.map(frame_tokens, jnp.arange(FRAMES, dtype=jnp.int32))
        pooled = pooled.reshape(N_TM, SLAB_FRAMES, N_HEIGHT, patch_rows, patch_cols, 4 * CH)
        pooled = pooled.transpose(2, 0, 1, 3, 4, 5).reshape(TOKENS, 4 * CH)
        patch_grads = jnp.dot(pooled, join_w, preferred_element_type=jnp.float32).astype(jnp.bfloat16)
        token_grads = jnp.take(patch_grads, token_index, axis=0)
        grad_out = jnp.dot(token_grads, out_w.T, preferred_element_type=jnp.float32).astype(jnp.bfloat16)
        query_acc, key_acc, value_acc = lax.map(head_grads, (split_heads(queries[clip_index]), split_heads(keys[clip_index]), split_heads(values[clip_index]), split_heads(attn_out[clip_index]), split_heads(grad_out)))
        query_list.append(merge_heads(query_acc))
        key_list.append(merge_heads(key_acc))
        value_list.append(merge_heads(value_acc))
        weight_grad = weight_grad + jnp.dot(token_grads.T, attn_out[clip_index], preferred_element_type=jnp.float32)
    weight_grad = weight_grad / math.sqrt(TOKENS * CLIPS)
    return (jnp.stack(query_list), jnp.stack(key_list), jnp.stack(value_list), weight_grad)
```

```python
import functools
import math

import jax
import jax.numpy as jnp
import numpy as np
from jax import lax
from jax.experimental import pallas as pl
from jax.experimental.pallas import tpu as pltpu
from jax.sharding import Mesh
from jax.sharding import PartitionSpec as P

HDIM = 128
IMG = 224
PATCH = 14
SIDE = IMG // PATCH
GRID = 4
HEADS_HERE = 3
ROWS_HERE = 256
FEATS = HEADS_HERE * HDIM
BLOCK = GRID * ROWS_HERE
FRAMES = 64
LANES = 128
QUARTERS = 4
QUARTER_LANES = 32
TAPS = 27
ORDER_LANE = TAPS
QUARTER_CELLS = (PATCH // 2) * (2 * PATCH)

epsilon = 1e-05
pixel_std = (0.26862954, 0.26130258, 0.27577711)

f32 = jnp.float32
bf16 = jnp.bfloat16
VMEM_LIMIT = 56 * 1024 * 1024
HIGHEST = lax.Precision.HIGHEST
LOG2E = math.log2(math.e)
SCORE_SCALE = HDIM ** (-0.5)


def row_masks():
    masks = np.zeros((8, PATCH), np.float32)
    for half in range(2):
        for shift in range(3):
            low = half * 7 + shift - 1
            masks[half * 3 + shift, max(low, 0) : min(low + 7, PATCH)] = 1
    masks[6, 0] = 1
    masks[7, PATCH - 1] = 1
    return masks


def basis_matrix():
    rows = row_masks()
    columns = np.zeros((3, PATCH), np.float32)
    columns[0] = 1
    columns[1, 0] = 1
    columns[2, PATCH - 1] = 1
    basis = np.zeros((LANES, 3, PATCH, PATCH), np.float32)
    for col in range(3):
        for row in range(8):
            for channel in range(3):
                basis[col * 24 + row * 3 + channel, channel] = np.outer(rows[row], columns[col])
    return basis.reshape(LANES, 3 * PATCH * PATCH)


def basis_scale():
    scale = np.zeros((LANES, 1), np.float32)
    for lane in range(72):
        scale[lane, 0] = 1.0 / (pixel_std[lane % 3] * QUARTER_CELLS)
    return scale


def spread_matrix():
    spread = np.zeros((6, LANES, LANES), np.float32)
    for half in range(2):
        for side in range(2):
            first = 2 * side + 1
            terms = {
                0: [(first - 1, 2, 1), (first, 0, 1), (first + 1, 0, 1), (first + 1, 2, -1)],
                1: [(first, 0, 1), (first + 1, 0, 1)],
                2: [(first, 0, 1), (first, 1, -1), (first + 1, 0, 1), (first + 2, 1, 1)],
            }
            for shift in range(3):
                groups = [half * 3 + shift]
                if (half, shift) == (0, 0):
                    groups.append(7)
                if (half, shift) == (1, 2):
                    groups.append(6)
                for offset in range(3):
                    for channel in range(3):
                        lane = (half * 2 + side) * QUARTER_LANES + (shift * 3 + offset) * 3 + channel
                        for place, col, sign in terms[offset]:
                            for row in groups:
                                spread[place, col * 24 + row * 3 + channel, lane] += sign
    return spread.reshape(6 * LANES, LANES)


def window_kernel(
    cot_ref, pre_ref, gain_ref, patch_ref, basis_ref, scale_ref, spread_ref, order_ref, out_ref, sums
):
    pre = pre_ref[...].astype(f32)
    centered = pre - jnp.mean(pre, axis=-1, keepdims=True)
    inverse = lax.rsqrt(jnp.mean(centered * centered, axis=-1, keepdims=True) + epsilon)
    normed = centered * inverse
    scaled = cot_ref[...].astype(f32) * gain_ref[...].astype(f32)
    grad_rows = inverse * (
        scaled
        - jnp.mean(scaled, axis=-1, keepdims=True)
        - normed * jnp.mean(scaled * normed, axis=-1, keepdims=True)
    )
    grad_rows = grad_rows.astype(bf16)
    weights = (
        jnp.dot(basis_ref[...], patch_ref[...], preferred_element_type=f32) * scale_ref[...]
    )
    high = weights.astype(bf16)
    low = (weights - high.astype(f32)).astype(bf16)
    both = lax.dot_general(
        grad_rows,
        jnp.concatenate([high, low], axis=0),
        (((1,), (1,)), ((), ())),
        preferred_element_type=f32,
    )
    patch_sums = both[:, :LANES] + both[:, LANES:]
    group = (lax.broadcasted_iota(jnp.int32, (SIDE * SIDE, LANES), 1) // 3) % 8
    edge = jnp.zeros((SIDE, LANES), f32)
    above = jnp.concatenate([edge, patch_sums[:-SIDE]], axis=0)
    below = jnp.concatenate([patch_sums[SIDE:], edge], axis=0)
    patch_sums = jnp.where(group == 7, above, jnp.where(group == 6, below, patch_sums))
    sums[pl.ds(0, 8), :] = jnp.zeros((8, LANES), f32)
    sums[pl.ds(8 + SIDE * SIDE, 8), :] = jnp.zeros((8, LANES), f32)
    sums[pl.ds(8, SIDE * SIDE), :] = patch_sums
    column = lax.broadcasted_iota(jnp.int32, (SIDE * GRID, LANES), 0) % GRID
    total = jnp.zeros((SIDE * GRID, LANES), f32)
    for place in range(6):
        picked = sums[pl.ds(7 + place, SIDE * GRID, stride=GRID), :]
        if place == 0:
            picked = jnp.where(column == 0, 0.0, picked)
        if place == 5:
            picked = jnp.where(column == GRID - 1, 0.0, picked)
        total = total + jnp.dot(
            picked,
            spread_ref[pl.ds(place * LANES, LANES), :],
            preferred_element_type=f32,
            precision=HIGHEST,
        )
    windows = total.astype(bf16)
    for target_x in range(GRID):
        block = windows[target_x * 16 : (target_x + 1) * 16] + order_ref[...]
        for target_t in range(GRID):
            for target_y in range(GRID):
                out_ref[(target_t * GRID + target_x) * GRID + target_y] = block


def token_kernel(
    place_ref, owner_ref, recv_ref, conv_ref, joint_ref, *refs
):
    out_refs, (grad_ref, dots_ref, outer_ref, frames, conv_big, ordered) = refs[:GRID], refs[GRID:]
    here_x = place_ref[0]
    here_y = place_ref[1]
    frames[0] = jnp.zeros((16, LANES), bf16)
    frames[FRAMES + 1] = jnp.zeros((16, LANES), bf16)

    def fetch(frame, carry):
        frames[frame + 1] = recv_ref[(frame // 16) * 16 + owner_ref[frame]]
        return carry

    lax.fori_loop(0, FRAMES, fetch, 0, unroll=8)
    conv_big[...] = jnp.zeros_like(conv_big)
    for quarter in range(QUARTERS):
        for shift in range(3):
            conv_big[
                pl.ds(shift * LANES + quarter * QUARTER_LANES, QUARTER_LANES),
                pl.ds(quarter * LANES, LANES),
            ] = conv_ref[shift]
    lane = lax.broadcasted_iota(jnp.int32, (16, ROWS_HERE), 1)
    for slab_t in range(GRID):
        pooled = jnp.zeros((ROWS_HERE, QUARTERS * LANES), f32)
        for shift in range(3):
            window = frames[pl.ds(slab_t * 16 + shift, 16)].reshape(ROWS_HERE, LANES)
            pooled = pooled + jnp.dot(
                window, conv_big[pl.ds(shift * LANES, LANES), :], preferred_element_type=f32
            )
        pooled = pooled.astype(bf16)
        pieces = []
        for piece in range(GRID):
            slab = lax.rem(here_y + piece, GRID)
            block = recv_ref[slab_t * 16 + here_x * GRID + slab].astype(f32)
            for part in range(4):
                order = block[:, ORDER_LANE + part : ORDER_LANE + part + 1].astype(jnp.int32)
                target = (order // 4) * 16 + slab * 4 + lax.rem(order, 4)
                pieces.append(jnp.where(lane == target, 1.0, 0.0).astype(bf16))
        chosen = jnp.dot(
            jnp.concatenate(pieces, axis=0), pooled, preferred_element_type=f32
        ).astype(bf16)
        for piece in range(GRID):
            ordered[pl.ds(piece * ROWS_HERE + slab_t * 64, 64), :] = chosen[
                piece * 64 : (piece + 1) * 64
            ]
    outer = jnp.zeros((QUARTERS * LANES, FEATS), f32)
    ones = jnp.ones((8, HDIM), f32)
    for piece in range(GRID):
        rows = ordered[pl.ds(piece * ROWS_HERE, ROWS_HERE), :]
        grads = jnp.dot(rows, joint_ref[...], preferred_element_type=f32).astype(bf16)
        grad_ref[piece] = grads
        outs = out_refs[piece][...]
        products = grads.astype(f32) * outs.astype(f32)
        for head in range(HEADS_HERE):
            dots = lax.dot_general(
                ones,
                products[:, head * HDIM : (head + 1) * HDIM],
                (((1,), (1,)), ((), ())),
                preferred_element_type=f32,
                precision=HIGHEST,
            )
            dots_ref[head, :, pl.ds(piece * ROWS_HERE, ROWS_HERE)] = dots
        outer = outer + lax.dot_general(
            rows, outs, (((0,), (0,)), ((), ())), preferred_element_type=f32
        )
    outer_ref[...] = outer.astype(bf16)


def totals_kernel(*refs):
    query_refs, key_refs, out_ref = refs[:GRID], refs[GRID : 2 * GRID], refs[2 * GRID]

    def one_head(head, carry):
        columns = pl.ds(pl.multiple_of(head * HDIM, HDIM), HDIM)
        for piece in range(GRID):
            query = query_refs[piece][:, columns]
            scores = [
                lax.dot_general(
                    key_ref[:, columns],
                    query,
                    (((1,), (1,)), ((), ())),
                    preferred_element_type=f32,
                )
                for key_ref in key_refs
            ]
            top = functools.reduce(
                jnp.maximum, [jnp.max(tile, axis=0, keepdims=True) for tile in scores]
            )
            shifted = top * (SCORE_SCALE * LOG2E)
            total = sum(
                jnp.sum(
                    jnp.exp2(tile * (SCORE_SCALE * LOG2E) - shifted), axis=0, keepdims=True
                )
                for tile in scores
            )
            out_ref[head, :, pl.ds(piece * ROWS_HERE, ROWS_HERE)] = jnp.broadcast_to(
                shifted + jnp.log2(total), (8, ROWS_HERE)
            )
        return carry

    lax.fori_loop(0, HEADS_HERE, one_head, 0)


def grads_kernel(*refs):
    query_refs, key_refs, value_refs, total_refs = (
        refs[GRID * i : GRID * (i + 1)] for i in range(4)
    )
    grad_ref, dots_ref = refs[4 * GRID : 4 * GRID + 2]
    rest = refs[4 * GRID + 2 :]
    query_out, pair_out, (key_sums, value_sums) = rest[:GRID], rest[GRID : 2 * GRID], rest[2 * GRID :]
    root = math.sqrt(FRAMES * 64)

    def one_head(head, carry):
        columns = pl.ds(pl.multiple_of(head * HDIM, HDIM), HDIM)
        for piece in range(GRID):
            parts = [
                total_refs[step][
                    head, 0:1, pl.ds(((piece - step) % GRID) * ROWS_HERE, ROWS_HERE)
                ]
                for step in range(GRID)
            ]
            top = functools.reduce(jnp.maximum, parts)
            totals = top + jnp.log2(sum(jnp.exp2(part - top) for part in parts))
            dots = dots_ref[head, 0:1, pl.ds(piece * ROWS_HERE, ROWS_HERE)]
            query = query_refs[piece][:, columns]
            grad = grad_ref[piece, :, columns]
            query_sum = jnp.zeros((ROWS_HERE, HDIM), f32)
            for other in range(GRID):
                key = key_refs[other][:, columns]
                scores = lax.dot_general(
                    key, query, (((1,), (1,)), ((), ())), preferred_element_type=f32
                )
                weights = jnp.exp2(scores * (SCORE_SCALE * LOG2E) - totals)
                mixed = lax.dot_general(
                    value_refs[other][:, columns],
                    grad,
                    (((1,), (1,)), ((), ())),
                    preferred_element_type=f32,
                )
                dscore = (weights * (mixed - dots)).astype(bf16)
                value_part = jnp.dot(weights.astype(bf16), grad, preferred_element_type=f32)
                key_part = jnp.dot(dscore, query, preferred_element_type=f32)
                query_sum = query_sum + lax.dot_general(
                    dscore, key, (((0,), (0,)), ((), ())), preferred_element_type=f32
                )
                if piece == 0:
                    value_sums[other] = value_part
                    key_sums[other] = key_part
                else:
                    value_sums[other] += value_part
                    key_sums[other] += key_part
            query_out[piece][:, columns] = (query_sum * (root * SCORE_SCALE)).astype(bf16)
        for other in range(GRID):
            pair_out[other][0, :, columns] = (key_sums[other] * (root * SCORE_SCALE)).astype(bf16)
            pair_out[other][1, :, columns] = (value_sums[other] * root).astype(bf16)
        return carry

    lax.fori_loop(0, HEADS_HERE, one_head, 0)


def call(kernel, out_shape, scratch=(), scalars=0, operands=0, flops=0, moved=0):
    vmem = pl.BlockSpec(memory_space=pltpu.VMEM)
    smem = pl.BlockSpec(memory_space=pltpu.SMEM)
    return pl.pallas_call(
        kernel,
        out_shape=out_shape,
        in_specs=[smem] * scalars + [vmem] * operands,
        out_specs=jax.tree.map(lambda _: vmem, out_shape),
        scratch_shapes=list(scratch),
        compiler_params=pltpu.CompilerParams(vmem_limit_bytes=VMEM_LIMIT),
        cost_estimate=pl.CostEstimate(flops=flops, bytes_accessed=moved, transcendentals=0),
    )


def shape(dims, dtype):
    return jax.ShapeDtypeStruct(dims, dtype)


def from_ahead(block, axis, step):
    return lax.ppermute(block, axis, [(i, (i - step) % GRID) for i in range(GRID)])


def to_ahead(block, axis, step):
    return lax.ppermute(block, axis, [(i, (i + step) % GRID) for i in range(GRID)])


def per_device(
    vit_cot,
    vit_pre,
    ln_gain,
    patch_w,
    frame_owner,
    conv_w,
    join_w,
    token_order,
    queries,
    keys,
    values,
    attn_out,
    out_w,
):
    here_x = lax.axis_index("hx")
    here_y = lax.axis_index("hy")
    place = jnp.stack([here_x, here_y]).astype(jnp.int32)

    def gather(block, axis):
        return [block] + [from_ahead(block, axis, step) for step in range(1, GRID)]

    key_pieces = gather(keys[0], "hx")
    query_pieces = gather(queries[0], "hy")
    value_pieces = gather(values[0], "hx")
    out_pieces = gather(attn_out[0], "hy")

    order_lanes = jnp.pad(
        token_order.reshape(4, 16).T.astype(bf16),
        ((0, 0), (ORDER_LANE, LANES - ORDER_LANE - 4)),
    )
    windows = call(
        window_kernel,
        shape((FRAMES, 16, LANES), bf16),
        scratch=[pltpu.VMEM((SIDE * SIDE + 16, LANES), f32)],
        operands=8,
        flops=400 * 10**6,
        moved=3 * 10**6,
    )(
        vit_cot[0, 0],
        vit_pre[0, 0],
        ln_gain[None],
        patch_w,
        jnp.asarray(basis_matrix(), bf16),
        jnp.asarray(basis_scale(), f32),
        jnp.asarray(spread_matrix(), f32),
        order_lanes,
    )
    received = lax.all_to_all(
        windows, ("tm", "hx", "hy"), split_axis=0, concat_axis=0, tiled=True
    )

    totals = call(
        totals_kernel,
        shape((HEADS_HERE, 8, BLOCK), f32),
        operands=2 * GRID,
        flops=8 * 10**8,
        moved=2 * 10**6,
    )(*query_pieces, *key_pieces)
    total_pieces = gather(totals, "hy")

    joint = lax.dot_general(
        join_w, out_w, (((1,), (1,)), ((), ())), preferred_element_type=f32
    ).astype(bf16)
    conv_rows = jnp.pad(
        conv_w.reshape(3, TAPS, LANES), ((0, 0), (0, QUARTER_LANES - TAPS), (0, 0))
    )
    grad_out, row_dots, outer = call(
        token_kernel,
        (
            shape((GRID, ROWS_HERE, FEATS), bf16),
            shape((HEADS_HERE, 8, BLOCK), f32),
            shape((QUARTERS * LANES, FEATS), bf16),
        ),
        scratch=[
            pltpu.VMEM((FRAMES + 2, 16, LANES), bf16),
            pltpu.VMEM((3 * LANES, QUARTERS * LANES), bf16),
            pltpu.VMEM((BLOCK, QUARTERS * LANES), bf16),
        ],
        scalars=2,
        operands=3 + GRID,
        flops=2 * 10**9,
        moved=3 * 10**6,
    )(place, frame_owner, received, conv_rows, joint, *out_pieces)

    weight_part = lax.dot_general(
        join_w, outer, (((0,), (0,)), ((), ())), preferred_element_type=f32
    ) * (1.0 / math.sqrt(FRAMES * 64 * 4))
    weight_part = weight_part.astype(bf16).reshape(2, 2, GRID, GRID, 48, FEATS)
    weight_part = lax.dynamic_index_in_dim(weight_part, here_y, 3, keepdims=False)
    weight_part = weight_part.transpose(1, 2, 0, 3, 4).reshape(8, 2, 48, FEATS)
    weight_parts = lax.all_to_all(
        weight_part, ("core", "hx"), split_axis=0, concat_axis=0, tiled=True
    )
    weight_half = jnp.sum(weight_parts.astype(f32), axis=0)
    here_z = lax.axis_index("zh")
    weight_other = lax.ppermute(
        lax.dynamic_index_in_dim(weight_half, 1 - here_z, 0, keepdims=False),
        "zh",
        [(0, 1), (1, 0)],
    )
    weight_grad = lax.dynamic_index_in_dim(weight_half, here_z, 0, keepdims=False) + weight_other

    outs = call(
        grads_kernel,
        tuple([shape((ROWS_HERE, FEATS), bf16)] * GRID)
        + tuple([shape((2, ROWS_HERE, FEATS), bf16)] * GRID),
        scratch=[pltpu.VMEM((GRID, ROWS_HERE, HDIM), f32)] * 2,
        operands=4 * GRID + 2,
        flops=8 * 10**9,
        moved=6 * 10**6,
    )(*query_pieces, *key_pieces, *value_pieces, *total_pieces, grad_out, row_dots)
    query_parts, pair_parts = outs[:GRID], outs[GRID:]
    pair_back = [pair_parts[0]] + [
        to_ahead(pair_parts[step], "hx", step) for step in range(1, GRID)
    ]
    query_back = [query_parts[0]] + [
        to_ahead(query_parts[step], "hy", step) for step in range(1, GRID)
    ]

    def total(parts):
        return sum(part.astype(f32) for part in parts).astype(bf16)

    query_grad = total(query_back)
    key_grad = total([part[0] for part in pair_back])
    value_grad = total([part[1] for part in pair_back])
    return (query_grad[None], key_grad[None], value_grad[None], weight_grad)


def solution(mesh):
    fine = Mesh(
        mesh.devices.reshape(2, 2, GRID, GRID, GRID), ("zh", "core", "tm", "hx", "hy")
    )
    dp, height = ("zh", "core"), ("hx", "hy")
    rows = P(dp, height, "tm")
    slots = P(dp, ("tm",) + height, None, None)
    placed = (
        slots,
        slots,
        P(),
        P(),
        P(),
        P(),
        P(),
        P(height, "tm"),
        rows,
        rows,
        rows,
        rows,
        P("tm", None),
    )
    return jax.shard_map(
        per_device,
        mesh=fine,
        in_specs=placed,
        out_specs=(rows, rows, rows, P(dp + height, "tm")),
        check_vma=False,
    )
```

```python
import functools
import math

import jax
import jax.numpy as jnp
import numpy as np
from jax import lax
from jax.experimental import pallas as pl
from jax.experimental.pallas import tpu as pltpu
from jax.sharding import Mesh
from jax.sharding import PartitionSpec as P

HDIM = 128
IMG = 224
PATCH = 14
SIDE = IMG // PATCH
GRID = 4
HEADS_HERE = 3
ROWS_HERE = 256
FEATS = HEADS_HERE * HDIM
BLOCK = GRID * ROWS_HERE
FRAMES = 64
LANES = 128
QUARTERS = 4
QUARTER_LANES = 32
TAPS = 27
ORDER_LANE = TAPS
QUARTER_CELLS = (PATCH // 2) * (2 * PATCH)

epsilon = 1e-05
pixel_std = (0.26862954, 0.26130258, 0.27577711)

f32 = jnp.float32
bf16 = jnp.bfloat16
MIB = 1024 * 1024
HIGHEST = lax.Precision.HIGHEST
LOG2E = math.log2(math.e)
SCORE_SCALE = HDIM ** (-0.5)


def row_masks():
    masks = np.zeros((8, PATCH), np.float32)
    for half in range(2):
        for shift in range(3):
            low = half * 7 + shift - 1
            masks[half * 3 + shift, max(low, 0) : min(low + 7, PATCH)] = 1
    masks[6, 0] = 1
    masks[7, PATCH - 1] = 1
    return masks


def basis_matrix():
    rows = row_masks()
    columns = np.zeros((3, PATCH), np.float32)
    columns[0] = 1
    columns[1, 0] = 1
    columns[2, PATCH - 1] = 1
    basis = np.zeros((LANES, 3, PATCH, PATCH), np.float32)
    for col in range(3):
        for row in range(8):
            for channel in range(3):
                basis[col * 24 + row * 3 + channel, channel] = np.outer(rows[row], columns[col])
    return basis.reshape(LANES, 3 * PATCH * PATCH)


def spread_matrix():
    spread = np.zeros((6, LANES, LANES), np.float32)
    for half in range(2):
        for side in range(2):
            first = 2 * side + 1
            terms = {
                0: [(first - 1, 2, 1), (first, 0, 1), (first + 1, 0, 1), (first + 1, 2, -1)],
                1: [(first, 0, 1), (first + 1, 0, 1)],
                2: [(first, 0, 1), (first, 1, -1), (first + 1, 0, 1), (first + 2, 1, 1)],
            }
            for shift in range(3):
                groups = [half * 3 + shift]
                if (half, shift) == (0, 0):
                    groups.append(7)
                if (half, shift) == (1, 2):
                    groups.append(6)
                for offset in range(3):
                    for channel in range(3):
                        lane = (half * 2 + side) * QUARTER_LANES + (shift * 3 + offset) * 3 + channel
                        for place, col, sign in terms[offset]:
                            for row in groups:
                                spread[place, col * 24 + row * 3 + channel, lane] += sign
    return spread.reshape(6 * LANES, LANES)


NN = (((1,), (0,)), ((), ()))
NT = (((1,), (1,)), ((), ()))
TN = (((0,), (0,)), ((), ()))


def dot(left, right, dims=NN):
    return lax.dot_general(left, right, dims, preferred_element_type=f32)


def one_hot(condition):
    return jnp.where(condition, 1.0, 0.0).astype(bf16)


def iota(dims, axis):
    return lax.broadcasted_iota(jnp.int32, dims, axis)


def fetch_halves(refs, column, held, arrived):
    copies = [
        pltpu.make_async_copy(
            ref.at[:, pl.ds(column * FEATS, FEATS)], held.at[place], arrived.at[place]
        )
        for place, ref in enumerate(refs)
    ]
    for copy in copies:
        copy.start()
    return copies


def window_kernel(
    cot_ref, pre_ref, gain_ref, patch_ref, basis_ref, spread_ref, order_ref, out_ref, sums
):
    pre = pre_ref[...].astype(f32)
    centered = pre - jnp.mean(pre, axis=-1, keepdims=True)
    inverse = lax.rsqrt(jnp.mean(centered * centered, axis=-1, keepdims=True) + epsilon)
    normed = centered * inverse
    scaled = cot_ref[...].astype(f32) * gain_ref[...].astype(f32).reshape(1, -1)
    grad_rows = inverse * (
        scaled
        - jnp.mean(scaled, axis=-1, keepdims=True)
        - normed * jnp.mean(scaled * normed, axis=-1, keepdims=True)
    )
    grad_rows = grad_rows.astype(bf16)
    channel = iota((LANES, 1), 0) % 3
    scale = jnp.where(
        channel == 0, 1.0 / pixel_std[0], jnp.where(channel == 1, 1.0 / pixel_std[1], 1.0 / pixel_std[2])
    ) * (1.0 / QUARTER_CELLS)
    weights = dot(basis_ref[...], patch_ref[...]) * scale
    high = weights.astype(bf16)
    low = (weights - high.astype(f32)).astype(bf16)
    both = dot(grad_rows, jnp.concatenate([high, low], axis=0), NT)
    patch_sums = both[:, :LANES] + both[:, LANES:]
    group = (iota((SIDE * SIDE, LANES), 1) // 3) % 8
    edge = jnp.zeros((SIDE, LANES), f32)
    above = jnp.concatenate([edge, patch_sums[:-SIDE]], axis=0)
    below = jnp.concatenate([patch_sums[SIDE:], edge], axis=0)
    patch_sums = jnp.where(group == 7, above, jnp.where(group == 6, below, patch_sums))
    sums[pl.ds(0, 8), :] = jnp.zeros((8, LANES), f32)
    sums[pl.ds(8 + SIDE * SIDE, 8), :] = jnp.zeros((8, LANES), f32)
    sums[pl.ds(8, SIDE * SIDE), :] = patch_sums
    column = iota((SIDE * GRID, LANES), 0) % GRID
    total = jnp.zeros((SIDE * GRID, LANES), f32)
    for place in range(6):
        picked = sums[pl.ds(7 + place, SIDE * GRID, stride=GRID), :]
        if place == 0:
            picked = jnp.where(column == 0, 0.0, picked)
        if place == 5:
            picked = jnp.where(column == GRID - 1, 0.0, picked)
        high = picked.astype(bf16)
        low = (picked - high.astype(f32)).astype(bf16)
        both = dot(
            jnp.concatenate([high, low], axis=0), spread_ref[pl.ds(place * LANES, LANES), :]
        )
        total = total + (both[: SIDE * GRID] + both[SIDE * GRID :])
    windows = total.astype(bf16)
    entries = jnp.where(
        iota((16, 64), 1) % 16 == iota((16, 64), 0), order_ref[...].astype(f32), 0.0
    ).astype(bf16)
    order = dot(entries, one_hot(iota((64, LANES), 1) == ORDER_LANE + iota((64, LANES), 0) // 16))
    order = order.astype(bf16)
    for target_x in range(GRID):
        block = windows[target_x * 16 : (target_x + 1) * 16] + order
        for target_t in range(GRID):
            for target_y in range(GRID):
                out_ref[(target_t * GRID + target_x) * GRID + target_y] = block


def weights_kernel(join_ref, out_w_ref, joint_ref, picked_ref):
    here_y = lax.axis_index("hy")
    joint_ref[...] = dot(join_ref[...], out_w_ref[...], NT).astype(bf16)
    row, column = iota((96, 384), 0), iota((96, 384), 1)
    half = row // 48
    pick = one_hot(column == half * 192 + here_y * 48 + (row - half * 48))
    for pair in range(8):
        rows = dot(pick, join_ref[:, pl.ds(pair * 384, 384)], NT).astype(bf16)
        z, core, x = pair // 4, (pair % 4) // 2, (pair % 2) * 2
        for step in range(2):
            picked_ref[pl.ds((core * GRID + x + step) * 96 + z * 48, 48), :] = rows[
                step * 48 : (step + 1) * 48
            ]


def token_kernel(owner_ref, recv_ref, conv_ref, joint_ref, picked_ref, *refs):
    grad_ref, dots_ref, weight_ref, frames, conv_big, ordered, held, arrived = refs[GRID:]
    copies = fetch_halves(refs[:GRID], 1, held, arrived)
    here_x = lax.axis_index("hx")
    here_y = lax.axis_index("hy")
    frames[0] = jnp.zeros((16, LANES), bf16)
    frames[FRAMES + 1] = jnp.zeros((16, LANES), bf16)

    def fetch(frame, carry):
        frames[frame + 1] = recv_ref[(frame // 16) * 16 + owner_ref[frame]]
        return carry

    lax.fori_loop(0, FRAMES, fetch, 0, unroll=8)
    row, column = iota((3 * QUARTER_LANES, 3 * TAPS), 0), iota((3 * QUARTER_LANES, 3 * TAPS), 1)
    tap = row % QUARTER_LANES
    conv = dot(
        one_hot((tap < TAPS) & (column == (row // QUARTER_LANES) * TAPS + tap)), conv_ref[...]
    ).astype(bf16)
    conv_big[...] = jnp.zeros_like(conv_big)
    for quarter in range(QUARTERS):
        for shift in range(3):
            conv_big[
                pl.ds(shift * LANES + quarter * QUARTER_LANES, QUARTER_LANES),
                pl.ds(quarter * LANES, LANES),
            ] = conv[shift * QUARTER_LANES : (shift + 1) * QUARTER_LANES]
    lane = iota((16, ROWS_HERE), 1)
    for slab_t in range(GRID):
        pooled = sum(
            dot(
                frames[pl.ds(slab_t * 16 + shift, 16)].reshape(ROWS_HERE, LANES),
                conv_big[pl.ds(shift * LANES, LANES), :],
            )
            for shift in range(3)
        ).astype(bf16)
        pieces = []
        for piece in range(GRID):
            slab = lax.rem(here_y + piece, GRID)
            block = recv_ref[slab_t * 16 + here_x * GRID + slab].astype(f32)
            for part in range(4):
                order = block[:, ORDER_LANE + part : ORDER_LANE + part + 1].astype(jnp.int32)
                target = (order // 4) * 16 + slab * 4 + lax.rem(order, 4)
                pieces.append(one_hot(lane == target))
        chosen = dot(jnp.concatenate(pieces, axis=0), pooled).astype(bf16)
        for piece in range(GRID):
            ordered[pl.ds(piece * ROWS_HERE + slab_t * 64, 64), :] = chosen[
                piece * 64 : (piece + 1) * 64
            ]
    ones = jnp.ones((8, HDIM), f32)
    outer = jnp.zeros((QUARTERS * LANES, FEATS), f32)
    for piece in range(GRID):
        rows = ordered[pl.ds(piece * ROWS_HERE, ROWS_HERE), :]
        copies[piece].wait()
        outs = held[piece]
        grads = dot(rows, joint_ref[...]).astype(bf16)
        grad_ref[piece] = grads
        products = grads.astype(f32) * outs.astype(f32)
        for head in range(HEADS_HERE):
            dots_ref[head, :, pl.ds(piece * ROWS_HERE, ROWS_HERE)] = lax.dot_general(
                ones,
                products[:, head * HDIM : (head + 1) * HDIM],
                NT,
                preferred_element_type=f32,
                precision=HIGHEST,
            )
        outer = outer + dot(rows, outs, TN)
    weight_ref[...] = (
        dot(picked_ref[...], outer.astype(bf16)) * (1.0 / math.sqrt(FRAMES * 64 * 4))
    ).astype(bf16)


def totals_kernel(*refs):
    out_ref, query_held, key_held, query_arrived, key_arrived = refs[2 * GRID :]
    key_copies = fetch_halves(refs[GRID : 2 * GRID], 0, key_held, key_arrived)
    query_copies = fetch_halves(refs[:GRID], 0, query_held, query_arrived)
    for copy in key_copies + query_copies:
        copy.wait()
    for head in range(HEADS_HERE):
        columns = pl.ds(head * HDIM, HDIM)
        for piece in range(GRID):
            query = query_held[piece, :, columns]
            scores = [dot(key_held[other, :, columns], query, NT) for other in range(GRID)]
            top = functools.reduce(
                jnp.maximum, [jnp.max(tile, axis=0, keepdims=True) for tile in scores]
            ) * (SCORE_SCALE * LOG2E)
            total = sum(
                jnp.sum(jnp.exp2(tile * (SCORE_SCALE * LOG2E) - top), axis=0, keepdims=True)
                for tile in scores
            )
            out_ref[pl.ds(head, 1), pl.ds(piece * ROWS_HERE, ROWS_HERE)] = top + jnp.log2(total)
    out_ref[pl.ds(HEADS_HERE, 8 - HEADS_HERE), :] = jnp.zeros((8 - HEADS_HERE, BLOCK), f32)


def grads_kernel(*refs):
    pair_refs, total_refs = refs[GRID : 2 * GRID], refs[2 * GRID : 3 * GRID]
    grad_ref, dots_ref = refs[3 * GRID : 3 * GRID + 2]
    rest = refs[3 * GRID + 2 :]
    query_out, pair_out = rest[:GRID], rest[GRID : 2 * GRID]
    sums, query_held, key_held, value_held, query_arrived, key_arrived, value_arrived = rest[
        2 * GRID :
    ]
    query_copies = fetch_halves(refs[:GRID], 0, query_held, query_arrived)
    key_copies = fetch_halves(pair_refs, 0, key_held, key_arrived)
    value_copies = fetch_halves(pair_refs, 1, value_held, value_arrived)
    for copy in query_copies:
        copy.wait()
    root = math.sqrt(FRAMES * 64)
    for head in range(HEADS_HERE):
        columns = pl.ds(head * HDIM, HDIM)
        totals = []
        for piece in range(GRID):
            parts = [
                total_refs[step][
                    pl.ds(head, 1), pl.ds(((piece - step) % GRID) * ROWS_HERE, ROWS_HERE)
                ]
                for step in range(GRID)
            ]
            top = functools.reduce(jnp.maximum, parts)
            totals.append(top + jnp.log2(sum(jnp.exp2(part - top) for part in parts)))
        totals = jnp.concatenate(totals, axis=1)
        dots = dots_ref[head, 0:1, :]
        query = query_held[:, :, columns].reshape(BLOCK, HDIM)
        grad = grad_ref[:, :, columns].reshape(BLOCK, HDIM)
        for other in range(GRID):
            if head == 0:
                key_copies[other].wait()
                value_copies[other].wait()
            key = key_held[other, :, columns]
            value = value_held[other, :, columns]
            weights = jnp.exp2(dot(key, query, NT) * (SCORE_SCALE * LOG2E) - totals)
            dscore = (weights * (dot(value, grad, NT) - dots)).astype(bf16)
            pair_out[other][1, :, columns] = (dot(weights.astype(bf16), grad) * root).astype(bf16)
            pair_out[other][0, :, columns] = (
                dot(dscore, query) * (root * SCORE_SCALE)
            ).astype(bf16)
            part = dot(key.T, dscore)
            if other == 0:
                sums[...] = part
            else:
                sums[...] += part
        for piece in range(GRID):
            query_out[piece][:, columns] = (
                sums[:, pl.ds(piece * ROWS_HERE, ROWS_HERE)].T * (root * SCORE_SCALE)
            ).astype(bf16)


def call(kernel, out_shape, in_specs, scratch=(), limit=16, flops=0, moved=0):
    return pl.pallas_call(
        kernel,
        out_shape=out_shape,
        in_specs=in_specs,
        out_specs=jax.tree.map(lambda _: VMEM, out_shape),
        scratch_shapes=list(scratch),
        compiler_params=pltpu.CompilerParams(vmem_limit_bytes=limit * MIB),
        cost_estimate=pl.CostEstimate(flops=flops, bytes_accessed=moved, transcendentals=0),
    )


VMEM = pl.BlockSpec(memory_space=pltpu.VMEM)
SMEM = pl.BlockSpec(memory_space=pltpu.SMEM)
ANY = pl.BlockSpec(memory_space=pl.ANY)
HELD = [pltpu.VMEM((GRID, ROWS_HERE, FEATS), bf16)]
ARRIVED = [pltpu.SemaphoreType.DMA((GRID,))]


def shape(dims, dtype):
    return jax.ShapeDtypeStruct(dims, dtype)


def from_ahead(block, axis, step):
    return lax.ppermute(block, axis, [(i, (i - step) % GRID) for i in range(GRID)])


def to_ahead(block, axis, step):
    return lax.ppermute(block, axis, [(i, (i + step) % GRID) for i in range(GRID)])


def gather(block, axis):
    return [block] + [from_ahead(block, axis, step) for step in range(1, GRID)]


def per_device(
    vit_cot,
    vit_pre,
    ln_gain,
    patch_w,
    frame_owner,
    conv_w,
    join_w,
    token_order,
    queries,
    keys,
    values,
    attn_out,
    out_w,
):
    key_values = gather(jnp.concatenate([keys[0], values[0]], axis=1), "hx")
    query_outs = gather(jnp.concatenate([queries[0], attn_out[0]], axis=1), "hy")
    windows = call(
        window_kernel,
        shape((FRAMES, 16, LANES), bf16),
        [VMEM] * 7,
        scratch=[pltpu.VMEM((SIDE * SIDE + 16, LANES), f32)],
        flops=400 * 10**6,
        moved=3 * 10**6,
    )(
        vit_cot[0, 0],
        vit_pre[0, 0],
        ln_gain,
        patch_w,
        jnp.asarray(basis_matrix(), bf16),
        jnp.asarray(spread_matrix(), bf16),
        token_order,
    )
    received = lax.all_to_all(
        windows, ("tm", "hx", "hy"), split_axis=0, concat_axis=0, tiled=True
    )
    joint, picked = call(
        weights_kernel,
        (shape((QUARTERS * LANES, FEATS), bf16), shape((768, QUARTERS * LANES), bf16)),
        [VMEM] * 2,
        flops=2 * 10**9,
        moved=6 * 10**6,
    )(join_w, out_w)
    totals = call(
        totals_kernel,
        shape((8, BLOCK), f32),
        [ANY] * (2 * GRID),
        scratch=HELD * 2 + ARRIVED * 2,
        flops=8 * 10**8,
        moved=2 * 10**6,
    )(*query_outs, *key_values)
    total_pieces = gather(totals, "hy")
    grad_out, row_dots, weight_part = call(
        token_kernel,
        (
            shape((GRID, ROWS_HERE, FEATS), bf16),
            shape((HEADS_HERE, 8, BLOCK), f32),
            shape((768, FEATS), bf16),
        ),
        [SMEM] + [VMEM] * 4 + [ANY] * GRID,
        scratch=[
            pltpu.VMEM((FRAMES + 2, 16, LANES), bf16),
            pltpu.VMEM((3 * LANES, QUARTERS * LANES), bf16),
            pltpu.VMEM((BLOCK, QUARTERS * LANES), bf16),
        ]
        + HELD
        + ARRIVED,
        flops=2 * 10**9,
        moved=3 * 10**6,
    )(frame_owner, received, conv_w, joint, picked, *query_outs)
    weight_parts = lax.all_to_all(
        weight_part.reshape(8, 2, 48, FEATS),
        ("core", "hx"),
        split_axis=0,
        concat_axis=0,
        tiled=True,
    )
    weight_half = jnp.sum(weight_parts.astype(f32), axis=0)
    here_z = lax.axis_index("zh")
    weight_other = lax.ppermute(
        lax.dynamic_index_in_dim(weight_half, 1 - here_z, 0, keepdims=False),
        "zh",
        [(0, 1), (1, 0)],
    )
    weight_grad = lax.dynamic_index_in_dim(weight_half, here_z, 0, keepdims=False) + weight_other

    outs = call(
        grads_kernel,
        tuple([shape((ROWS_HERE, FEATS), bf16)] * GRID)
        + tuple([shape((2, ROWS_HERE, FEATS), bf16)] * GRID),
        [ANY] * (2 * GRID) + [VMEM] * (GRID + 2),
        scratch=[pltpu.VMEM((HDIM, BLOCK), f32)] + HELD * 3 + ARRIVED * 3,
        limit=24,
        flops=8 * 10**9,
        moved=6 * 10**6,
    )(*query_outs, *key_values, *total_pieces, grad_out, row_dots)
    query_parts, pair_parts = outs[:GRID], outs[GRID:]
    pair_back = [pair_parts[0]] + [
        to_ahead(pair_parts[step], "hx", step) for step in range(1, GRID)
    ]
    query_back = [query_parts[0]] + [
        to_ahead(query_parts[step], "hy", step) for step in range(1, GRID)
    ]

    def total(parts):
        return sum(part.astype(f32) for part in parts).astype(bf16)

    query_grad = total(query_back)
    key_grad = total([part[0] for part in pair_back])
    value_grad = total([part[1] for part in pair_back])
    return (query_grad[None], key_grad[None], value_grad[None], weight_grad)


def solution(mesh):
    fine = Mesh(
        mesh.devices.reshape(2, 2, GRID, GRID, GRID), ("zh", "core", "tm", "hx", "hy")
    )
    dp, height = ("zh", "core"), ("hx", "hy")
    rows = P(dp, height, "tm")
    slots = P(dp, ("tm",) + height, None, None)
    placed = (
        slots,
        slots,
        P(),
        P(),
        P(),
        P(),
        P(),
        P(height, "tm"),
        rows,
        rows,
        rows,
        rows,
        P("tm", None),
    )
    return jax.shard_map(
        per_device,
        mesh=fine,
        in_specs=placed,
        out_specs=(rows, rows, rows, P(dp + height, "tm")),
        check_vma=False,
    )
```

```python
import functools
import math

import jax
import jax.numpy as jnp
import numpy as np
from jax import lax
from jax.experimental import pallas as pl
from jax.experimental.pallas import tpu as pltpu
from jax.sharding import Mesh
from jax.sharding import PartitionSpec as P

HDIM = 128
IMG = 224
PATCH = 14
SIDE = IMG // PATCH
GRID = 4
HEADS_HERE = 3
ROWS_HERE = 256
FEATS = HEADS_HERE * HDIM
BLOCK = GRID * ROWS_HERE
FRAMES = 64
LANES = 128
QUARTERS = 4
QUARTER_LANES = 32
TAPS = 27
ORDER_LANE = TAPS
QUARTER_CELLS = (PATCH // 2) * (2 * PATCH)

epsilon = 1e-05
pixel_std = (0.26862954, 0.26130258, 0.27577711)

f32 = jnp.float32
bf16 = jnp.bfloat16
MIB = 1024 * 1024
HIGHEST = lax.Precision.HIGHEST
LOG2E = math.log2(math.e)
SCORE_SCALE = HDIM ** (-0.5)


def row_masks():
    masks = np.zeros((8, PATCH), np.float32)
    for half in range(2):
        for shift in range(3):
            low = half * 7 + shift - 1
            masks[half * 3 + shift, max(low, 0) : min(low + 7, PATCH)] = 1
    masks[6, 0] = 1
    masks[7, PATCH - 1] = 1
    return masks


def basis_matrix():
    rows = row_masks()
    columns = np.zeros((3, PATCH), np.float32)
    columns[0] = 1
    columns[1, 0] = 1
    columns[2, PATCH - 1] = 1
    basis = np.zeros((LANES, 3, PATCH, PATCH), np.float32)
    for col in range(3):
        for row in range(8):
            for channel in range(3):
                basis[col * 24 + row * 3 + channel, channel] = np.outer(rows[row], columns[col])
    return basis.reshape(LANES, 3 * PATCH * PATCH)


def spread_matrix():
    spread = np.zeros((6, LANES, LANES), np.float32)
    for half in range(2):
        for side in range(2):
            first = 2 * side + 1
            terms = {
                0: [(first - 1, 2, 1), (first, 0, 1), (first + 1, 0, 1), (first + 1, 2, -1)],
                1: [(first, 0, 1), (first + 1, 0, 1)],
                2: [(first, 0, 1), (first, 1, -1), (first + 1, 0, 1), (first + 2, 1, 1)],
            }
            for shift in range(3):
                groups = [half * 3 + shift]
                if (half, shift) == (0, 0):
                    groups.append(7)
                if (half, shift) == (1, 2):
                    groups.append(6)
                for offset in range(3):
                    for channel in range(3):
                        lane = (half * 2 + side) * QUARTER_LANES + (shift * 3 + offset) * 3 + channel
                        for place, col, sign in terms[offset]:
                            for row in groups:
                                spread[place, col * 24 + row * 3 + channel, lane] += sign
    return spread.reshape(6 * LANES, LANES)


NN = (((1,), (0,)), ((), ()))
NT = (((1,), (1,)), ((), ()))
TN = (((0,), (0,)), ((), ()))


def dot(left, right, dims=NN):
    return lax.dot_general(left, right, dims, preferred_element_type=f32)


def one_hot(condition):
    return jnp.where(condition, 1.0, 0.0).astype(bf16)


def iota(dims, axis):
    return lax.broadcasted_iota(jnp.int32, dims, axis)


def start(copies):
    for copy in copies:
        copy.start()


def fetch(refs, held, arrived):
    copies = [
        pltpu.make_async_copy(ref, kept, arrived.at[place])
        for place, (ref, kept) in enumerate(zip(refs, held))
    ]
    start(copies)
    return copies


def fetch_halves(refs, column, held, arrived):
    return fetch(
        [ref.at[:, pl.ds(column * FEATS, FEATS)] for ref in refs],
        [held.at[place] for place in range(len(refs))],
        arrived,
    )


def window_kernel(gain_ref, order_ref, *refs):
    out_ref, cot_ref, pre_ref, patch_ref, basis_ref, spread_ref, sums, arrived = refs[5:]
    held = (pre_ref, cot_ref, basis_ref, patch_ref, spread_ref)
    copies = fetch(refs[:5], held, arrived)
    copies[0].wait()
    copies[1].wait()
    pre = pre_ref[...].astype(f32)
    centered = pre - jnp.mean(pre, axis=-1, keepdims=True)
    inverse = lax.rsqrt(jnp.mean(centered * centered, axis=-1, keepdims=True) + epsilon)
    normed = centered * inverse
    scaled = cot_ref[...].astype(f32) * gain_ref[...].astype(f32).reshape(1, -1)
    grad_rows = inverse * (
        scaled
        - jnp.mean(scaled, axis=-1, keepdims=True)
        - normed * jnp.mean(scaled * normed, axis=-1, keepdims=True)
    )
    grad_rows = grad_rows.astype(bf16)
    channel = iota((LANES, 1), 0) % 3
    scale = jnp.where(
        channel == 0, 1.0 / pixel_std[0], jnp.where(channel == 1, 1.0 / pixel_std[1], 1.0 / pixel_std[2])
    ) * (1.0 / QUARTER_CELLS)
    copies[2].wait()
    copies[3].wait()
    weights = dot(basis_ref[...], patch_ref[...]) * scale
    high = weights.astype(bf16)
    low = (weights - high.astype(f32)).astype(bf16)
    both = dot(grad_rows, jnp.concatenate([high, low], axis=0), NT)
    patch_sums = both[:, :LANES] + both[:, LANES:]
    group = (iota((SIDE * SIDE, LANES), 1) // 3) % 8
    edge = jnp.zeros((SIDE, LANES), f32)
    above = jnp.concatenate([edge, patch_sums[:-SIDE]], axis=0)
    below = jnp.concatenate([patch_sums[SIDE:], edge], axis=0)
    patch_sums = jnp.where(group == 7, above, jnp.where(group == 6, below, patch_sums))
    sums[pl.ds(0, 8), :] = jnp.zeros((8, LANES), f32)
    sums[pl.ds(8 + SIDE * SIDE, 8), :] = jnp.zeros((8, LANES), f32)
    sums[pl.ds(8, SIDE * SIDE), :] = patch_sums
    copies[4].wait()
    column = iota((SIDE * GRID, LANES), 0) % GRID
    total = jnp.zeros((SIDE * GRID, LANES), f32)
    for place in range(6):
        picked = sums[pl.ds(7 + place, SIDE * GRID, stride=GRID), :]
        if place == 0:
            picked = jnp.where(column == 0, 0.0, picked)
        if place == 5:
            picked = jnp.where(column == GRID - 1, 0.0, picked)
        high = picked.astype(bf16)
        low = (picked - high.astype(f32)).astype(bf16)
        both = dot(
            jnp.concatenate([high, low], axis=0), spread_ref[pl.ds(place * LANES, LANES), :]
        )
        total = total + (both[: SIDE * GRID] + both[SIDE * GRID :])
    windows = total.astype(bf16)
    entries = jnp.where(
        iota((16, 64), 1) % 16 == iota((16, 64), 0), order_ref[...].astype(f32), 0.0
    ).astype(bf16)
    order = dot(entries, one_hot(iota((64, LANES), 1) == ORDER_LANE + iota((64, LANES), 0) // 16))
    order = order.astype(bf16)
    for target_x in range(GRID):
        block = windows[target_x * 16 : (target_x + 1) * 16] + order
        for target_t in range(GRID):
            for target_y in range(GRID):
                out_ref[(target_t * GRID + target_x) * GRID + target_y] = block


def weights_kernel(join_from, out_w_from, joint_ref, picked_ref, join_ref, out_w_ref, arrived):
    here_y = lax.axis_index("hy")
    copies = fetch([join_from, out_w_from], [join_ref, out_w_ref], arrived)
    copies[0].wait()
    copies[1].wait()
    joint_ref[...] = dot(join_ref[...], out_w_ref[...], NT).astype(bf16)
    row, column = iota((96, 384), 0), iota((96, 384), 1)
    half = row // 48
    pick = one_hot(column == half * 192 + here_y * 48 + (row - half * 48))
    for pair in range(8):
        rows = dot(pick, join_ref[:, pl.ds(pair * 384, 384)], NT).astype(bf16)
        z, core, x = pair // 4, (pair % 4) // 2, (pair % 2) * 2
        for step in range(2):
            picked_ref[pl.ds((core * GRID + x + step) * 96 + z * 48, 48), :] = rows[
                step * 48 : (step + 1) * 48
            ]


def token_kernel(owner_ref, conv_ref, recv_from, joint_from, picked_from, *refs):
    grad_ref, dots_ref, weight_ref, frames, conv_big, ordered, *rest = refs[GRID:]
    recv_ref, joint_ref, picked_ref, held, arrived, held_arrived = rest
    firsts = fetch(
        [recv_from, joint_from, picked_from], [recv_ref, joint_ref, picked_ref], arrived
    )
    copies = fetch_halves(refs[:GRID], 1, held, held_arrived)
    here_x = lax.axis_index("hx")
    here_y = lax.axis_index("hy")
    frames[0] = jnp.zeros((16, LANES), bf16)
    frames[FRAMES + 1] = jnp.zeros((16, LANES), bf16)

    row, column = iota((3 * QUARTER_LANES, 3 * TAPS), 0), iota((3 * QUARTER_LANES, 3 * TAPS), 1)
    tap = row % QUARTER_LANES
    conv = dot(
        one_hot((tap < TAPS) & (column == (row // QUARTER_LANES) * TAPS + tap)), conv_ref[...]
    ).astype(bf16)
    conv_big[...] = jnp.zeros_like(conv_big)
    for quarter in range(QUARTERS):
        for shift in range(3):
            conv_big[
                pl.ds(shift * LANES + quarter * QUARTER_LANES, QUARTER_LANES),
                pl.ds(quarter * LANES, LANES),
            ] = conv[shift * QUARTER_LANES : (shift + 1) * QUARTER_LANES]
    firsts[0].wait()

    def place_frame(frame, carry):
        frames[frame + 1] = recv_ref[(frame // 16) * 16 + owner_ref[frame]]
        return carry

    lax.fori_loop(0, FRAMES, place_frame, 0, unroll=8)
    lane = iota((16, ROWS_HERE), 1)
    for slab_t in range(GRID):
        pooled = sum(
            dot(
                frames[pl.ds(slab_t * 16 + shift, 16)].reshape(ROWS_HERE, LANES),
                conv_big[pl.ds(shift * LANES, LANES), :],
            )
            for shift in range(3)
        ).astype(bf16)
        pieces = []
        for piece in range(GRID):
            slab = lax.rem(here_y + piece, GRID)
            block = recv_ref[slab_t * 16 + here_x * GRID + slab].astype(f32)
            for part in range(4):
                order = block[:, ORDER_LANE + part : ORDER_LANE + part + 1].astype(jnp.int32)
                target = (order // 4) * 16 + slab * 4 + lax.rem(order, 4)
                pieces.append(one_hot(lane == target))
        chosen = dot(jnp.concatenate(pieces, axis=0), pooled).astype(bf16)
        for piece in range(GRID):
            ordered[pl.ds(piece * ROWS_HERE + slab_t * 64, 64), :] = chosen[
                piece * 64 : (piece + 1) * 64
            ]
    firsts[1].wait()
    ones = jnp.ones((8, HDIM), f32)
    outer = jnp.zeros((QUARTERS * LANES, FEATS), f32)
    for piece in range(GRID):
        rows = ordered[pl.ds(piece * ROWS_HERE, ROWS_HERE), :]
        copies[piece].wait()
        outs = held[piece]
        grads = dot(rows, joint_ref[...]).astype(bf16)
        grad_ref[piece] = grads
        products = grads.astype(f32) * outs.astype(f32)
        for head in range(HEADS_HERE):
            dots_ref[head, :, pl.ds(piece * ROWS_HERE, ROWS_HERE)] = lax.dot_general(
                ones,
                products[:, head * HDIM : (head + 1) * HDIM],
                NT,
                preferred_element_type=f32,
                precision=HIGHEST,
            )
        outer = outer + dot(rows, outs, TN)
    firsts[2].wait()
    weight_ref[...] = (
        dot(picked_ref[...], outer.astype(bf16)) * (1.0 / math.sqrt(FRAMES * 64 * 4))
    ).astype(bf16)


def totals_kernel(*refs):
    out_ref, query_held, key_held, query_arrived, key_arrived = refs[2 * GRID :]
    key_copies = fetch_halves(refs[GRID : 2 * GRID], 0, key_held, key_arrived)
    query_copies = fetch_halves(refs[:GRID], 0, query_held, query_arrived)
    for copy in key_copies:
        copy.wait()
    for head in range(HEADS_HERE):
        columns = pl.ds(head * HDIM, HDIM)
        for piece in range(GRID):
            if head == 0:
                query_copies[piece].wait()
            query = query_held[piece, :, columns]
            scores = [dot(key_held[other, :, columns], query, NT) for other in range(GRID)]
            top = functools.reduce(
                jnp.maximum, [jnp.max(tile, axis=0, keepdims=True) for tile in scores]
            ) * (SCORE_SCALE * LOG2E)
            total = sum(
                jnp.sum(jnp.exp2(tile * (SCORE_SCALE * LOG2E) - top), axis=0, keepdims=True)
                for tile in scores
            )
            out_ref[pl.ds(head, 1), pl.ds(piece * ROWS_HERE, ROWS_HERE)] = top + jnp.log2(total)
    out_ref[pl.ds(HEADS_HERE, 8 - HEADS_HERE), :] = jnp.zeros((8 - HEADS_HERE, BLOCK), f32)


def grads_kernel(*refs):
    query_refs, pair_refs, total_refs = (refs[GRID * i : GRID * (i + 1)] for i in range(3))
    grad_from, dots_ref = refs[3 * GRID : 3 * GRID + 2]
    rest = refs[3 * GRID + 2 :]
    query_out, pair_out = rest[:GRID], rest[GRID : 2 * GRID]
    (
        sums,
        query_held,
        key_held,
        value_held,
        grad_ref,
        query_made,
        pair_made,
        query_arrived,
        key_arrived,
        value_arrived,
        grad_arrived,
        query_sent,
        pair_sent,
    ) = rest[2 * GRID :]
    sends_order = (2, 1, 3, 0)
    query_copies = fetch_halves(query_refs, 0, query_held, query_arrived)
    (grad_copy,) = fetch([grad_from], [grad_ref], grad_arrived)
    pair_copies = [
        (
            pltpu.make_async_copy(
                pair_refs[other].at[:, pl.ds(0, FEATS)], key_held.at[other], key_arrived.at[other]
            ),
            pltpu.make_async_copy(
                pair_refs[other].at[:, pl.ds(FEATS, FEATS)],
                value_held.at[other],
                value_arrived.at[other],
            ),
        )
        for other in range(GRID)
    ]
    for other in sends_order:
        start(pair_copies[other])
    root = math.sqrt(FRAMES * 64)
    totals = []
    for piece in range(GRID):
        parts = [
            total_refs[step][:, pl.ds(((piece - step) % GRID) * ROWS_HERE, ROWS_HERE)]
            for step in range(GRID)
        ]
        top = functools.reduce(jnp.maximum, parts)
        totals.append(top + jnp.log2(sum(jnp.exp2(part - top) for part in parts)))
    totals = jnp.concatenate(totals, axis=1)
    for copy in query_copies + [grad_copy]:
        copy.wait()
    sends = []
    for other in sends_order:
        for copy in pair_copies[other]:
            copy.wait()
        for head in range(HEADS_HERE):
            columns = pl.ds(head * HDIM, HDIM)
            query = query_held[:, :, columns].reshape(BLOCK, HDIM)
            grad = grad_ref[:, :, columns].reshape(BLOCK, HDIM)
            key = key_held[other, :, columns]
            value = value_held[other, :, columns]
            weights = jnp.exp2(
                dot(key, query, NT) * (SCORE_SCALE * LOG2E) - totals[head : head + 1]
            )
            dscore = (weights * (dot(value, grad, NT) - dots_ref[head, 0:1, :])).astype(bf16)
            pair_made[other, 1, :, columns] = (dot(weights.astype(bf16), grad) * root).astype(bf16)
            pair_made[other, 0, :, columns] = (
                dot(dscore, query) * (root * SCORE_SCALE)
            ).astype(bf16)
            part = dot(key.T, dscore)
            if other == sends_order[0]:
                sums[head] = part
            else:
                sums[head] += part
        send = pltpu.make_async_copy(pair_made.at[other], pair_out[other], pair_sent.at[other])
        send.start()
        sends.append(send)
    for piece in sends_order:
        for head in range(HEADS_HERE):
            query_made[piece, :, pl.ds(head * HDIM, HDIM)] = (
                sums[head, :, pl.ds(piece * ROWS_HERE, ROWS_HERE)].T * (root * SCORE_SCALE)
            ).astype(bf16)
        send = pltpu.make_async_copy(query_made.at[piece], query_out[piece], query_sent.at[piece])
        send.start()
        sends.append(send)
    for send in sends:
        send.wait()


def call(kernel, out_shape, in_specs, scratch=(), out_spec=None):
    return pl.pallas_call(
        kernel,
        out_shape=out_shape,
        in_specs=in_specs,
        out_specs=jax.tree.map(lambda _: out_spec or VMEM, out_shape),
        scratch_shapes=list(scratch),
        compiler_params=pltpu.CompilerParams(vmem_limit_bytes=56 * MIB),
        cost_estimate=pl.CostEstimate(flops=10**6, bytes_accessed=10**5, transcendentals=0),
    )


VMEM = pl.BlockSpec(memory_space=pltpu.VMEM)
SMEM = pl.BlockSpec(memory_space=pltpu.SMEM)
ANY = pl.BlockSpec(memory_space=pl.ANY)
HELD = [pltpu.VMEM((GRID, ROWS_HERE, FEATS), bf16)]
ARRIVED = [pltpu.SemaphoreType.DMA((GRID,))]


def shape(dims, dtype):
    return jax.ShapeDtypeStruct(dims, dtype)


def from_ahead(block, axis, step):
    return lax.ppermute(block, axis, [(i, (i - step) % GRID) for i in range(GRID)])


def to_ahead(block, axis, step):
    return lax.ppermute(block, axis, [(i, (i + step) % GRID) for i in range(GRID)])


def gather(block, axis):
    return [block] + [from_ahead(block, axis, step) for step in range(1, GRID)]


def per_device(
    vit_cot,
    vit_pre,
    ln_gain,
    patch_w,
    frame_owner,
    conv_w,
    join_w,
    token_order,
    queries,
    keys,
    values,
    attn_out,
    out_w,
):
    key_values = gather(jnp.concatenate([keys[0], values[0]], axis=1), "hx")
    query_outs = gather(jnp.concatenate([queries[0], attn_out[0]], axis=1), "hy")
    windows = call(
        window_kernel,
        shape((FRAMES, 16, LANES), bf16),
        [VMEM] * 2 + [ANY] * 5,
        scratch=[
            pltpu.VMEM(vit_cot.shape[2:], bf16),
            pltpu.VMEM(vit_pre.shape[2:], bf16),
            pltpu.VMEM(patch_w.shape, bf16),
            pltpu.VMEM((LANES, patch_w.shape[0]), bf16),
            pltpu.VMEM((6 * LANES, LANES), bf16),
            pltpu.VMEM((SIDE * SIDE + 16, LANES), f32),
            pltpu.SemaphoreType.DMA((5,)),
        ],
    )(
        ln_gain,
        token_order,
        vit_pre[0, 0],
        vit_cot[0, 0],
        jnp.asarray(basis_matrix(), bf16),
        patch_w,
        jnp.asarray(spread_matrix(), bf16),
    )
    received = lax.all_to_all(
        windows, ("tm", "hx", "hy"), split_axis=0, concat_axis=0, tiled=True
    )
    joint, picked = call(
        weights_kernel,
        (shape((QUARTERS * LANES, FEATS), bf16), shape((768, QUARTERS * LANES), bf16)),
        [ANY] * 2,
        scratch=[
            pltpu.VMEM(join_w.shape, bf16),
            pltpu.VMEM(out_w.shape, bf16),
            pltpu.SemaphoreType.DMA((2,)),
        ],
    )(join_w, out_w)
    totals = call(
        totals_kernel,
        shape((8, BLOCK), f32),
        [ANY] * (2 * GRID),
        scratch=HELD * 2 + ARRIVED * 2,
    )(*query_outs, *key_values)
    total_pieces = gather(totals, "hy")
    grad_out, row_dots, weight_part = call(
        token_kernel,
        (
            shape((GRID, ROWS_HERE, FEATS), bf16),
            shape((HEADS_HERE, 8, BLOCK), f32),
            shape((768, FEATS), bf16),
        ),
        [SMEM, VMEM] + [ANY] * (3 + GRID),
        scratch=[
            pltpu.VMEM((FRAMES + 2, 16, LANES), bf16),
            pltpu.VMEM((3 * LANES, QUARTERS * LANES), bf16),
            pltpu.VMEM((BLOCK, QUARTERS * LANES), bf16),
        ]
        + [
            pltpu.VMEM((FRAMES, 16, LANES), bf16),
            pltpu.VMEM((QUARTERS * LANES, FEATS), bf16),
            pltpu.VMEM((768, QUARTERS * LANES), bf16),
        ]
        + HELD
        + [pltpu.SemaphoreType.DMA((3,))]
        + ARRIVED,
    )(frame_owner, conv_w, received, joint, picked, *query_outs)
    weight_parts = lax.all_to_all(
        weight_part.reshape(8, 2, 48, FEATS),
        ("core", "hx"),
        split_axis=0,
        concat_axis=0,
        tiled=True,
    )
    weight_half = jnp.sum(weight_parts.astype(f32), axis=0)
    here_z = lax.axis_index("zh")
    weight_other = lax.ppermute(
        lax.dynamic_index_in_dim(weight_half, 1 - here_z, 0, keepdims=False),
        "zh",
        [(0, 1), (1, 0)],
    )
    weight_grad = lax.dynamic_index_in_dim(weight_half, here_z, 0, keepdims=False) + weight_other

    outs = call(
        grads_kernel,
        tuple([shape((ROWS_HERE, FEATS), bf16)] * GRID)
        + tuple([shape((2, ROWS_HERE, FEATS), bf16)] * GRID),
        [ANY] * (2 * GRID) + [VMEM] * GRID + [ANY, VMEM],
        scratch=[pltpu.VMEM((HEADS_HERE, HDIM, BLOCK), f32)]
        + HELD * 5
        + [pltpu.VMEM((GRID, 2, ROWS_HERE, FEATS), bf16)]
        + ARRIVED * 3
        + [pltpu.SemaphoreType.DMA((1,))]
        + ARRIVED * 2,
        out_spec=ANY,
    )(*query_outs, *key_values, *total_pieces, grad_out, row_dots)
    query_parts, pair_parts = outs[:GRID], outs[GRID:]
    pair_back = [pair_parts[0]] + [
        to_ahead(pair_parts[step], "hx", step) for step in range(1, GRID)
    ]
    query_back = [query_parts[0]] + [
        to_ahead(query_parts[step], "hy", step) for step in range(1, GRID)
    ]

    def total(parts):
        return sum(part.astype(f32) for part in parts).astype(bf16)

    query_grad = total(query_back)
    key_grad = total([part[0] for part in pair_back])
    value_grad = total([part[1] for part in pair_back])
    return (query_grad[None], key_grad[None], value_grad[None], weight_grad)


def solution(mesh):
    fine = Mesh(
        mesh.devices.reshape(2, 2, GRID, GRID, GRID), ("zh", "core", "tm", "hx", "hy")
    )
    dp, height = ("zh", "core"), ("hx", "hy")
    rows = P(dp, height, "tm")
    slots = P(dp, ("tm",) + height, None, None)
    placed = (
        slots,
        slots,
        P(),
        P(),
        P(),
        P(),
        P(),
        P(height, "tm"),
        rows,
        rows,
        rows,
        rows,
        P("tm", None),
    )
    return jax.shard_map(
        per_device,
        mesh=fine,
        in_specs=placed,
        out_specs=(rows, rows, rows, P(dp + height, "tm")),
        check_vma=False,
    )
```

```python
import functools
import math

import jax
import jax.numpy as jnp
import numpy as np
from jax import lax
from jax.experimental import pallas as pl
from jax.experimental.pallas import tpu as pltpu
from jax.sharding import Mesh
from jax.sharding import PartitionSpec as P

HDIM = 128
IMG = 224
PATCH = 14
SIDE = IMG // PATCH
GRID = 4
HEADS_HERE = 3
ROWS_HERE = 256
FEATS = HEADS_HERE * HDIM
BLOCK = GRID * ROWS_HERE
FRAMES = 64
LANES = 128
QUARTERS = 4
QUARTER_LANES = 32
TAPS = 27
ORDER_LANE = TAPS
QUARTER_CELLS = (PATCH // 2) * (2 * PATCH)

epsilon = 1e-05
pixel_std = (0.26862954, 0.26130258, 0.27577711)

f32 = jnp.float32
bf16 = jnp.bfloat16
MIB = 1024 * 1024
HIGHEST = lax.Precision.HIGHEST
LOG2E = math.log2(math.e)
SCORE_SCALE = HDIM ** (-0.5)


def row_masks():
    masks = np.zeros((8, PATCH), np.float32)
    for half in range(2):
        for shift in range(3):
            low = half * 7 + shift - 1
            masks[half * 3 + shift, max(low, 0) : min(low + 7, PATCH)] = 1
    masks[6, 0] = 1
    masks[7, PATCH - 1] = 1
    return masks


def basis_matrix():
    rows = row_masks()
    columns = np.zeros((3, PATCH), np.float32)
    columns[0] = 1
    columns[1, 0] = 1
    columns[2, PATCH - 1] = 1
    basis = np.zeros((LANES, 3, PATCH, PATCH), np.float32)
    for col in range(3):
        for row in range(8):
            for channel in range(3):
                basis[col * 24 + row * 3 + channel, channel] = np.outer(rows[row], columns[col])
    return basis.reshape(LANES, 3 * PATCH * PATCH)


def spread_matrix():
    spread = np.zeros((6, LANES, LANES), np.float32)
    for half in range(2):
        for side in range(2):
            first = 2 * side + 1
            terms = {
                0: [(first - 1, 2, 1), (first, 0, 1), (first + 1, 0, 1), (first + 1, 2, -1)],
                1: [(first, 0, 1), (first + 1, 0, 1)],
                2: [(first, 0, 1), (first, 1, -1), (first + 1, 0, 1), (first + 2, 1, 1)],
            }
            for shift in range(3):
                groups = [half * 3 + shift]
                if (half, shift) == (0, 0):
                    groups.append(7)
                if (half, shift) == (1, 2):
                    groups.append(6)
                for offset in range(3):
                    for channel in range(3):
                        lane = (half * 2 + side) * QUARTER_LANES + (shift * 3 + offset) * 3 + channel
                        for place, col, sign in terms[offset]:
                            for row in groups:
                                spread[place, col * 24 + row * 3 + channel, lane] += sign
    return spread.reshape(6 * LANES, LANES)


NN = (((1,), (0,)), ((), ()))
NT = (((1,), (1,)), ((), ()))
TN = (((0,), (0,)), ((), ()))


def dot(left, right, dims=NN):
    return lax.dot_general(left, right, dims, preferred_element_type=f32)


def one_hot(condition):
    return jnp.where(condition, 1.0, 0.0).astype(bf16)


def iota(dims, axis):
    return lax.broadcasted_iota(jnp.int32, dims, axis)


def start(copies):
    for copy in copies:
        copy.start()


def fetch(refs, held, arrived):
    copies = [
        pltpu.make_async_copy(ref, kept, arrived.at[place])
        for place, (ref, kept) in enumerate(zip(refs, held))
    ]
    start(copies)
    return copies


def fetch_halves(refs, column, held, arrived):
    return fetch(
        [ref.at[:, pl.ds(column * FEATS, FEATS)] for ref in refs],
        [held.at[place] for place in range(len(refs))],
        arrived,
    )


def window_kernel(gain_ref, order_ref, *refs):
    out_ref, cot_ref, pre_ref, patch_ref, basis_ref, spread_ref, sums, arrived = refs[5:]
    held = (pre_ref, cot_ref, basis_ref, patch_ref, spread_ref)
    copies = fetch(refs[:5], held, arrived)
    copies[0].wait()
    copies[1].wait()
    pre = pre_ref[...].astype(f32)
    centered = pre - jnp.mean(pre, axis=-1, keepdims=True)
    inverse = lax.rsqrt(jnp.mean(centered * centered, axis=-1, keepdims=True) + epsilon)
    normed = centered * inverse
    scaled = cot_ref[...].astype(f32) * gain_ref[...].astype(f32).reshape(1, -1)
    grad_rows = inverse * (
        scaled
        - jnp.mean(scaled, axis=-1, keepdims=True)
        - normed * jnp.mean(scaled * normed, axis=-1, keepdims=True)
    )
    grad_rows = grad_rows.astype(bf16)
    channel = iota((LANES, 1), 0) % 3
    scale = jnp.where(
        channel == 0, 1.0 / pixel_std[0], jnp.where(channel == 1, 1.0 / pixel_std[1], 1.0 / pixel_std[2])
    ) * (1.0 / QUARTER_CELLS)
    copies[2].wait()
    copies[3].wait()
    weights = dot(basis_ref[...], patch_ref[...]) * scale
    high = weights.astype(bf16)
    low = (weights - high.astype(f32)).astype(bf16)
    both = dot(grad_rows, jnp.concatenate([high, low], axis=0), NT)
    patch_sums = both[:, :LANES] + both[:, LANES:]
    group = (iota((SIDE * SIDE, LANES), 1) // 3) % 8
    edge = jnp.zeros((SIDE, LANES), f32)
    above = jnp.concatenate([edge, patch_sums[:-SIDE]], axis=0)
    below = jnp.concatenate([patch_sums[SIDE:], edge], axis=0)
    patch_sums = jnp.where(group == 7, above, jnp.where(group == 6, below, patch_sums))
    sums[pl.ds(0, 8), :] = jnp.zeros((8, LANES), f32)
    sums[pl.ds(8 + SIDE * SIDE, 8), :] = jnp.zeros((8, LANES), f32)
    sums[pl.ds(8, SIDE * SIDE), :] = patch_sums
    copies[4].wait()
    column = iota((SIDE * GRID, LANES), 0) % GRID
    total = jnp.zeros((SIDE * GRID, LANES), f32)
    for place in range(6):
        picked = sums[pl.ds(7 + place, SIDE * GRID, stride=GRID), :]
        if place == 0:
            picked = jnp.where(column == 0, 0.0, picked)
        if place == 5:
            picked = jnp.where(column == GRID - 1, 0.0, picked)
        high = picked.astype(bf16)
        low = (picked - high.astype(f32)).astype(bf16)
        both = dot(
            jnp.concatenate([high, low], axis=0), spread_ref[pl.ds(place * LANES, LANES), :]
        )
        total = total + (both[: SIDE * GRID] + both[SIDE * GRID :])
    windows = total.astype(bf16)
    entries = jnp.where(
        iota((16, 64), 1) % 16 == iota((16, 64), 0), order_ref[...].astype(f32), 0.0
    ).astype(bf16)
    order = dot(entries, one_hot(iota((64, LANES), 1) == ORDER_LANE + iota((64, LANES), 0) // 16))
    order = order.astype(bf16)
    for target_x in range(GRID):
        block = windows[target_x * 16 : (target_x + 1) * 16] + order
        for target_t in range(GRID):
            for target_y in range(GRID):
                out_ref[(target_t * GRID + target_x) * GRID + target_y] = block


def weights_kernel(join_from, out_w_from, joint_ref, picked_ref, join_ref, out_w_ref, arrived):
    here_y = lax.axis_index("hy")
    copies = fetch([join_from, out_w_from], [join_ref, out_w_ref], arrived)
    copies[0].wait()
    copies[1].wait()
    joint_ref[...] = dot(join_ref[...], out_w_ref[...], NT).astype(bf16)
    row, column = iota((96, 384), 0), iota((96, 384), 1)
    half = row // 48
    pick = one_hot(column == half * 192 + here_y * 48 + (row - half * 48))
    for pair in range(8):
        rows = dot(pick, join_ref[:, pl.ds(pair * 384, 384)], NT).astype(bf16)
        z, core, x = pair // 4, (pair % 4) // 2, (pair % 2) * 2
        for step in range(2):
            picked_ref[pl.ds((core * GRID + x + step) * 96 + z * 48, 48), :] = rows[
                step * 48 : (step + 1) * 48
            ]


def totals_kernel(*refs):
    out_ref, query_held, key_held, query_arrived, key_arrived = refs[2 * GRID :]
    key_copies = fetch_halves(refs[GRID : 2 * GRID], 0, key_held, key_arrived)
    query_copies = fetch_halves(refs[:GRID], 0, query_held, query_arrived)
    for copy in key_copies:
        copy.wait()
    for head in range(HEADS_HERE):
        columns = pl.ds(head * HDIM, HDIM)
        for piece in range(GRID):
            if head == 0:
                query_copies[piece].wait()
            query = query_held[piece, :, columns]
            scores = [dot(key_held[other, :, columns], query, NT) for other in range(GRID)]
            top = functools.reduce(
                jnp.maximum, [jnp.max(tile, axis=0, keepdims=True) for tile in scores]
            ) * (SCORE_SCALE * LOG2E)
            total = sum(
                jnp.sum(jnp.exp2(tile * (SCORE_SCALE * LOG2E) - top), axis=0, keepdims=True)
                for tile in scores
            )
            out_ref[pl.ds(head, 1), pl.ds(piece * ROWS_HERE, ROWS_HERE)] = top + jnp.log2(total)
    out_ref[pl.ds(HEADS_HERE, 8 - HEADS_HERE), :] = jnp.zeros((8 - HEADS_HERE, BLOCK), f32)


def token_part(owner_ref, conv_ref, recv_ref, arrivals, frames, conv_big, ordered):
    here_x = lax.axis_index("hx")
    here_y = lax.axis_index("hy")
    frames[0] = jnp.zeros((16, LANES), bf16)
    frames[FRAMES + 1] = jnp.zeros((16, LANES), bf16)
    row, column = iota((3 * QUARTER_LANES, 3 * TAPS), 0), iota((3 * QUARTER_LANES, 3 * TAPS), 1)
    tap = row % QUARTER_LANES
    conv = dot(
        one_hot((tap < TAPS) & (column == (row // QUARTER_LANES) * TAPS + tap)), conv_ref[...]
    ).astype(bf16)
    conv_big[...] = jnp.zeros_like(conv_big)
    for quarter in range(QUARTERS):
        for shift in range(3):
            conv_big[
                pl.ds(shift * LANES + quarter * QUARTER_LANES, QUARTER_LANES),
                pl.ds(quarter * LANES, LANES),
            ] = conv[shift * QUARTER_LANES : (shift + 1) * QUARTER_LANES]
    arrivals.wait()

    def place_frame(frame, carry):
        frames[frame + 1] = recv_ref[(frame // 16) * 16 + owner_ref[frame]]
        return carry

    lax.fori_loop(0, FRAMES, place_frame, 0, unroll=8)
    lane = iota((16, ROWS_HERE), 1)
    for slab_t in range(GRID):
        pooled = sum(
            dot(
                frames[pl.ds(slab_t * 16 + shift, 16)].reshape(ROWS_HERE, LANES),
                conv_big[pl.ds(shift * LANES, LANES), :],
            )
            for shift in range(3)
        ).astype(bf16)
        pieces = []
        for piece in range(GRID):
            slab = lax.rem(here_y + piece, GRID)
            block = recv_ref[slab_t * 16 + here_x * GRID + slab].astype(f32)
            for part in range(4):
                order = block[:, ORDER_LANE + part : ORDER_LANE + part + 1].astype(jnp.int32)
                target = (order // 4) * 16 + slab * 4 + lax.rem(order, 4)
                pieces.append(one_hot(lane == target))
        chosen = dot(jnp.concatenate(pieces, axis=0), pooled).astype(bf16)
        for piece in range(GRID):
            ordered[pl.ds(piece * ROWS_HERE + slab_t * 64, 64), :] = chosen[
                piece * 64 : (piece + 1) * 64
            ]


def grads_kernel(owner_ref, conv_ref, *refs):
    total_refs, (recv_from, joint_from, picked_from) = refs[:GRID], refs[GRID : GRID + 3]
    query_refs, pair_refs = refs[GRID + 3 : 2 * GRID + 3], refs[2 * GRID + 3 : 3 * GRID + 3]
    rest = refs[3 * GRID + 3 :]
    query_out, pair_out, weight_out = rest[:GRID], rest[GRID : 2 * GRID], rest[2 * GRID]
    (
        frames,
        conv_big,
        ordered,
        recv_ref,
        joint_ref,
        picked_ref,
        weight_made,
        dots_ref,
        sums,
        out_held,
        query_held,
        key_held,
        value_held,
        grad_ref,
        query_made,
        pair_made,
        first_arrived,
        out_arrived,
        query_arrived,
        key_arrived,
        value_arrived,
        query_sent,
        pair_sent,
        weight_sent,
    ) = rest[2 * GRID + 1 :]
    sends_order = (2, 1, 3, 0)
    firsts = fetch(
        [recv_from, joint_from, picked_from], [recv_ref, joint_ref, picked_ref], first_arrived
    )
    out_copies = fetch_halves(query_refs, 1, out_held, out_arrived)
    query_copies = fetch_halves(query_refs, 0, query_held, query_arrived)
    key_copies = fetch_halves(pair_refs, 0, key_held, key_arrived)
    value_copies = fetch_halves(pair_refs, 1, value_held, value_arrived)
    token_part(owner_ref, conv_ref, recv_ref, firsts[0], frames, conv_big, ordered)
    firsts[1].wait()
    ones = jnp.ones((8, 2 * HDIM), bf16)
    outer = jnp.zeros((QUARTERS * LANES, FEATS), f32)
    for piece in range(GRID):
        rows = ordered[pl.ds(piece * ROWS_HERE, ROWS_HERE), :]
        grads = dot(rows, joint_ref[...]).astype(bf16)
        grad_ref[piece] = grads
        out_copies[piece].wait()
        outs = out_held[piece]
        products = grads.astype(f32) * outs.astype(f32)
        high = products.astype(bf16)
        low = (products - high.astype(f32)).astype(bf16)
        for head in range(HEADS_HERE):
            columns = slice(head * HDIM, (head + 1) * HDIM)
            both = jnp.concatenate([high[:, columns], low[:, columns]], axis=1)
            dots_ref[head, :, pl.ds(piece * ROWS_HERE, ROWS_HERE)] = dot(ones, both, NT)
        outer = outer + dot(rows, outs, TN)
    firsts[2].wait()
    weight_made[...] = (
        dot(picked_ref[...], outer.astype(bf16)) * (1.0 / math.sqrt(FRAMES * 64 * 4))
    ).astype(bf16)
    sends = fetch([weight_made], [weight_out], weight_sent)
    root = math.sqrt(FRAMES * 64)
    totals = []
    for piece in range(GRID):
        parts = [
            total_refs[step][:, pl.ds(((piece - step) % GRID) * ROWS_HERE, ROWS_HERE)]
            for step in range(GRID)
        ]
        top = functools.reduce(jnp.maximum, parts)
        totals.append(top + jnp.log2(sum(jnp.exp2(part - top) for part in parts)))
    totals = jnp.concatenate(totals, axis=1)
    for copy in query_copies:
        copy.wait()
    for other in sends_order:
        key_copies[other].wait()
        value_copies[other].wait()
        for head in range(HEADS_HERE):
            columns = pl.ds(head * HDIM, HDIM)
            query = query_held[:, :, columns].reshape(BLOCK, HDIM)
            grad = grad_ref[:, :, columns].reshape(BLOCK, HDIM)
            key = key_held[other, :, columns]
            value = value_held[other, :, columns]
            weights = jnp.exp2(
                dot(key, query, NT) * (SCORE_SCALE * LOG2E) - totals[head : head + 1]
            )
            dscore = (weights * (dot(value, grad, NT) - dots_ref[head, 0:1, :])).astype(bf16)
            pair_made[other, 1, :, columns] = (dot(weights.astype(bf16), grad) * root).astype(bf16)
            pair_made[other, 0, :, columns] = (
                dot(dscore, query) * (root * SCORE_SCALE)
            ).astype(bf16)
            part = dot(key.T, dscore)
            if other == sends_order[0]:
                sums[head] = part
            else:
                sums[head] += part
        send = pltpu.make_async_copy(pair_made.at[other], pair_out[other], pair_sent.at[other])
        send.start()
        sends.append(send)
    for piece in sends_order:
        for head in range(HEADS_HERE):
            query_made[piece, :, pl.ds(head * HDIM, HDIM)] = (
                sums[head, :, pl.ds(piece * ROWS_HERE, ROWS_HERE)].T * (root * SCORE_SCALE)
            ).astype(bf16)
        send = pltpu.make_async_copy(query_made.at[piece], query_out[piece], query_sent.at[piece])
        send.start()
        sends.append(send)
    for send in sends:
        send.wait()


def call(kernel, out_shape, in_specs, scratch=(), out_spec=None):
    return pl.pallas_call(
        kernel,
        out_shape=out_shape,
        in_specs=in_specs,
        out_specs=jax.tree.map(lambda _: out_spec or VMEM, out_shape),
        scratch_shapes=list(scratch),
        compiler_params=pltpu.CompilerParams(vmem_limit_bytes=56 * MIB),
        cost_estimate=pl.CostEstimate(flops=10**6, bytes_accessed=10**5, transcendentals=0),
    )


VMEM = pl.BlockSpec(memory_space=pltpu.VMEM)
SMEM = pl.BlockSpec(memory_space=pltpu.SMEM)
ANY = pl.BlockSpec(memory_space=pl.ANY)
HELD = [pltpu.VMEM((GRID, ROWS_HERE, FEATS), bf16)]
ARRIVED = [pltpu.SemaphoreType.DMA((GRID,))]


def shape(dims, dtype):
    return jax.ShapeDtypeStruct(dims, dtype)


def from_ahead(block, axis, step):
    return lax.ppermute(block, axis, [(i, (i - step) % GRID) for i in range(GRID)])


def to_ahead(block, axis, step):
    return lax.ppermute(block, axis, [(i, (i + step) % GRID) for i in range(GRID)])


def gather(block, axis):
    return [block] + [from_ahead(block, axis, step) for step in range(1, GRID)]


def per_device(
    vit_cot,
    vit_pre,
    ln_gain,
    patch_w,
    frame_owner,
    conv_w,
    join_w,
    token_order,
    queries,
    keys,
    values,
    attn_out,
    out_w,
):
    key_values = gather(jnp.concatenate([keys[0], values[0]], axis=1), "hx")
    query_outs = gather(jnp.concatenate([queries[0], attn_out[0]], axis=1), "hy")
    windows = call(
        window_kernel,
        shape((FRAMES, 16, LANES), bf16),
        [VMEM] * 2 + [ANY] * 5,
        scratch=[
            pltpu.VMEM(vit_cot.shape[2:], bf16),
            pltpu.VMEM(vit_pre.shape[2:], bf16),
            pltpu.VMEM(patch_w.shape, bf16),
            pltpu.VMEM((LANES, patch_w.shape[0]), bf16),
            pltpu.VMEM((6 * LANES, LANES), bf16),
            pltpu.VMEM((SIDE * SIDE + 16, LANES), f32),
            pltpu.SemaphoreType.DMA((5,)),
        ],
    )(
        ln_gain,
        token_order,
        vit_pre[0, 0],
        vit_cot[0, 0],
        jnp.asarray(basis_matrix(), bf16),
        patch_w,
        jnp.asarray(spread_matrix(), bf16),
    )
    join_late, windows = lax.optimization_barrier((join_w, windows))
    joint, picked = call(
        weights_kernel,
        (shape((QUARTERS * LANES, FEATS), bf16), shape((768, QUARTERS * LANES), bf16)),
        [ANY] * 2,
        scratch=[
            pltpu.VMEM(join_w.shape, bf16),
            pltpu.VMEM(out_w.shape, bf16),
            pltpu.SemaphoreType.DMA((2,)),
        ],
    )(join_late, out_w)
    windows, joint, picked, query_outs, key_values = lax.optimization_barrier(
        (windows, joint, picked, query_outs, key_values)
    )
    received = lax.all_to_all(
        windows, ("tm", "hx", "hy"), split_axis=0, concat_axis=0, tiled=True
    )
    totals = call(
        totals_kernel,
        shape((8, BLOCK), f32),
        [ANY] * (2 * GRID),
        scratch=HELD * 2 + ARRIVED * 2,
    )(*query_outs, *key_values)
    total_pieces = gather(totals, "hy")
    outs = call(
        grads_kernel,
        tuple([shape((ROWS_HERE, FEATS), bf16)] * GRID)
        + tuple([shape((2, ROWS_HERE, FEATS), bf16)] * GRID)
        + (shape((768, FEATS), bf16),),
        [SMEM] + [VMEM] * (1 + GRID) + [ANY] * (3 + 2 * GRID),
        scratch=[
            pltpu.VMEM((FRAMES + 2, 16, LANES), bf16),
            pltpu.VMEM((3 * LANES, QUARTERS * LANES), bf16),
            pltpu.VMEM((BLOCK, QUARTERS * LANES), bf16),
            pltpu.VMEM((FRAMES, 16, LANES), bf16),
            pltpu.VMEM((QUARTERS * LANES, FEATS), bf16),
            pltpu.VMEM((768, QUARTERS * LANES), bf16),
            pltpu.VMEM((768, FEATS), bf16),
            pltpu.VMEM((HEADS_HERE, 8, BLOCK), f32),
            pltpu.VMEM((HEADS_HERE, HDIM, BLOCK), f32),
        ]
        + HELD * 6
        + [pltpu.VMEM((GRID, 2, ROWS_HERE, FEATS), bf16), pltpu.SemaphoreType.DMA((3,))]
        + ARRIVED * 6
        + [pltpu.SemaphoreType.DMA((1,))],
        out_spec=ANY,
    )(frame_owner, conv_w, *total_pieces, received, joint, picked, *query_outs, *key_values)
    query_parts, pair_parts, weight_part = outs[:GRID], outs[GRID : 2 * GRID], outs[2 * GRID]
    weight_parts = lax.all_to_all(
        weight_part.reshape(8, 2, 48, FEATS),
        ("core", "hx"),
        split_axis=0,
        concat_axis=0,
        tiled=True,
    )
    weight_half = jnp.sum(weight_parts.astype(f32), axis=0)
    here_z = lax.axis_index("zh")
    weight_other = lax.ppermute(
        lax.dynamic_index_in_dim(weight_half, 1 - here_z, 0, keepdims=False),
        "zh",
        [(0, 1), (1, 0)],
    )
    weight_grad = lax.dynamic_index_in_dim(weight_half, here_z, 0, keepdims=False) + weight_other

    pair_back = [pair_parts[0]] + [
        to_ahead(pair_parts[step], "hx", step) for step in range(1, GRID)
    ]
    query_back = [query_parts[0]] + [
        to_ahead(query_parts[step], "hy", step) for step in range(1, GRID)
    ]

    def total(parts):
        return sum(part.astype(f32) for part in parts).astype(bf16)

    query_grad = total(query_back)
    key_grad = total([part[0] for part in pair_back])
    value_grad = total([part[1] for part in pair_back])
    return (query_grad[None], key_grad[None], value_grad[None], weight_grad)


def solution(mesh):
    fine = Mesh(
        mesh.devices.reshape(2, 2, GRID, GRID, GRID), ("zh", "core", "tm", "hx", "hy")
    )
    dp, height = ("zh", "core"), ("hx", "hy")
    rows = P(dp, height, "tm")
    slots = P(dp, ("tm",) + height, None, None)
    placed = (
        slots,
        slots,
        P(),
        P(),
        P(),
        P(),
        P(),
        P(height, "tm"),
        rows,
        rows,
        rows,
        rows,
        P("tm", None),
    )
    return jax.shard_map(
        per_device,
        mesh=fine,
        in_specs=placed,
        out_specs=(rows, rows, rows, P(dp + height, "tm")),
        check_vma=False,
    )
```

```python
import functools
import math

import jax
import jax.numpy as jnp
import numpy as np
from jax import lax
from jax.experimental import pallas as pl
from jax.experimental.pallas import tpu as pltpu
from jax.sharding import Mesh
from jax.sharding import PartitionSpec as P

HDIM = 128
IMG = 224
PATCH = 14
SIDE = IMG // PATCH
GRID = 4
HEADS_HERE = 3
ROWS_HERE = 256
FEATS = HEADS_HERE * HDIM
BLOCK = GRID * ROWS_HERE
FRAMES = 64
LANES = 128
QUARTERS = 4
QUARTER_LANES = 32
TAPS = 27
ORDER_LANE = TAPS
QUARTER_CELLS = (PATCH // 2) * (2 * PATCH)

epsilon = 1e-05
pixel_std = (0.26862954, 0.26130258, 0.27577711)

f32 = jnp.float32
bf16 = jnp.bfloat16
MIB = 1024 * 1024
HIGHEST = lax.Precision.HIGHEST
LOG2E = math.log2(math.e)
SCORE_SCALE = HDIM ** (-0.5)


def row_masks():
    masks = np.zeros((8, PATCH), np.float32)
    for half in range(2):
        for shift in range(3):
            low = half * 7 + shift - 1
            masks[half * 3 + shift, max(low, 0) : min(low + 7, PATCH)] = 1
    masks[6, 0] = 1
    masks[7, PATCH - 1] = 1
    return masks


def basis_matrix():
    rows = row_masks()
    columns = np.zeros((3, PATCH), np.float32)
    columns[0] = 1
    columns[1, 0] = 1
    columns[2, PATCH - 1] = 1
    basis = np.zeros((LANES, 3, PATCH, PATCH), np.float32)
    for col in range(3):
        for row in range(8):
            for channel in range(3):
                basis[col * 24 + row * 3 + channel, channel] = np.outer(rows[row], columns[col])
    return basis.reshape(LANES, 3 * PATCH * PATCH)


def spread_matrix():
    spread = np.zeros((6, LANES, LANES), np.float32)
    for half in range(2):
        for side in range(2):
            first = 2 * side + 1
            terms = {
                0: [(first - 1, 2, 1), (first, 0, 1), (first + 1, 0, 1), (first + 1, 2, -1)],
                1: [(first, 0, 1), (first + 1, 0, 1)],
                2: [(first, 0, 1), (first, 1, -1), (first + 1, 0, 1), (first + 2, 1, 1)],
            }
            for shift in range(3):
                groups = [half * 3 + shift]
                if (half, shift) == (0, 0):
                    groups.append(7)
                if (half, shift) == (1, 2):
                    groups.append(6)
                for offset in range(3):
                    for channel in range(3):
                        lane = (half * 2 + side) * QUARTER_LANES + (shift * 3 + offset) * 3 + channel
                        for place, col, sign in terms[offset]:
                            for row in groups:
                                spread[place, col * 24 + row * 3 + channel, lane] += sign
    return spread.reshape(6 * LANES, LANES)


NN = (((1,), (0,)), ((), ()))
NT = (((1,), (1,)), ((), ()))
TN = (((0,), (0,)), ((), ()))


def dot(left, right, dims=NN):
    return lax.dot_general(left, right, dims, preferred_element_type=f32)


def one_hot(condition):
    return jnp.where(condition, 1.0, 0.0).astype(bf16)


def iota(dims, axis):
    return lax.broadcasted_iota(jnp.int32, dims, axis)


def start(copies):
    for copy in copies:
        copy.start()


def fetch(refs, held, arrived):
    copies = [
        pltpu.make_async_copy(ref, kept, arrived.at[place])
        for place, (ref, kept) in enumerate(zip(refs, held))
    ]
    start(copies)
    return copies


def fetch_halves(refs, column, held, arrived):
    return fetch(
        [ref.at[:, pl.ds(column * FEATS, FEATS)] for ref in refs],
        [held.at[place] for place in range(len(refs))],
        arrived,
    )


def window_kernel(gain_ref, order_ref, *refs):
    out_ref, cot_ref, pre_ref, patch_ref, basis_ref, spread_ref, sums, arrived = refs[5:]
    held = (pre_ref, cot_ref, basis_ref, patch_ref, spread_ref)
    copies = fetch(refs[:5], held, arrived)
    copies[0].wait()
    copies[1].wait()
    pre = pre_ref[...].astype(f32)
    centered = pre - jnp.mean(pre, axis=-1, keepdims=True)
    inverse = lax.rsqrt(jnp.mean(centered * centered, axis=-1, keepdims=True) + epsilon)
    normed = centered * inverse
    scaled = cot_ref[...].astype(f32) * gain_ref[...].astype(f32).reshape(1, -1)
    grad_rows = inverse * (
        scaled
        - jnp.mean(scaled, axis=-1, keepdims=True)
        - normed * jnp.mean(scaled * normed, axis=-1, keepdims=True)
    )
    grad_rows = grad_rows.astype(bf16)
    channel = iota((LANES, 1), 0) % 3
    scale = jnp.where(
        channel == 0, 1.0 / pixel_std[0], jnp.where(channel == 1, 1.0 / pixel_std[1], 1.0 / pixel_std[2])
    ) * (1.0 / QUARTER_CELLS)
    copies[2].wait()
    copies[3].wait()
    weights = dot(basis_ref[...], patch_ref[...]) * scale
    high = weights.astype(bf16)
    low = (weights - high.astype(f32)).astype(bf16)
    both = dot(grad_rows, jnp.concatenate([high, low], axis=0), NT)
    patch_sums = both[:, :LANES] + both[:, LANES:]
    group = (iota((SIDE * SIDE, LANES), 1) // 3) % 8
    edge = jnp.zeros((SIDE, LANES), f32)
    above = jnp.concatenate([edge, patch_sums[:-SIDE]], axis=0)
    below = jnp.concatenate([patch_sums[SIDE:], edge], axis=0)
    patch_sums = jnp.where(group == 7, above, jnp.where(group == 6, below, patch_sums))
    sums[pl.ds(0, 8), :] = jnp.zeros((8, LANES), f32)
    sums[pl.ds(8 + SIDE * SIDE, 8), :] = jnp.zeros((8, LANES), f32)
    sums[pl.ds(8, SIDE * SIDE), :] = patch_sums
    copies[4].wait()
    column = iota((SIDE * GRID, LANES), 0) % GRID
    total = jnp.zeros((SIDE * GRID, LANES), f32)
    for place in range(6):
        picked = sums[pl.ds(7 + place, SIDE * GRID, stride=GRID), :]
        if place == 0:
            picked = jnp.where(column == 0, 0.0, picked)
        if place == 5:
            picked = jnp.where(column == GRID - 1, 0.0, picked)
        high = picked.astype(bf16)
        low = (picked - high.astype(f32)).astype(bf16)
        both = dot(
            jnp.concatenate([high, low], axis=0), spread_ref[pl.ds(place * LANES, LANES), :]
        )
        total = total + (both[: SIDE * GRID] + both[SIDE * GRID :])
    windows = total.astype(bf16)
    entries = jnp.where(
        iota((16, 64), 1) % 16 == iota((16, 64), 0), order_ref[...].astype(f32), 0.0
    ).astype(bf16)
    order = dot(entries, one_hot(iota((64, LANES), 1) == ORDER_LANE + iota((64, LANES), 0) // 16))
    order = order.astype(bf16)
    for target_x in range(GRID):
        block = windows[target_x * 16 : (target_x + 1) * 16] + order
        for target_t in range(GRID):
            for target_y in range(GRID):
                out_ref[(target_t * GRID + target_x) * GRID + target_y] = block


def weights_kernel(join_from, out_w_from, joint_ref, picked_ref, join_ref, out_w_ref, arrived):
    here_y = lax.axis_index("hy")
    copies = fetch([join_from, out_w_from], [join_ref, out_w_ref], arrived)
    copies[0].wait()
    copies[1].wait()
    joint_ref[...] = dot(join_ref[...], out_w_ref[...], NT).astype(bf16)
    row, column = iota((96, 384), 0), iota((96, 384), 1)
    half = row // 48
    pick = one_hot(column == half * 192 + here_y * 48 + (row - half * 48))
    for pair in range(8):
        rows = dot(pick, join_ref[:, pl.ds(pair * 384, 384)], NT).astype(bf16)
        z, core, x = pair // 4, (pair % 4) // 2, (pair % 2) * 2
        for step in range(2):
            picked_ref[pl.ds((core * GRID + x + step) * 96 + z * 48, 48), :] = rows[
                step * 48 : (step + 1) * 48
            ]


def totals_kernel(*refs):
    out_ref, query_held, key_held, query_arrived, key_arrived = refs[2 * GRID :]
    key_copies = fetch_halves(refs[GRID : 2 * GRID], 0, key_held, key_arrived)
    query_copies = fetch_halves(refs[:GRID], 0, query_held, query_arrived)
    for copy in key_copies:
        copy.wait()
    for head in range(HEADS_HERE):
        columns = pl.ds(head * HDIM, HDIM)
        for piece in range(GRID):
            if head == 0:
                query_copies[piece].wait()
            query = query_held[piece, :, columns]
            scores = [dot(key_held[other, :, columns], query, NT) for other in range(GRID)]
            top = functools.reduce(
                jnp.maximum, [jnp.max(tile, axis=0, keepdims=True) for tile in scores]
            ) * (SCORE_SCALE * LOG2E)
            total = sum(
                jnp.sum(jnp.exp2(tile * (SCORE_SCALE * LOG2E) - top), axis=0, keepdims=True)
                for tile in scores
            )
            out_ref[pl.ds(head, 1), pl.ds(piece * ROWS_HERE, ROWS_HERE)] = top + jnp.log2(total)
    out_ref[pl.ds(HEADS_HERE, 8 - HEADS_HERE), :] = jnp.zeros((8 - HEADS_HERE, BLOCK), f32)


def token_part(owner_ref, conv_ref, recv_ref, arrivals, frames, conv_big, ordered):
    here_x = lax.axis_index("hx")
    here_y = lax.axis_index("hy")
    frames[0] = jnp.zeros((16, LANES), bf16)
    frames[FRAMES + 1] = jnp.zeros((16, LANES), bf16)
    row, column = iota((3 * QUARTER_LANES, 3 * TAPS), 0), iota((3 * QUARTER_LANES, 3 * TAPS), 1)
    tap = row % QUARTER_LANES
    conv = dot(
        one_hot((tap < TAPS) & (column == (row // QUARTER_LANES) * TAPS + tap)), conv_ref[...]
    ).astype(bf16)
    conv_big[...] = jnp.zeros_like(conv_big)
    for quarter in range(QUARTERS):
        for shift in range(3):
            conv_big[
                pl.ds(shift * LANES + quarter * QUARTER_LANES, QUARTER_LANES),
                pl.ds(quarter * LANES, LANES),
            ] = conv[shift * QUARTER_LANES : (shift + 1) * QUARTER_LANES]
    arrivals.wait()

    def place_frame(frame, carry):
        frames[frame + 1] = recv_ref[(frame // 16) * 16 + owner_ref[frame]]
        return carry

    lax.fori_loop(0, FRAMES, place_frame, 0, unroll=8)
    lane = iota((16, ROWS_HERE), 1)
    for slab_t in range(GRID):
        pooled = sum(
            dot(
                frames[pl.ds(slab_t * 16 + shift, 16)].reshape(ROWS_HERE, LANES),
                conv_big[pl.ds(shift * LANES, LANES), :],
            )
            for shift in range(3)
        ).astype(bf16)
        pieces = []
        for piece in range(GRID):
            slab = lax.rem(here_y + piece, GRID)
            block = recv_ref[slab_t * 16 + here_x * GRID + slab].astype(f32)
            for part in range(4):
                order = block[:, ORDER_LANE + part : ORDER_LANE + part + 1].astype(jnp.int32)
                target = (order // 4) * 16 + slab * 4 + lax.rem(order, 4)
                pieces.append(one_hot(lane == target))
        chosen = dot(jnp.concatenate(pieces, axis=0), pooled).astype(bf16)
        for piece in range(GRID):
            ordered[pl.ds(piece * ROWS_HERE + slab_t * 64, 64), :] = chosen[
                piece * 64 : (piece + 1) * 64
            ]


def grads_kernel(owner_ref, conv_ref, *refs):
    total_refs, (recv_from, joint_from, picked_from) = refs[:GRID], refs[GRID : GRID + 3]
    query_refs, pair_refs = refs[GRID + 3 : 2 * GRID + 3], refs[2 * GRID + 3 : 3 * GRID + 3]
    rest = refs[3 * GRID + 3 :]
    query_out, pair_out, weight_out = rest[:GRID], rest[GRID : 2 * GRID], rest[2 * GRID]
    (
        frames,
        conv_big,
        ordered,
        recv_ref,
        joint_ref,
        picked_ref,
        weight_made,
        dots_ref,
        sums,
        out_held,
        query_held,
        key_held,
        value_held,
        grad_ref,
        query_made,
        pair_made,
        first_arrived,
        out_arrived,
        query_arrived,
        key_arrived,
        value_arrived,
        query_sent,
        pair_sent,
        weight_sent,
    ) = rest[2 * GRID + 1 :]
    sends_order = (2, 1, 3, 0)
    firsts = fetch(
        [recv_from, joint_from, picked_from], [recv_ref, joint_ref, picked_ref], first_arrived
    )
    out_copies = fetch_halves(query_refs, 1, out_held, out_arrived)
    query_copies = fetch_halves(query_refs, 0, query_held, query_arrived)
    key_copies = fetch_halves(pair_refs, 0, key_held, key_arrived)
    value_copies = fetch_halves(pair_refs, 1, value_held, value_arrived)
    token_part(owner_ref, conv_ref, recv_ref, firsts[0], frames, conv_big, ordered)
    firsts[1].wait()
    ones = jnp.ones((8, 2 * HDIM), bf16)
    outer = jnp.zeros((QUARTERS * LANES, FEATS), f32)
    for piece in range(GRID):
        rows = ordered[pl.ds(piece * ROWS_HERE, ROWS_HERE), :]
        grads = dot(rows, joint_ref[...]).astype(bf16)
        grad_ref[piece] = grads
        out_copies[piece].wait()
        outs = out_held[piece]
        products = grads.astype(f32) * outs.astype(f32)
        high = products.astype(bf16)
        low = (products - high.astype(f32)).astype(bf16)
        for head in range(HEADS_HERE):
            columns = slice(head * HDIM, (head + 1) * HDIM)
            both = jnp.concatenate([high[:, columns], low[:, columns]], axis=1)
            dots_ref[head, :, pl.ds(piece * ROWS_HERE, ROWS_HERE)] = dot(ones, both, NT)
        outer = outer + dot(rows, outs, TN)
    firsts[2].wait()
    weight_made[...] = (
        dot(picked_ref[...], outer.astype(bf16)) * (1.0 / math.sqrt(FRAMES * 64 * 4))
    ).astype(bf16)
    sends = fetch([weight_made], [weight_out], weight_sent)
    root = math.sqrt(FRAMES * 64)
    totals = []
    for piece in range(GRID):
        parts = [
            total_refs[step][:, pl.ds(((piece - step) % GRID) * ROWS_HERE, ROWS_HERE)]
            for step in range(GRID)
        ]
        top = functools.reduce(jnp.maximum, parts)
        totals.append(top + jnp.log2(sum(jnp.exp2(part - top) for part in parts)))
    totals = jnp.concatenate(totals, axis=1)
    for copy in query_copies:
        copy.wait()
    for other in sends_order:
        key_copies[other].wait()
        value_copies[other].wait()
        for head in range(HEADS_HERE):
            columns = pl.ds(head * HDIM, HDIM)
            query = query_held[:, :, columns].reshape(BLOCK, HDIM)
            grad = grad_ref[:, :, columns].reshape(BLOCK, HDIM)
            key = key_held[other, :, columns]
            value = value_held[other, :, columns]
            weights = jnp.exp2(
                dot(key, query, NT) * (SCORE_SCALE * LOG2E) - totals[head : head + 1]
            )
            dscore = (weights * (dot(value, grad, NT) - dots_ref[head, 0:1, :])).astype(bf16)
            pair_made[other, 1, :, columns] = (dot(weights.astype(bf16), grad) * root).astype(bf16)
            pair_made[other, 0, :, columns] = (
                dot(dscore, query) * (root * SCORE_SCALE)
            ).astype(bf16)
            part = dot(key.T, dscore)
            if other == sends_order[0]:
                sums[head] = part
            else:
                sums[head] += part
        send = pltpu.make_async_copy(pair_made.at[other], pair_out[other], pair_sent.at[other])
        send.start()
        sends.append(send)
    for piece in sends_order:
        for head in range(HEADS_HERE):
            query_made[piece, :, pl.ds(head * HDIM, HDIM)] = (
                sums[head, :, pl.ds(piece * ROWS_HERE, ROWS_HERE)].T * (root * SCORE_SCALE)
            ).astype(bf16)
        send = pltpu.make_async_copy(query_made.at[piece], query_out[piece], query_sent.at[piece])
        send.start()
        sends.append(send)
    for send in sends:
        send.wait()


def half_kernel(parts_ref, kept_ref, sent_ref):
    here_z = lax.axis_index("zh")
    for out_ref, half in ((kept_ref, here_z), (sent_ref, 1 - here_z)):
        out_ref[...] = sum(parts_ref[source, half].astype(f32) for source in range(2 * GRID))


def sum_kernel(kept_ref, other_ref, *refs):
    pair_refs, query_refs = refs[:GRID], refs[GRID : 2 * GRID]
    query_out, key_out, value_out, weight_out, query_held, pair_held, *arrived = refs[2 * GRID :]
    pair_copies = fetch(pair_refs, [pair_held.at[step] for step in range(GRID)], arrived[1])
    query_copies = fetch(query_refs, [query_held.at[step] for step in range(GRID)], arrived[0])
    weight_out[...] = kept_ref[...] + other_ref[...]
    for copy in query_copies:
        copy.wait()
    query_out[0] = sum(query_held[step].astype(f32) for step in range(GRID)).astype(bf16)
    for copy in pair_copies:
        copy.wait()
    for place, out_ref in enumerate((key_out, value_out)):
        out_ref[0] = sum(pair_held[step, place].astype(f32) for step in range(GRID)).astype(bf16)


def call(kernel, out_shape, in_specs, scratch=(), out_spec=None, limit=56):
    return pl.pallas_call(
        kernel,
        out_shape=out_shape,
        in_specs=in_specs,
        out_specs=jax.tree.map(lambda _: out_spec or VMEM, out_shape),
        scratch_shapes=list(scratch),
        compiler_params=pltpu.CompilerParams(vmem_limit_bytes=limit * MIB),
        cost_estimate=pl.CostEstimate(flops=10**6, bytes_accessed=10**5, transcendentals=0),
    )


VMEM = pl.BlockSpec(memory_space=pltpu.VMEM)
SMEM = pl.BlockSpec(memory_space=pltpu.SMEM)
ANY = pl.BlockSpec(memory_space=pl.ANY)
HELD = [pltpu.VMEM((GRID, ROWS_HERE, FEATS), bf16)]
ARRIVED = [pltpu.SemaphoreType.DMA((GRID,))]


def shape(dims, dtype):
    return jax.ShapeDtypeStruct(dims, dtype)


def from_ahead(block, axis, step):
    return lax.ppermute(block, axis, [(i, (i - step) % GRID) for i in range(GRID)])


def to_ahead(block, axis, step):
    return lax.ppermute(block, axis, [(i, (i + step) % GRID) for i in range(GRID)])


def gather(block, axis):
    return [block] + [from_ahead(block, axis, step) for step in range(1, GRID)]


def per_device(
    vit_cot,
    vit_pre,
    ln_gain,
    patch_w,
    frame_owner,
    conv_w,
    join_w,
    token_order,
    queries,
    keys,
    values,
    attn_out,
    out_w,
):
    key_values = gather(jnp.concatenate([keys[0], values[0]], axis=1), "hx")
    query_outs = gather(jnp.concatenate([queries[0], attn_out[0]], axis=1), "hy")
    windows = call(
        window_kernel,
        shape((FRAMES, 16, LANES), bf16),
        [VMEM] * 2 + [ANY] * 5,
        scratch=[
            pltpu.VMEM(vit_cot.shape[2:], bf16),
            pltpu.VMEM(vit_pre.shape[2:], bf16),
            pltpu.VMEM(patch_w.shape, bf16),
            pltpu.VMEM((LANES, patch_w.shape[0]), bf16),
            pltpu.VMEM((6 * LANES, LANES), bf16),
            pltpu.VMEM((SIDE * SIDE + 16, LANES), f32),
            pltpu.SemaphoreType.DMA((5,)),
        ],
    )(
        ln_gain,
        token_order,
        vit_pre[0, 0],
        vit_cot[0, 0],
        jnp.asarray(basis_matrix(), bf16),
        patch_w,
        jnp.asarray(spread_matrix(), bf16),
    )
    joint, picked = call(
        weights_kernel,
        (shape((QUARTERS * LANES, FEATS), bf16), shape((768, QUARTERS * LANES), bf16)),
        [ANY] * 2,
        scratch=[
            pltpu.VMEM(join_w.shape, bf16),
            pltpu.VMEM(out_w.shape, bf16),
            pltpu.SemaphoreType.DMA((2,)),
        ],
    )(join_w, out_w)
    received = lax.all_to_all(
        windows, ("tm", "hx", "hy"), split_axis=0, concat_axis=0, tiled=True
    )
    joint, picked, key_values[0] = lax.optimization_barrier((joint, picked, key_values[0]))
    totals = call(
        totals_kernel,
        shape((8, BLOCK), f32),
        [ANY] * (2 * GRID),
        scratch=HELD * 2 + ARRIVED * 2,
        limit=24,
    )(*query_outs, *key_values)
    total_pieces = gather(totals, "hy")
    outs = call(
        grads_kernel,
        tuple([shape((ROWS_HERE, FEATS), bf16)] * GRID)
        + tuple([shape((2, ROWS_HERE, FEATS), bf16)] * GRID)
        + (shape((768, FEATS), bf16),),
        [SMEM] + [VMEM] * (1 + GRID) + [ANY] * (3 + 2 * GRID),
        scratch=[
            pltpu.VMEM((FRAMES + 2, 16, LANES), bf16),
            pltpu.VMEM((3 * LANES, QUARTERS * LANES), bf16),
            pltpu.VMEM((BLOCK, QUARTERS * LANES), bf16),
            pltpu.VMEM((FRAMES, 16, LANES), bf16),
            pltpu.VMEM((QUARTERS * LANES, FEATS), bf16),
            pltpu.VMEM((768, QUARTERS * LANES), bf16),
            pltpu.VMEM((768, FEATS), bf16),
            pltpu.VMEM((HEADS_HERE, 8, BLOCK), f32),
            pltpu.VMEM((HEADS_HERE, HDIM, BLOCK), f32),
        ]
        + HELD * 6
        + [pltpu.VMEM((GRID, 2, ROWS_HERE, FEATS), bf16), pltpu.SemaphoreType.DMA((3,))]
        + ARRIVED * 6
        + [pltpu.SemaphoreType.DMA((1,))],
        out_spec=ANY,
        limit=40,
    )(frame_owner, conv_w, *total_pieces, received, joint, picked, *query_outs, *key_values)
    query_parts, pair_parts, weight_part = outs[:GRID], outs[GRID : 2 * GRID], outs[2 * GRID]
    weight_parts = lax.all_to_all(
        weight_part.reshape(8, 2, 48, FEATS),
        ("core", "hx"),
        split_axis=0,
        concat_axis=0,
        tiled=True,
    )
    weight_kept, weight_sent = call(
        half_kernel,
        (shape((48, FEATS), f32), shape((48, FEATS), f32)),
        [VMEM],
        limit=8,
    )(weight_parts)
    weight_other = lax.ppermute(weight_sent, "zh", [(0, 1), (1, 0)])
    pair_back = [pair_parts[0]] + [
        to_ahead(pair_parts[step], "hx", step) for step in range(1, GRID)
    ]
    query_back = [query_parts[0]] + [
        to_ahead(query_parts[step], "hy", step) for step in range(1, GRID)
    ]

    rows = shape((1, ROWS_HERE, FEATS), bf16)
    return call(
        sum_kernel,
        (rows, rows, rows, shape((48, FEATS), f32)),
        [VMEM] * 2 + [ANY] * (2 * GRID),
        scratch=HELD + [pltpu.VMEM((GRID, 2, ROWS_HERE, FEATS), bf16)] + ARRIVED * 2,
        limit=8,
    )(weight_kept, weight_other, *pair_back, *query_back)


def solution(mesh):
    fine = Mesh(
        mesh.devices.reshape(2, 2, GRID, GRID, GRID), ("zh", "core", "tm", "hx", "hy")
    )
    dp, height = ("zh", "core"), ("hx", "hy")
    rows = P(dp, height, "tm")
    slots = P(dp, ("tm",) + height, None, None)
    placed = (
        slots,
        slots,
        P(),
        P(),
        P(),
        P(),
        P(),
        P(height, "tm"),
        rows,
        rows,
        rows,
        rows,
        P("tm", None),
    )
    return jax.shard_map(
        per_device,
        mesh=fine,
        in_specs=placed,
        out_specs=(rows, rows, rows, P(dp + height, "tm")),
        check_vma=False,
    )
```

```python
import functools
import math

import jax
import jax.numpy as jnp
import numpy as np
from jax import lax
from jax.experimental import pallas as pl
from jax.experimental.pallas import tpu as pltpu
from jax.sharding import Mesh
from jax.sharding import PartitionSpec as P

HDIM = 128
IMG = 224
PATCH = 14
SIDE = IMG // PATCH
GRID = 4
HEADS_HERE = 3
ROWS_HERE = 256
FEATS = HEADS_HERE * HDIM
BLOCK = GRID * ROWS_HERE
FRAMES = 64
LANES = 128
QUARTERS = 4
QUARTER_LANES = 32
TAPS = 27
ORDER_LANE = TAPS
QUARTER_CELLS = (PATCH // 2) * (2 * PATCH)

epsilon = 1e-05
pixel_std = (0.26862954, 0.26130258, 0.27577711)

f32 = jnp.float32
bf16 = jnp.bfloat16
MIB = 1024 * 1024
HIGHEST = lax.Precision.HIGHEST
LOG2E = math.log2(math.e)
SCORE_SCALE = HDIM ** (-0.5)


def row_masks():
    masks = np.zeros((8, PATCH), np.float32)
    for half in range(2):
        for shift in range(3):
            low = half * 7 + shift - 1
            masks[half * 3 + shift, max(low, 0) : min(low + 7, PATCH)] = 1
    masks[6, 0] = 1
    masks[7, PATCH - 1] = 1
    return masks


def basis_matrix():
    rows = row_masks()
    columns = np.zeros((3, PATCH), np.float32)
    columns[0] = 1
    columns[1, 0] = 1
    columns[2, PATCH - 1] = 1
    basis = np.zeros((LANES, 3, PATCH, PATCH), np.float32)
    for col in range(3):
        for row in range(8):
            for channel in range(3):
                basis[col * 24 + row * 3 + channel, channel] = np.outer(rows[row], columns[col])
    return basis.reshape(LANES, 3 * PATCH * PATCH)


def spread_matrix():
    spread = np.zeros((6, LANES, LANES), np.float32)
    for half in range(2):
        for side in range(2):
            first = 2 * side + 1
            terms = {
                0: [(first - 1, 2, 1), (first, 0, 1), (first + 1, 0, 1), (first + 1, 2, -1)],
                1: [(first, 0, 1), (first + 1, 0, 1)],
                2: [(first, 0, 1), (first, 1, -1), (first + 1, 0, 1), (first + 2, 1, 1)],
            }
            for shift in range(3):
                groups = [half * 3 + shift]
                if (half, shift) == (0, 0):
                    groups.append(7)
                if (half, shift) == (1, 2):
                    groups.append(6)
                for offset in range(3):
                    for channel in range(3):
                        lane = (half * 2 + side) * QUARTER_LANES + (shift * 3 + offset) * 3 + channel
                        for place, col, sign in terms[offset]:
                            for row in groups:
                                spread[place, col * 24 + row * 3 + channel, lane] += sign
    return spread.reshape(6 * LANES, LANES)


NN = (((1,), (0,)), ((), ()))
NT = (((1,), (1,)), ((), ()))
TN = (((0,), (0,)), ((), ()))


def dot(left, right, dims=NN):
    return lax.dot_general(left, right, dims, preferred_element_type=f32)


def one_hot(condition):
    return jnp.where(condition, 1.0, 0.0).astype(bf16)


def iota(dims, axis):
    return lax.broadcasted_iota(jnp.int32, dims, axis)


def start(copies):
    for copy in copies:
        copy.start()


def fetch(refs, held, arrived):
    copies = [
        pltpu.make_async_copy(ref, kept, arrived.at[place])
        for place, (ref, kept) in enumerate(zip(refs, held))
    ]
    start(copies)
    return copies


def fetch_halves(refs, column, held, arrived):
    return fetch(
        [ref.at[:, pl.ds(column * FEATS, FEATS)] for ref in refs],
        [held.at[place] for place in range(len(refs))],
        arrived,
    )


def window_kernel(gain_ref, order_ref, *refs):
    out_ref, cot_ref, pre_ref, patch_ref, basis_ref, spread_ref, sums, arrived = refs[5:]
    held = (pre_ref, cot_ref, basis_ref, patch_ref, spread_ref)
    copies = fetch(refs[:5], held, arrived)
    copies[0].wait()
    copies[1].wait()
    pre = pre_ref[...].astype(f32)
    centered = pre - jnp.mean(pre, axis=-1, keepdims=True)
    inverse = lax.rsqrt(jnp.mean(centered * centered, axis=-1, keepdims=True) + epsilon)
    normed = centered * inverse
    scaled = cot_ref[...].astype(f32) * gain_ref[...].astype(f32).reshape(1, -1)
    grad_rows = inverse * (
        scaled
        - jnp.mean(scaled, axis=-1, keepdims=True)
        - normed * jnp.mean(scaled * normed, axis=-1, keepdims=True)
    )
    grad_rows = grad_rows.astype(bf16)
    channel = iota((LANES, 1), 0) % 3
    scale = jnp.where(
        channel == 0, 1.0 / pixel_std[0], jnp.where(channel == 1, 1.0 / pixel_std[1], 1.0 / pixel_std[2])
    ) * (1.0 / QUARTER_CELLS)
    copies[2].wait()
    copies[3].wait()
    weights = dot(basis_ref[...], patch_ref[...]) * scale
    high = weights.astype(bf16)
    low = (weights - high.astype(f32)).astype(bf16)
    both = dot(grad_rows, jnp.concatenate([high, low], axis=0), NT)
    patch_sums = both[:, :LANES] + both[:, LANES:]
    group = (iota((SIDE * SIDE, LANES), 1) // 3) % 8
    edge = jnp.zeros((SIDE, LANES), f32)
    above = jnp.concatenate([edge, patch_sums[:-SIDE]], axis=0)
    below = jnp.concatenate([patch_sums[SIDE:], edge], axis=0)
    patch_sums = jnp.where(group == 7, above, jnp.where(group == 6, below, patch_sums))
    sums[pl.ds(0, 8), :] = jnp.zeros((8, LANES), f32)
    sums[pl.ds(8 + SIDE * SIDE, 8), :] = jnp.zeros((8, LANES), f32)
    sums[pl.ds(8, SIDE * SIDE), :] = patch_sums
    copies[4].wait()
    column = iota((SIDE * GRID, LANES), 0) % GRID
    total = jnp.zeros((SIDE * GRID, LANES), f32)
    for place in range(6):
        picked = sums[pl.ds(7 + place, SIDE * GRID, stride=GRID), :]
        if place == 0:
            picked = jnp.where(column == 0, 0.0, picked)
        if place == 5:
            picked = jnp.where(column == GRID - 1, 0.0, picked)
        high = picked.astype(bf16)
        low = (picked - high.astype(f32)).astype(bf16)
        both = dot(
            jnp.concatenate([high, low], axis=0), spread_ref[pl.ds(place * LANES, LANES), :]
        )
        total = total + (both[: SIDE * GRID] + both[SIDE * GRID :])
    windows = total.astype(bf16)
    entries = jnp.where(
        iota((16, 64), 1) % 16 == iota((16, 64), 0), order_ref[...].astype(f32), 0.0
    ).astype(bf16)
    order = dot(entries, one_hot(iota((64, LANES), 1) == ORDER_LANE + iota((64, LANES), 0) // 16))
    order = order.astype(bf16)
    for target_x in range(GRID):
        block = windows[target_x * 16 : (target_x + 1) * 16] + order
        for target_t in range(GRID):
            for target_y in range(GRID):
                out_ref[(target_t * GRID + target_x) * GRID + target_y] = block


def weights_kernel(join_from, out_w_from, joint_ref, picked_ref, join_ref, out_w_ref, arrived):
    here_y = lax.axis_index("hy")
    copies = fetch([join_from, out_w_from], [join_ref, out_w_ref], arrived)
    copies[0].wait()
    copies[1].wait()
    joint_ref[...] = dot(join_ref[...], out_w_ref[...], NT).astype(bf16)
    row, column = iota((96, 384), 0), iota((96, 384), 1)
    half = row // 48
    pick = one_hot(column == half * 192 + here_y * 48 + (row - half * 48))
    for pair in range(8):
        rows = dot(pick, join_ref[:, pl.ds(pair * 384, 384)], NT).astype(bf16)
        z, core, x = pair // 4, (pair % 4) // 2, (pair % 2) * 2
        for step in range(2):
            picked_ref[pl.ds((core * GRID + x + step) * 96 + z * 48, 48), :] = rows[
                step * 48 : (step + 1) * 48
            ]


def totals_kernel(*refs):
    out_ref, query_held, key_held, query_arrived, key_arrived = refs[2 * GRID :]
    key_copies = fetch_halves(refs[GRID : 2 * GRID], 0, key_held, key_arrived)
    query_copies = fetch_halves(refs[:GRID], 0, query_held, query_arrived)
    for copy in key_copies:
        copy.wait()
    for head in range(HEADS_HERE):
        columns = pl.ds(head * HDIM, HDIM)
        for piece in range(GRID):
            if head == 0:
                query_copies[piece].wait()
            query = query_held[piece, :, columns]
            scores = [dot(key_held[other, :, columns], query, NT) for other in range(GRID)]
            top = functools.reduce(
                jnp.maximum, [jnp.max(tile, axis=0, keepdims=True) for tile in scores]
            ) * (SCORE_SCALE * LOG2E)
            total = sum(
                jnp.sum(jnp.exp2(tile * (SCORE_SCALE * LOG2E) - top), axis=0, keepdims=True)
                for tile in scores
            )
            out_ref[pl.ds(head, 1), pl.ds(piece * ROWS_HERE, ROWS_HERE)] = top + jnp.log2(total)
    out_ref[pl.ds(HEADS_HERE, 8 - HEADS_HERE), :] = jnp.zeros((8 - HEADS_HERE, BLOCK), f32)


def token_part(owner_ref, conv_ref, recv_ref, arrivals, frames, conv_big, ordered):
    here_x = lax.axis_index("hx")
    here_y = lax.axis_index("hy")
    frames[0] = jnp.zeros((16, LANES), bf16)
    frames[FRAMES + 1] = jnp.zeros((16, LANES), bf16)
    row, column = iota((3 * QUARTER_LANES, 3 * TAPS), 0), iota((3 * QUARTER_LANES, 3 * TAPS), 1)
    tap = row % QUARTER_LANES
    conv = dot(
        one_hot((tap < TAPS) & (column == (row // QUARTER_LANES) * TAPS + tap)), conv_ref[...]
    ).astype(bf16)
    conv_big[...] = jnp.zeros_like(conv_big)
    for quarter in range(QUARTERS):
        for shift in range(3):
            conv_big[
                pl.ds(shift * LANES + quarter * QUARTER_LANES, QUARTER_LANES),
                pl.ds(quarter * LANES, LANES),
            ] = conv[shift * QUARTER_LANES : (shift + 1) * QUARTER_LANES]
    arrivals.wait()

    def place_frame(frame, carry):
        frames[frame + 1] = recv_ref[(frame // 16) * 16 + owner_ref[frame]]
        return carry

    lax.fori_loop(0, FRAMES, place_frame, 0, unroll=8)
    lane = iota((16, ROWS_HERE), 1)
    for slab_t in range(GRID):
        pooled = sum(
            dot(
                frames[pl.ds(slab_t * 16 + shift, 16)].reshape(ROWS_HERE, LANES),
                conv_big[pl.ds(shift * LANES, LANES), :],
            )
            for shift in range(3)
        ).astype(bf16)
        pieces = []
        for piece in range(GRID):
            slab = lax.rem(here_y + piece, GRID)
            block = recv_ref[slab_t * 16 + here_x * GRID + slab].astype(f32)
            for part in range(4):
                order = block[:, ORDER_LANE + part : ORDER_LANE + part + 1].astype(jnp.int32)
                target = (order // 4) * 16 + slab * 4 + lax.rem(order, 4)
                pieces.append(one_hot(lane == target))
        chosen = dot(jnp.concatenate(pieces, axis=0), pooled).astype(bf16)
        for piece in range(GRID):
            ordered[pl.ds(piece * ROWS_HERE + slab_t * 64, 64), :] = chosen[
                piece * 64 : (piece + 1) * 64
            ]


def grads_kernel(owner_ref, conv_ref, *refs):
    total_refs, (recv_from, joint_from, picked_from) = refs[:GRID], refs[GRID : GRID + 3]
    query_refs, pair_refs = refs[GRID + 3 : 2 * GRID + 3], refs[2 * GRID + 3 : 3 * GRID + 3]
    rest = refs[3 * GRID + 3 :]
    query_out, pair_out, weight_out = rest[:GRID], rest[GRID : 2 * GRID], rest[2 * GRID]
    (
        frames,
        conv_big,
        ordered,
        recv_ref,
        joint_ref,
        picked_ref,
        weight_made,
        dots_ref,
        sums,
        out_held,
        query_held,
        key_held,
        value_held,
        grad_ref,
        query_made,
        pair_made,
        first_arrived,
        out_arrived,
        query_arrived,
        key_arrived,
        value_arrived,
        query_sent,
        pair_sent,
        weight_sent,
    ) = rest[2 * GRID + 1 :]
    sends_order = (2, 1, 3, 0)
    firsts = fetch(
        [recv_from, joint_from, picked_from], [recv_ref, joint_ref, picked_ref], first_arrived
    )
    out_copies = fetch_halves(query_refs, 1, out_held, out_arrived)
    query_copies = fetch_halves(query_refs, 0, query_held, query_arrived)
    key_copies = fetch_halves(pair_refs, 0, key_held, key_arrived)
    value_copies = fetch_halves(pair_refs, 1, value_held, value_arrived)
    token_part(owner_ref, conv_ref, recv_ref, firsts[0], frames, conv_big, ordered)
    firsts[1].wait()
    ones = jnp.ones((8, 2 * HDIM), bf16)
    outer = jnp.zeros((QUARTERS * LANES, FEATS), f32)
    for piece in range(GRID):
        rows = ordered[pl.ds(piece * ROWS_HERE, ROWS_HERE), :]
        grads = dot(rows, joint_ref[...]).astype(bf16)
        grad_ref[piece] = grads
        out_copies[piece].wait()
        outs = out_held[piece]
        products = grads.astype(f32) * outs.astype(f32)
        high = products.astype(bf16)
        low = (products - high.astype(f32)).astype(bf16)
        for head in range(HEADS_HERE):
            columns = slice(head * HDIM, (head + 1) * HDIM)
            both = jnp.concatenate([high[:, columns], low[:, columns]], axis=1)
            dots_ref[head, :, pl.ds(piece * ROWS_HERE, ROWS_HERE)] = dot(ones, both, NT)
        outer = outer + dot(rows, outs, TN)
    firsts[2].wait()
    weight_made[...] = (
        dot(picked_ref[...], outer.astype(bf16)) * (1.0 / math.sqrt(FRAMES * 64 * 4))
    ).astype(bf16)
    sends = fetch([weight_made], [weight_out], weight_sent)
    root = math.sqrt(FRAMES * 64)
    totals = []
    for piece in range(GRID):
        parts = [
            total_refs[step][:, pl.ds(((piece - step) % GRID) * ROWS_HERE, ROWS_HERE)]
            for step in range(GRID)
        ]
        top = functools.reduce(jnp.maximum, parts)
        totals.append(top + jnp.log2(sum(jnp.exp2(part - top) for part in parts)))
    totals = jnp.concatenate(totals, axis=1)
    for copy in query_copies:
        copy.wait()
    for other in sends_order:
        key_copies[other].wait()
        value_copies[other].wait()
        for head in range(HEADS_HERE):
            columns = pl.ds(head * HDIM, HDIM)
            query = query_held[:, :, columns].reshape(BLOCK, HDIM)
            grad = grad_ref[:, :, columns].reshape(BLOCK, HDIM)
            key = key_held[other, :, columns]
            value = value_held[other, :, columns]
            weights = jnp.exp2(
                dot(key, query, NT) * (SCORE_SCALE * LOG2E) - totals[head : head + 1]
            )
            dscore = (weights * (dot(value, grad, NT) - dots_ref[head, 0:1, :])).astype(bf16)
            pair_made[other, 1, :, columns] = (dot(weights.astype(bf16), grad) * root).astype(bf16)
            pair_made[other, 0, :, columns] = (
                dot(dscore, query) * (root * SCORE_SCALE)
            ).astype(bf16)
            part = dot(key.T, dscore)
            if other == sends_order[0]:
                sums[head] = part
            else:
                sums[head] += part
        send = pltpu.make_async_copy(pair_made.at[other], pair_out[other], pair_sent.at[other])
        send.start()
        sends.append(send)
    for piece in sends_order:
        for head in range(HEADS_HERE):
            query_made[piece, :, pl.ds(head * HDIM, HDIM)] = (
                sums[head, :, pl.ds(piece * ROWS_HERE, ROWS_HERE)].T * (root * SCORE_SCALE)
            ).astype(bf16)
        send = pltpu.make_async_copy(query_made.at[piece], query_out[piece], query_sent.at[piece])
        send.start()
        sends.append(send)
    for send in sends:
        send.wait()


def half_kernel(parts_ref, kept_ref, sent_ref):
    here_z = lax.axis_index("zh")
    for out_ref, half in ((kept_ref, here_z), (sent_ref, 1 - here_z)):
        out_ref[...] = sum(parts_ref[source, half].astype(f32) for source in range(2 * GRID))


def sum_kernel(kept_ref, other_ref, *refs):
    pair_refs, query_refs = refs[:GRID], refs[GRID : 2 * GRID]
    query_out, key_out, value_out, weight_out, query_held, pair_held, *arrived = refs[2 * GRID :]
    pair_copies = fetch(pair_refs, [pair_held.at[step] for step in range(GRID)], arrived[1])
    query_copies = fetch(query_refs, [query_held.at[step] for step in range(GRID)], arrived[0])
    weight_out[...] = kept_ref[...] + other_ref[...]
    for copy in query_copies:
        copy.wait()
    query_out[0] = sum(query_held[step].astype(f32) for step in range(GRID)).astype(bf16)
    for copy in pair_copies:
        copy.wait()
    for place, out_ref in enumerate((key_out, value_out)):
        out_ref[0] = sum(pair_held[step, place].astype(f32) for step in range(GRID)).astype(bf16)


def call(kernel, out_shape, in_specs, scratch=(), out_spec=None, limit=56):
    return pl.pallas_call(
        kernel,
        out_shape=out_shape,
        in_specs=in_specs,
        out_specs=jax.tree.map(lambda _: out_spec or VMEM, out_shape),
        scratch_shapes=list(scratch),
        compiler_params=pltpu.CompilerParams(vmem_limit_bytes=limit * MIB),
        cost_estimate=pl.CostEstimate(flops=10**6, bytes_accessed=10**5, transcendentals=0),
    )


VMEM = pl.BlockSpec(memory_space=pltpu.VMEM)
SMEM = pl.BlockSpec(memory_space=pltpu.SMEM)
ANY = pl.BlockSpec(memory_space=pl.ANY)
HELD = [pltpu.VMEM((GRID, ROWS_HERE, FEATS), bf16)]
ARRIVED = [pltpu.SemaphoreType.DMA((GRID,))]


def shape(dims, dtype):
    return jax.ShapeDtypeStruct(dims, dtype)


def from_ahead(block, axis, step):
    return lax.ppermute(block, axis, [(i, (i - step) % GRID) for i in range(GRID)])


def to_ahead(block, axis, step):
    return lax.ppermute(block, axis, [(i, (i + step) % GRID) for i in range(GRID)])


def gather(block, axis):
    return [block] + [from_ahead(block, axis, step) for step in range(1, GRID)]


def per_device(
    vit_cot,
    vit_pre,
    ln_gain,
    patch_w,
    frame_owner,
    conv_w,
    join_w,
    token_order,
    queries,
    keys,
    values,
    attn_out,
    out_w,
):
    key_value = jnp.concatenate([keys[0], values[0]], axis=1)
    query_out = jnp.concatenate([queries[0], attn_out[0]], axis=1)
    sides = [from_ahead(key_value, "hx", step) for step in (1, 3)]
    sides += [from_ahead(query_out, "hy", step) for step in (1, 3)]
    windows = call(
        window_kernel,
        shape((FRAMES, 16, LANES), bf16),
        [VMEM] * 2 + [ANY] * 5,
        scratch=[
            pltpu.VMEM(vit_cot.shape[2:], bf16),
            pltpu.VMEM(vit_pre.shape[2:], bf16),
            pltpu.VMEM(patch_w.shape, bf16),
            pltpu.VMEM((LANES, patch_w.shape[0]), bf16),
            pltpu.VMEM((6 * LANES, LANES), bf16),
            pltpu.VMEM((SIDE * SIDE + 16, LANES), f32),
            pltpu.SemaphoreType.DMA((5,)),
        ],
    )(
        ln_gain,
        token_order,
        vit_pre[0, 0],
        vit_cot[0, 0],
        jnp.asarray(basis_matrix(), bf16),
        patch_w,
        jnp.asarray(spread_matrix(), bf16),
    )
    windows, join_w, key_value, query_out, sides = lax.optimization_barrier(
        (windows, join_w, key_value, query_out, sides)
    )
    key_values = [key_value, sides[0], from_ahead(key_value, "hx", 2), sides[1]]
    query_outs = [query_out, sides[2], from_ahead(query_out, "hy", 2), sides[3]]
    joint, picked = call(
        weights_kernel,
        (shape((QUARTERS * LANES, FEATS), bf16), shape((768, QUARTERS * LANES), bf16)),
        [ANY] * 2,
        scratch=[
            pltpu.VMEM(join_w.shape, bf16),
            pltpu.VMEM(out_w.shape, bf16),
            pltpu.SemaphoreType.DMA((2,)),
        ],
    )(join_w, out_w)
    windows, joint, picked, key_values, query_outs = lax.optimization_barrier(
        (windows, joint, picked, key_values, query_outs)
    )
    received = lax.all_to_all(
        windows, ("tm", "hx", "hy"), split_axis=0, concat_axis=0, tiled=True
    )
    totals = call(
        totals_kernel,
        shape((8, BLOCK), f32),
        [ANY] * (2 * GRID),
        scratch=HELD * 2 + ARRIVED * 2,
        limit=24,
    )(*query_outs, *key_values)
    total_pieces = gather(totals, "hy")
    outs = call(
        grads_kernel,
        tuple([shape((ROWS_HERE, FEATS), bf16)] * GRID)
        + tuple([shape((2, ROWS_HERE, FEATS), bf16)] * GRID)
        + (shape((768, FEATS), bf16),),
        [SMEM] + [VMEM] * (1 + GRID) + [ANY] * (3 + 2 * GRID),
        scratch=[
            pltpu.VMEM((FRAMES + 2, 16, LANES), bf16),
            pltpu.VMEM((3 * LANES, QUARTERS * LANES), bf16),
            pltpu.VMEM((BLOCK, QUARTERS * LANES), bf16),
            pltpu.VMEM((FRAMES, 16, LANES), bf16),
            pltpu.VMEM((QUARTERS * LANES, FEATS), bf16),
            pltpu.VMEM((768, QUARTERS * LANES), bf16),
            pltpu.VMEM((768, FEATS), bf16),
            pltpu.VMEM((HEADS_HERE, 8, BLOCK), f32),
            pltpu.VMEM((HEADS_HERE, HDIM, BLOCK), f32),
        ]
        + HELD * 6
        + [pltpu.VMEM((GRID, 2, ROWS_HERE, FEATS), bf16), pltpu.SemaphoreType.DMA((3,))]
        + ARRIVED * 6
        + [pltpu.SemaphoreType.DMA((1,))],
        out_spec=ANY,
        limit=56,
    )(frame_owner, conv_w, *total_pieces, received, joint, picked, *query_outs, *key_values)
    query_parts, pair_parts, weight_part = outs[:GRID], outs[GRID : 2 * GRID], outs[2 * GRID]
    weight_parts = lax.all_to_all(
        weight_part.reshape(8, 2, 48, FEATS),
        ("core", "hx"),
        split_axis=0,
        concat_axis=0,
        tiled=True,
    )
    weight_kept, weight_sent = call(
        half_kernel,
        (shape((48, FEATS), f32), shape((48, FEATS), f32)),
        [VMEM],
        limit=8,
    )(weight_parts)
    weight_other = lax.ppermute(weight_sent, "zh", [(0, 1), (1, 0)])
    pair_back = [pair_parts[0]] + [
        to_ahead(pair_parts[step], "hx", step) for step in range(1, GRID)
    ]
    query_back = [query_parts[0]] + [
        to_ahead(query_parts[step], "hy", step) for step in range(1, GRID)
    ]

    rows = shape((1, ROWS_HERE, FEATS), bf16)
    return call(
        sum_kernel,
        (rows, rows, rows, shape((48, FEATS), f32)),
        [VMEM] * 2 + [ANY] * (2 * GRID),
        scratch=HELD + [pltpu.VMEM((GRID, 2, ROWS_HERE, FEATS), bf16)] + ARRIVED * 2,
        limit=8,
    )(weight_kept, weight_other, *pair_back, *query_back)


def solution(mesh):
    fine = Mesh(
        mesh.devices.reshape(2, 2, GRID, GRID, GRID), ("zh", "core", "tm", "hx", "hy")
    )
    dp, height = ("zh", "core"), ("hx", "hy")
    rows = P(dp, height, "tm")
    slots = P(dp, ("tm",) + height, None, None)
    placed = (
        slots,
        slots,
        P(),
        P(),
        P(),
        P(),
        P(),
        P(height, "tm"),
        rows,
        rows,
        rows,
        rows,
        P("tm", None),
    )
    return jax.shard_map(
        per_device,
        mesh=fine,
        in_specs=placed,
        out_specs=(rows, rows, rows, P(dp + height, "tm")),
        check_vma=False,
    )
```

```python
import functools
import math

import jax
import jax.numpy as jnp
import numpy as np
from jax import lax
from jax.experimental import pallas as pl
from jax.experimental.pallas import tpu as pltpu
from jax.sharding import Mesh
from jax.sharding import PartitionSpec as P

HDIM = 128
IMG = 224
PATCH = 14
SIDE = IMG // PATCH
GRID = 4
HEADS_HERE = 3
ROWS_HERE = 256
FEATS = HEADS_HERE * HDIM
BLOCK = GRID * ROWS_HERE
FRAMES = 64
LANES = 128
QUARTERS = 4
QUARTER_LANES = 32
TAPS = 27
ORDER_LANE = TAPS
QUARTER_CELLS = (PATCH // 2) * (2 * PATCH)

epsilon = 1e-05
pixel_std = (0.26862954, 0.26130258, 0.27577711)

f32 = jnp.float32
bf16 = jnp.bfloat16
MIB = 1024 * 1024
HIGHEST = lax.Precision.HIGHEST
LOG2E = math.log2(math.e)
SCORE_SCALE = HDIM ** (-0.5)


def row_masks():
    masks = np.zeros((8, PATCH), np.float32)
    for half in range(2):
        for shift in range(3):
            low = half * 7 + shift - 1
            masks[half * 3 + shift, max(low, 0) : min(low + 7, PATCH)] = 1
    masks[6, 0] = 1
    masks[7, PATCH - 1] = 1
    return masks


def basis_matrix():
    rows = row_masks()
    columns = np.zeros((3, PATCH), np.float32)
    columns[0] = 1
    columns[1, 0] = 1
    columns[2, PATCH - 1] = 1
    basis = np.zeros((LANES, 3, PATCH, PATCH), np.float32)
    for col in range(3):
        for row in range(8):
            for channel in range(3):
                basis[col * 24 + row * 3 + channel, channel] = np.outer(rows[row], columns[col])
    return basis.reshape(LANES, 3 * PATCH * PATCH)


def spread_matrix():
    spread = np.zeros((6, LANES, LANES), np.float32)
    for half in range(2):
        for side in range(2):
            first = 2 * side + 1
            terms = {
                0: [(first - 1, 2, 1), (first, 0, 1), (first + 1, 0, 1), (first + 1, 2, -1)],
                1: [(first, 0, 1), (first + 1, 0, 1)],
                2: [(first, 0, 1), (first, 1, -1), (first + 1, 0, 1), (first + 2, 1, 1)],
            }
            for shift in range(3):
                groups = [half * 3 + shift]
                if (half, shift) == (0, 0):
                    groups.append(7)
                if (half, shift) == (1, 2):
                    groups.append(6)
                for offset in range(3):
                    for channel in range(3):
                        lane = (half * 2 + side) * QUARTER_LANES + (shift * 3 + offset) * 3 + channel
                        for place, col, sign in terms[offset]:
                            for row in groups:
                                spread[place, col * 24 + row * 3 + channel, lane] += sign
    return spread.reshape(6 * LANES, LANES)


NN = (((1,), (0,)), ((), ()))
NT = (((1,), (1,)), ((), ()))
TN = (((0,), (0,)), ((), ()))


def dot(left, right, dims=NN):
    return lax.dot_general(left, right, dims, preferred_element_type=f32)


def one_hot(condition):
    return jnp.where(condition, 1.0, 0.0).astype(bf16)


def iota(dims, axis):
    return lax.broadcasted_iota(jnp.int32, dims, axis)


def start(copies):
    for copy in copies:
        copy.start()


def fetch(refs, held, arrived):
    copies = [
        pltpu.make_async_copy(ref, kept, arrived.at[place])
        for place, (ref, kept) in enumerate(zip(refs, held))
    ]
    start(copies)
    return copies


def fetch_halves(refs, column, held, arrived):
    return fetch(
        [ref.at[:, pl.ds(column * FEATS, FEATS)] for ref in refs],
        [held.at[place] for place in range(len(refs))],
        arrived,
    )


def window_kernel(gain_ref, order_ref, *refs):
    out_ref, cot_ref, pre_ref, patch_ref, basis_ref, spread_ref, sums, arrived = refs[5:]
    held = (pre_ref, cot_ref, basis_ref, patch_ref, spread_ref)
    copies = fetch(refs[:5], held, arrived)
    copies[0].wait()
    copies[1].wait()
    pre = pre_ref[...].astype(f32)
    centered = pre - jnp.mean(pre, axis=-1, keepdims=True)
    inverse = lax.rsqrt(jnp.mean(centered * centered, axis=-1, keepdims=True) + epsilon)
    normed = centered * inverse
    scaled = cot_ref[...].astype(f32) * gain_ref[...].astype(f32).reshape(1, -1)
    grad_rows = inverse * (
        scaled
        - jnp.mean(scaled, axis=-1, keepdims=True)
        - normed * jnp.mean(scaled * normed, axis=-1, keepdims=True)
    )
    grad_rows = grad_rows.astype(bf16)
    channel = iota((LANES, 1), 0) % 3
    scale = jnp.where(
        channel == 0, 1.0 / pixel_std[0], jnp.where(channel == 1, 1.0 / pixel_std[1], 1.0 / pixel_std[2])
    ) * (1.0 / QUARTER_CELLS)
    copies[2].wait()
    copies[3].wait()
    weights = dot(basis_ref[...], patch_ref[...]) * scale
    high = weights.astype(bf16)
    low = (weights - high.astype(f32)).astype(bf16)
    both = dot(grad_rows, jnp.concatenate([high, low], axis=0), NT)
    patch_sums = both[:, :LANES] + both[:, LANES:]
    group = (iota((SIDE * SIDE, LANES), 1) // 3) % 8
    edge = jnp.zeros((SIDE, LANES), f32)
    above = jnp.concatenate([edge, patch_sums[:-SIDE]], axis=0)
    below = jnp.concatenate([patch_sums[SIDE:], edge], axis=0)
    patch_sums = jnp.where(group == 7, above, jnp.where(group == 6, below, patch_sums))
    sums[pl.ds(0, 8), :] = jnp.zeros((8, LANES), f32)
    sums[pl.ds(8 + SIDE * SIDE, 8), :] = jnp.zeros((8, LANES), f32)
    sums[pl.ds(8, SIDE * SIDE), :] = patch_sums
    copies[4].wait()
    column = iota((SIDE * GRID, LANES), 0) % GRID
    total = jnp.zeros((SIDE * GRID, LANES), f32)
    for place in range(6):
        picked = sums[pl.ds(7 + place, SIDE * GRID, stride=GRID), :]
        if place == 0:
            picked = jnp.where(column == 0, 0.0, picked)
        if place == 5:
            picked = jnp.where(column == GRID - 1, 0.0, picked)
        high = picked.astype(bf16)
        low = (picked - high.astype(f32)).astype(bf16)
        both = dot(
            jnp.concatenate([high, low], axis=0), spread_ref[pl.ds(place * LANES, LANES), :]
        )
        total = total + (both[: SIDE * GRID] + both[SIDE * GRID :])
    windows = total.astype(bf16)
    entries = jnp.where(
        iota((16, 64), 1) % 16 == iota((16, 64), 0), order_ref[...].astype(f32), 0.0
    ).astype(bf16)
    order = dot(entries, one_hot(iota((64, LANES), 1) == ORDER_LANE + iota((64, LANES), 0) // 16))
    order = order.astype(bf16)
    for target_x in range(GRID):
        block = windows[target_x * 16 : (target_x + 1) * 16] + order
        for target_t in range(GRID):
            for target_y in range(GRID):
                out_ref[(target_t * GRID + target_x) * GRID + target_y] = block


def weights_kernel(join_from, out_w_from, joint_ref, picked_ref, join_ref, out_w_ref, arrived):
    here_y = lax.axis_index("hy")
    copies = fetch([join_from, out_w_from], [join_ref, out_w_ref], arrived)
    copies[0].wait()
    copies[1].wait()
    joint_ref[...] = dot(join_ref[...], out_w_ref[...], NT).astype(bf16)
    row, column = iota((96, 384), 0), iota((96, 384), 1)
    half = row // 48
    pick = one_hot(column == half * 192 + here_y * 48 + (row - half * 48))
    for pair in range(8):
        rows = dot(pick, join_ref[:, pl.ds(pair * 384, 384)], NT).astype(bf16)
        z, core, x = pair // 4, (pair % 4) // 2, (pair % 2) * 2
        for step in range(2):
            picked_ref[pl.ds((core * GRID + x + step) * 96 + z * 48, 48), :] = rows[
                step * 48 : (step + 1) * 48
            ]


def totals_kernel(*refs):
    out_ref, query_held, key_held, query_arrived, key_arrived = refs[2 * GRID :]
    key_copies = fetch_halves(refs[GRID : 2 * GRID], 0, key_held, key_arrived)
    query_copies = fetch_halves(refs[:GRID], 0, query_held, query_arrived)
    for copy in key_copies:
        copy.wait()
    for head in range(HEADS_HERE):
        columns = pl.ds(head * HDIM, HDIM)
        for piece in range(GRID):
            if head == 0:
                query_copies[piece].wait()
            query = query_held[piece, :, columns]
            scores = [dot(key_held[other, :, columns], query, NT) for other in range(GRID)]
            top = functools.reduce(
                jnp.maximum, [jnp.max(tile, axis=0, keepdims=True) for tile in scores]
            ) * (SCORE_SCALE * LOG2E)
            total = sum(
                jnp.sum(jnp.exp2(tile * (SCORE_SCALE * LOG2E) - top), axis=0, keepdims=True)
                for tile in scores
            )
            out_ref[pl.ds(head, 1), pl.ds(piece * ROWS_HERE, ROWS_HERE)] = top + jnp.log2(total)
    out_ref[pl.ds(HEADS_HERE, 8 - HEADS_HERE), :] = jnp.zeros((8 - HEADS_HERE, BLOCK), f32)


def token_part(owner_ref, conv_ref, recv_ref, arrivals, frames, conv_big, ordered):
    here_x = lax.axis_index("hx")
    here_y = lax.axis_index("hy")
    frames[0] = jnp.zeros((16, LANES), bf16)
    frames[FRAMES + 1] = jnp.zeros((16, LANES), bf16)
    row, column = iota((3 * QUARTER_LANES, 3 * TAPS), 0), iota((3 * QUARTER_LANES, 3 * TAPS), 1)
    tap = row % QUARTER_LANES
    conv = dot(
        one_hot((tap < TAPS) & (column == (row // QUARTER_LANES) * TAPS + tap)), conv_ref[...]
    ).astype(bf16)
    conv_big[...] = jnp.zeros_like(conv_big)
    for quarter in range(QUARTERS):
        for shift in range(3):
            conv_big[
                pl.ds(shift * LANES + quarter * QUARTER_LANES, QUARTER_LANES),
                pl.ds(quarter * LANES, LANES),
            ] = conv[shift * QUARTER_LANES : (shift + 1) * QUARTER_LANES]
    arrivals.wait()

    def place_frame(frame, carry):
        frames[frame + 1] = recv_ref[(frame // 16) * 16 + owner_ref[frame]]
        return carry

    lax.fori_loop(0, FRAMES, place_frame, 0, unroll=8)
    lane = iota((16, ROWS_HERE), 1)
    for slab_t in range(GRID):
        pooled = sum(
            dot(
                frames[pl.ds(slab_t * 16 + shift, 16)].reshape(ROWS_HERE, LANES),
                conv_big[pl.ds(shift * LANES, LANES), :],
            )
            for shift in range(3)
        ).astype(bf16)
        pieces = []
        for piece in range(GRID):
            slab = lax.rem(here_y + piece, GRID)
            block = recv_ref[slab_t * 16 + here_x * GRID + slab].astype(f32)
            for part in range(4):
                order = block[:, ORDER_LANE + part : ORDER_LANE + part + 1].astype(jnp.int32)
                target = (order // 4) * 16 + slab * 4 + lax.rem(order, 4)
                pieces.append(one_hot(lane == target))
        chosen = dot(jnp.concatenate(pieces, axis=0), pooled).astype(bf16)
        for piece in range(GRID):
            ordered[pl.ds(piece * ROWS_HERE + slab_t * 64, 64), :] = chosen[
                piece * 64 : (piece + 1) * 64
            ]


def token_kernel(owner_ref, conv_ref, *refs):
    recv_from, joint_from, picked_from = refs[:3]
    (
        dots_ref,
        grad_out,
        weight_out,
        frames,
        conv_big,
        ordered,
        recv_ref,
        joint_ref,
        picked_ref,
        weight_made,
        out_held,
        grad_made,
        first_arrived,
        out_arrived,
        grad_sent,
        weight_sent,
    ) = refs[GRID + 3 :]
    firsts = fetch(
        [recv_from, joint_from, picked_from], [recv_ref, joint_ref, picked_ref], first_arrived
    )
    out_copies = fetch_halves(refs[3 : GRID + 3], 1, out_held, out_arrived)
    token_part(owner_ref, conv_ref, recv_ref, firsts[0], frames, conv_big, ordered)
    firsts[1].wait()
    ones = jnp.ones((8, 2 * HDIM), bf16)
    sends = []
    dots_ref[...] = jnp.zeros_like(dots_ref)
    outer = jnp.zeros((QUARTERS * LANES, FEATS), f32)
    for piece in range(GRID):
        rows = ordered[pl.ds(piece * ROWS_HERE, ROWS_HERE), :]
        grads = dot(rows, joint_ref[...]).astype(bf16)
        grad_made[piece] = grads
        sends += fetch([grad_made.at[piece]], [grad_out.at[piece]], grad_sent.at[pl.ds(piece, 1)])
        out_copies[piece].wait()
        outs = out_held[piece]
        products = grads.astype(f32) * outs.astype(f32)
        high = products.astype(bf16)
        low = (products - high.astype(f32)).astype(bf16)
        for head in range(HEADS_HERE):
            columns = slice(head * HDIM, (head + 1) * HDIM)
            both = jnp.concatenate([high[:, columns], low[:, columns]], axis=1)
            dots_ref[pl.ds(head, 1), pl.ds(piece * ROWS_HERE, ROWS_HERE)] = dot(ones, both, NT)[
                0:1
            ]
        outer = outer + dot(rows, outs, TN)
    firsts[2].wait()
    weight_made[...] = (
        dot(picked_ref[...], outer.astype(bf16)) * (1.0 / math.sqrt(FRAMES * 64 * 4))
    ).astype(bf16)
    sends += fetch([weight_made], [weight_out], weight_sent)
    for send in sends:
        send.wait()


def grads_kernel(dots_ref, *refs):
    total_refs, grad_from = refs[:GRID], refs[GRID]
    query_refs, pair_refs = refs[GRID + 1 : 2 * GRID + 1], refs[2 * GRID + 1 : 3 * GRID + 1]
    rest = refs[3 * GRID + 1 :]
    query_out, pair_out = rest[:GRID], rest[GRID : 2 * GRID]
    (
        sums,
        query_held,
        key_held,
        value_held,
        grad_ref,
        query_made,
        pair_made,
        query_arrived,
        key_arrived,
        value_arrived,
        grad_arrived,
        query_sent,
        pair_sent,
    ) = rest[2 * GRID :]
    sends_order = (2, 1, 3, 0)
    query_copies = fetch_halves(query_refs, 0, query_held, query_arrived)
    query_copies += fetch([grad_from], [grad_ref], grad_arrived)
    key_copies = fetch_halves(pair_refs, 0, key_held, key_arrived)
    value_copies = fetch_halves(pair_refs, 1, value_held, value_arrived)
    root = math.sqrt(FRAMES * 64)
    totals = []
    for piece in range(GRID):
        parts = [
            total_refs[step][:, pl.ds(((piece - step) % GRID) * ROWS_HERE, ROWS_HERE)]
            for step in range(GRID)
        ]
        top = functools.reduce(jnp.maximum, parts)
        totals.append(top + jnp.log2(sum(jnp.exp2(part - top) for part in parts)))
    totals = jnp.concatenate(totals, axis=1)
    for copy in query_copies:
        copy.wait()
    sends = []
    for other in sends_order:
        key_copies[other].wait()
        value_copies[other].wait()
        for head in range(HEADS_HERE):
            columns = pl.ds(head * HDIM, HDIM)
            query = query_held[:, :, columns].reshape(BLOCK, HDIM)
            grad = grad_ref[:, :, columns].reshape(BLOCK, HDIM)
            key = key_held[other, :, columns]
            value = value_held[other, :, columns]
            weights = jnp.exp2(
                dot(key, query, NT) * (SCORE_SCALE * LOG2E) - totals[head : head + 1]
            )
            dscore = (weights * (dot(value, grad, NT) - dots_ref[pl.ds(head, 1), :])).astype(bf16)
            pair_made[other, 1, :, columns] = (dot(weights.astype(bf16), grad) * root).astype(bf16)
            pair_made[other, 0, :, columns] = (
                dot(dscore, query) * (root * SCORE_SCALE)
            ).astype(bf16)
            part = dot(key.T, dscore)
            if other == sends_order[0]:
                sums[head] = part
            else:
                sums[head] += part
        send = pltpu.make_async_copy(pair_made.at[other], pair_out[other], pair_sent.at[other])
        send.start()
        sends.append(send)
    for piece in sends_order:
        for head in range(HEADS_HERE):
            query_made[piece, :, pl.ds(head * HDIM, HDIM)] = (
                sums[head, :, pl.ds(piece * ROWS_HERE, ROWS_HERE)].T * (root * SCORE_SCALE)
            ).astype(bf16)
        send = pltpu.make_async_copy(query_made.at[piece], query_out[piece], query_sent.at[piece])
        send.start()
        sends.append(send)
    for send in sends:
        send.wait()


def half_kernel(parts_ref, kept_ref, sent_ref):
    here_z = lax.axis_index("zh")
    for out_ref, half in ((kept_ref, here_z), (sent_ref, 1 - here_z)):
        out_ref[...] = sum(parts_ref[source, half].astype(f32) for source in range(2 * GRID))


def sum_kernel(kept_ref, other_ref, *refs):
    pair_refs, query_refs = refs[:GRID], refs[GRID : 2 * GRID]
    query_out, key_out, value_out, weight_out, query_held, pair_held, *arrived = refs[2 * GRID :]
    pair_copies = fetch(pair_refs, [pair_held.at[step] for step in range(GRID)], arrived[1])
    query_copies = fetch(query_refs, [query_held.at[step] for step in range(GRID)], arrived[0])
    weight_out[...] = kept_ref[...] + other_ref[...]
    for copy in query_copies:
        copy.wait()
    query_out[0] = sum(query_held[step].astype(f32) for step in range(GRID)).astype(bf16)
    for copy in pair_copies:
        copy.wait()
    for place, out_ref in enumerate((key_out, value_out)):
        out_ref[0] = sum(pair_held[step, place].astype(f32) for step in range(GRID)).astype(bf16)


def call(kernel, out_shape, in_specs, scratch=(), out_spec=None, limit=56):
    return pl.pallas_call(
        kernel,
        out_shape=out_shape,
        in_specs=in_specs,
        out_specs=out_spec or jax.tree.map(lambda _: VMEM, out_shape),
        scratch_shapes=list(scratch),
        compiler_params=pltpu.CompilerParams(vmem_limit_bytes=limit * MIB),
        cost_estimate=pl.CostEstimate(flops=10**6, bytes_accessed=10**5, transcendentals=0),
    )


VMEM = pl.BlockSpec(memory_space=pltpu.VMEM)
SMEM = pl.BlockSpec(memory_space=pltpu.SMEM)
ANY = pl.BlockSpec(memory_space=pl.ANY)
HELD = [pltpu.VMEM((GRID, ROWS_HERE, FEATS), bf16)]
ARRIVED = [pltpu.SemaphoreType.DMA((GRID,))]


def shape(dims, dtype):
    return jax.ShapeDtypeStruct(dims, dtype)


def from_ahead(block, axis, step):
    return lax.ppermute(block, axis, [(i, (i - step) % GRID) for i in range(GRID)])


def to_ahead(block, axis, step):
    return lax.ppermute(block, axis, [(i, (i + step) % GRID) for i in range(GRID)])


def gather(block, axis):
    return [block] + [from_ahead(block, axis, step) for step in range(1, GRID)]


def per_device(
    vit_cot,
    vit_pre,
    ln_gain,
    patch_w,
    frame_owner,
    conv_w,
    join_w,
    token_order,
    queries,
    keys,
    values,
    attn_out,
    out_w,
):
    key_value = jnp.concatenate([keys[0], values[0]], axis=1)
    query_out = jnp.concatenate([queries[0], attn_out[0]], axis=1)
    sides = [from_ahead(key_value, "hx", step) for step in (1, 3)]
    sides += [from_ahead(query_out, "hy", step) for step in (1, 3)]
    windows = call(
        window_kernel,
        shape((FRAMES, 16, LANES), bf16),
        [VMEM] * 2 + [ANY] * 5,
        scratch=[
            pltpu.VMEM(vit_cot.shape[2:], bf16),
            pltpu.VMEM(vit_pre.shape[2:], bf16),
            pltpu.VMEM(patch_w.shape, bf16),
            pltpu.VMEM((LANES, patch_w.shape[0]), bf16),
            pltpu.VMEM((6 * LANES, LANES), bf16),
            pltpu.VMEM((SIDE * SIDE + 16, LANES), f32),
            pltpu.SemaphoreType.DMA((5,)),
        ],
    )(
        ln_gain,
        token_order,
        vit_pre[0, 0],
        vit_cot[0, 0],
        jnp.asarray(basis_matrix(), bf16),
        patch_w,
        jnp.asarray(spread_matrix(), bf16),
    )
    windows, join_w, key_value, query_out, sides = lax.optimization_barrier(
        (windows, join_w, key_value, query_out, sides)
    )
    key_values = [key_value, sides[0], from_ahead(key_value, "hx", 2), sides[1]]
    query_outs = [query_out, sides[2], from_ahead(query_out, "hy", 2), sides[3]]
    joint, picked = call(
        weights_kernel,
        (shape((QUARTERS * LANES, FEATS), bf16), shape((768, QUARTERS * LANES), bf16)),
        [ANY] * 2,
        scratch=[
            pltpu.VMEM(join_w.shape, bf16),
            pltpu.VMEM(out_w.shape, bf16),
            pltpu.SemaphoreType.DMA((2,)),
        ],
    )(join_w, out_w)
    windows, joint, picked, key_values, query_outs = lax.optimization_barrier(
        (windows, joint, picked, key_values, query_outs)
    )
    received = lax.all_to_all(
        windows, ("tm", "hx", "hy"), split_axis=0, concat_axis=0, tiled=True
    )
    totals = call(
        totals_kernel,
        shape((8, BLOCK), f32),
        [ANY] * (2 * GRID),
        scratch=HELD * 2 + ARRIVED * 2,
        limit=24,
    )(*query_outs, *key_values)
    totals, received = lax.optimization_barrier((totals, received))
    total_pieces = gather(totals, "hy")
    row_dots, grad_out, weight_part = call(
        token_kernel,
        (
            shape((8, BLOCK), f32),
            shape((GRID, ROWS_HERE, FEATS), bf16),
            shape((768, FEATS), bf16),
        ),
        [SMEM, VMEM] + [ANY] * (3 + GRID),
        scratch=[
            pltpu.VMEM((FRAMES + 2, 16, LANES), bf16),
            pltpu.VMEM((3 * LANES, QUARTERS * LANES), bf16),
            pltpu.VMEM((BLOCK, QUARTERS * LANES), bf16),
            pltpu.VMEM((FRAMES, 16, LANES), bf16),
            pltpu.VMEM((QUARTERS * LANES, FEATS), bf16),
            pltpu.VMEM((768, QUARTERS * LANES), bf16),
            pltpu.VMEM((768, FEATS), bf16),
        ]
        + HELD * 2
        + [pltpu.SemaphoreType.DMA((3,))]
        + ARRIVED * 2
        + [pltpu.SemaphoreType.DMA((1,))],
        out_spec=(VMEM, ANY, ANY),
    )(frame_owner, conv_w, received, joint, picked, *query_outs)
    outs = call(
        grads_kernel,
        tuple([shape((ROWS_HERE, FEATS), bf16)] * GRID)
        + tuple([shape((2, ROWS_HERE, FEATS), bf16)] * GRID),
        [VMEM] * (1 + GRID) + [ANY] * (1 + 2 * GRID),
        scratch=[pltpu.VMEM((HEADS_HERE, HDIM, BLOCK), f32)]
        + HELD * 5
        + [pltpu.VMEM((GRID, 2, ROWS_HERE, FEATS), bf16)]
        + ARRIVED * 3
        + [pltpu.SemaphoreType.DMA((1,))]
        + ARRIVED * 2,
        out_spec=tuple([ANY] * (2 * GRID)),
    )(row_dots, *total_pieces, grad_out, *query_outs, *key_values)
    query_parts, pair_parts = outs[:GRID], outs[GRID:]
    weight_parts = lax.all_to_all(
        weight_part.reshape(8, 2, 48, FEATS),
        ("core", "hx"),
        split_axis=0,
        concat_axis=0,
        tiled=True,
    )
    weight_kept, weight_sent = call(
        half_kernel,
        (shape((48, FEATS), f32), shape((48, FEATS), f32)),
        [VMEM],
        limit=8,
    )(weight_parts)
    weight_other = lax.ppermute(weight_sent, "zh", [(0, 1), (1, 0)])
    pair_back = [pair_parts[0]] + [
        to_ahead(pair_parts[step], "hx", step) for step in range(1, GRID)
    ]
    query_back = [query_parts[0]] + [
        to_ahead(query_parts[step], "hy", step) for step in range(1, GRID)
    ]

    rows = shape((1, ROWS_HERE, FEATS), bf16)
    return call(
        sum_kernel,
        (rows, rows, rows, shape((48, FEATS), f32)),
        [VMEM] * 2 + [ANY] * (2 * GRID),
        scratch=HELD + [pltpu.VMEM((GRID, 2, ROWS_HERE, FEATS), bf16)] + ARRIVED * 2,
        limit=8,
    )(weight_kept, weight_other, *pair_back, *query_back)


def solution(mesh):
    fine = Mesh(
        mesh.devices.reshape(2, 2, GRID, GRID, GRID), ("zh", "core", "tm", "hx", "hy")
    )
    dp, height = ("zh", "core"), ("hx", "hy")
    rows = P(dp, height, "tm")
    slots = P(dp, ("tm",) + height, None, None)
    placed = (
        slots,
        slots,
        P(),
        P(),
        P(),
        P(),
        P(),
        P(height, "tm"),
        rows,
        rows,
        rows,
        rows,
        P("tm", None),
    )
    return jax.shard_map(
        per_device,
        mesh=fine,
        in_specs=placed,
        out_specs=(rows, rows, rows, P(dp + height, "tm")),
        check_vma=False,
    )
```

```python
import functools
import math

import jax
import jax.numpy as jnp
import numpy as np
from jax import lax
from jax.experimental import pallas as pl
from jax.experimental.pallas import tpu as pltpu
from jax.sharding import Mesh
from jax.sharding import PartitionSpec as P

HDIM = 128
IMG = 224
PATCH = 14
SIDE = IMG // PATCH
GRID = 4
HEADS_HERE = 3
ROWS_HERE = 256
FEATS = HEADS_HERE * HDIM
BLOCK = GRID * ROWS_HERE
FRAMES = 64
LANES = 128
QUARTERS = 4
QUARTER_LANES = 32
TAPS = 27
ORDER_LANE = TAPS
QUARTER_CELLS = (PATCH // 2) * (2 * PATCH)

epsilon = 1e-05
pixel_std = (0.26862954, 0.26130258, 0.27577711)

f32 = jnp.float32
bf16 = jnp.bfloat16
MIB = 1024 * 1024
HIGHEST = lax.Precision.HIGHEST
LOG2E = math.log2(math.e)
SCORE_SCALE = HDIM ** (-0.5)


def row_masks():
    masks = np.zeros((8, PATCH), np.float32)
    for half in range(2):
        for shift in range(3):
            low = half * 7 + shift - 1
            masks[half * 3 + shift, max(low, 0) : min(low + 7, PATCH)] = 1
    masks[6, 0] = 1
    masks[7, PATCH - 1] = 1
    return masks


def basis_matrix():
    rows = row_masks()
    columns = np.zeros((3, PATCH), np.float32)
    columns[0] = 1
    columns[1, 0] = 1
    columns[2, PATCH - 1] = 1
    basis = np.zeros((LANES, 3, PATCH, PATCH), np.float32)
    for col in range(3):
        for row in range(8):
            for channel in range(3):
                basis[col * 24 + row * 3 + channel, channel] = np.outer(rows[row], columns[col])
    return basis.reshape(LANES, 3 * PATCH * PATCH)


def spread_matrix():
    spread = np.zeros((6, LANES, LANES), np.float32)
    for half in range(2):
        for side in range(2):
            first = 2 * side + 1
            terms = {
                0: [(first - 1, 2, 1), (first, 0, 1), (first + 1, 0, 1), (first + 1, 2, -1)],
                1: [(first, 0, 1), (first + 1, 0, 1)],
                2: [(first, 0, 1), (first, 1, -1), (first + 1, 0, 1), (first + 2, 1, 1)],
            }
            for shift in range(3):
                groups = [half * 3 + shift]
                if (half, shift) == (0, 0):
                    groups.append(7)
                if (half, shift) == (1, 2):
                    groups.append(6)
                for offset in range(3):
                    for channel in range(3):
                        lane = (half * 2 + side) * QUARTER_LANES + (shift * 3 + offset) * 3 + channel
                        for place, col, sign in terms[offset]:
                            for row in groups:
                                spread[place, col * 24 + row * 3 + channel, lane] += sign
    return spread.reshape(6 * LANES, LANES)


NN = (((1,), (0,)), ((), ()))
NT = (((1,), (1,)), ((), ()))
TN = (((0,), (0,)), ((), ()))


def dot(left, right, dims=NN):
    return lax.dot_general(left, right, dims, preferred_element_type=f32)


def one_hot(condition):
    return jnp.where(condition, 1.0, 0.0).astype(bf16)


def iota(dims, axis):
    return lax.broadcasted_iota(jnp.int32, dims, axis)


def start(copies):
    for copy in copies:
        copy.start()


def fetch(refs, held, arrived):
    copies = [
        pltpu.make_async_copy(ref, kept, arrived.at[place])
        for place, (ref, kept) in enumerate(zip(refs, held))
    ]
    start(copies)
    return copies


def fetch_halves(refs, column, held, arrived):
    return fetch(
        [ref.at[:, pl.ds(column * FEATS, FEATS)] for ref in refs],
        [held.at[place] for place in range(len(refs))],
        arrived,
    )


def window_kernel(gain_ref, order_ref, *refs):
    out_ref, cot_ref, pre_ref, patch_ref, basis_ref, spread_ref, sums, arrived = refs[5:]
    held = (pre_ref, cot_ref, basis_ref, patch_ref, spread_ref)
    copies = fetch(refs[:5], held, arrived)
    copies[0].wait()
    copies[1].wait()
    pre = pre_ref[...].astype(f32)
    centered = pre - jnp.mean(pre, axis=-1, keepdims=True)
    inverse = lax.rsqrt(jnp.mean(centered * centered, axis=-1, keepdims=True) + epsilon)
    normed = centered * inverse
    scaled = cot_ref[...].astype(f32) * gain_ref[...].astype(f32).reshape(1, -1)
    grad_rows = inverse * (
        scaled
        - jnp.mean(scaled, axis=-1, keepdims=True)
        - normed * jnp.mean(scaled * normed, axis=-1, keepdims=True)
    )
    grad_rows = grad_rows.astype(bf16)
    channel = iota((LANES, 1), 0) % 3
    scale = jnp.where(
        channel == 0, 1.0 / pixel_std[0], jnp.where(channel == 1, 1.0 / pixel_std[1], 1.0 / pixel_std[2])
    ) * (1.0 / QUARTER_CELLS)
    copies[2].wait()
    copies[3].wait()
    weights = dot(basis_ref[...], patch_ref[...]) * scale
    high = weights.astype(bf16)
    low = (weights - high.astype(f32)).astype(bf16)
    both = dot(grad_rows, jnp.concatenate([high, low], axis=0), NT)
    patch_sums = both[:, :LANES] + both[:, LANES:]
    group = (iota((SIDE * SIDE, LANES), 1) // 3) % 8
    edge = jnp.zeros((SIDE, LANES), f32)
    above = jnp.concatenate([edge, patch_sums[:-SIDE]], axis=0)
    below = jnp.concatenate([patch_sums[SIDE:], edge], axis=0)
    patch_sums = jnp.where(group == 7, above, jnp.where(group == 6, below, patch_sums))
    sums[pl.ds(0, 8), :] = jnp.zeros((8, LANES), f32)
    sums[pl.ds(8 + SIDE * SIDE, 8), :] = jnp.zeros((8, LANES), f32)
    sums[pl.ds(8, SIDE * SIDE), :] = patch_sums
    copies[4].wait()
    column = iota((SIDE * GRID, LANES), 0) % GRID
    total = jnp.zeros((SIDE * GRID, LANES), f32)
    for place in range(6):
        picked = sums[pl.ds(7 + place, SIDE * GRID, stride=GRID), :]
        if place == 0:
            picked = jnp.where(column == 0, 0.0, picked)
        if place == 5:
            picked = jnp.where(column == GRID - 1, 0.0, picked)
        high = picked.astype(bf16)
        low = (picked - high.astype(f32)).astype(bf16)
        both = dot(
            jnp.concatenate([high, low], axis=0), spread_ref[pl.ds(place * LANES, LANES), :]
        )
        total = total + (both[: SIDE * GRID] + both[SIDE * GRID :])
    windows = total.astype(bf16)
    entries = jnp.where(
        iota((16, 64), 1) % 16 == iota((16, 64), 0), order_ref[...].astype(f32), 0.0
    ).astype(bf16)
    order = dot(entries, one_hot(iota((64, LANES), 1) == ORDER_LANE + iota((64, LANES), 0) // 16))
    order = order.astype(bf16)
    for target_x in range(GRID):
        block = windows[target_x * 16 : (target_x + 1) * 16] + order
        for target_t in range(GRID):
            for target_y in range(GRID):
                out_ref[(target_t * GRID + target_x) * GRID + target_y] = block


def weights_kernel(join_from, out_w_from, joint_ref, picked_ref, join_ref, out_w_ref, arrived):
    here_y = lax.axis_index("hy")
    copies = fetch([join_from, out_w_from], [join_ref, out_w_ref], arrived)
    copies[0].wait()
    copies[1].wait()
    joint_ref[...] = dot(join_ref[...], out_w_ref[...], NT).astype(bf16)
    row, column = iota((96, 384), 0), iota((96, 384), 1)
    half = row // 48
    pick = one_hot(column == half * 192 + here_y * 48 + (row - half * 48))
    for pair in range(8):
        rows = dot(pick, join_ref[:, pl.ds(pair * 384, 384)], NT).astype(bf16)
        z, core, x = pair // 4, (pair % 4) // 2, (pair % 2) * 2
        for step in range(2):
            picked_ref[pl.ds((x + step) * 192 + (z * 2 + core) * 48, 48), :] = rows[
                step * 48 : (step + 1) * 48
            ]


def totals_kernel(*refs):
    out_ref, query_held, key_held, query_arrived, key_arrived = refs[2 * GRID :]
    key_copies = fetch_halves(refs[GRID : 2 * GRID], 0, key_held, key_arrived)
    query_copies = fetch_halves(refs[:GRID], 0, query_held, query_arrived)
    for copy in key_copies:
        copy.wait()
    for head in range(HEADS_HERE):
        columns = pl.ds(head * HDIM, HDIM)
        for piece in range(GRID):
            if head == 0:
                query_copies[piece].wait()
            query = query_held[piece, :, columns]
            scores = [dot(key_held[other, :, columns], query, NT) for other in range(GRID)]
            top = functools.reduce(
                jnp.maximum, [jnp.max(tile, axis=0, keepdims=True) for tile in scores]
            ) * (SCORE_SCALE * LOG2E)
            total = sum(
                jnp.sum(jnp.exp2(tile * (SCORE_SCALE * LOG2E) - top), axis=0, keepdims=True)
                for tile in scores
            )
            out_ref[pl.ds(head, 1), pl.ds(piece * ROWS_HERE, ROWS_HERE)] = top + jnp.log2(total)
    out_ref[pl.ds(HEADS_HERE, 8 - HEADS_HERE), :] = jnp.zeros((8 - HEADS_HERE, BLOCK), f32)


def token_part(owner_ref, conv_ref, recv_ref, arrivals, frames, conv_big, ordered):
    here_x = lax.axis_index("hx")
    here_y = lax.axis_index("hy")
    frames[0] = jnp.zeros((16, LANES), bf16)
    frames[FRAMES + 1] = jnp.zeros((16, LANES), bf16)
    row, column = iota((3 * QUARTER_LANES, 3 * TAPS), 0), iota((3 * QUARTER_LANES, 3 * TAPS), 1)
    tap = row % QUARTER_LANES
    conv = dot(
        one_hot((tap < TAPS) & (column == (row // QUARTER_LANES) * TAPS + tap)), conv_ref[...]
    ).astype(bf16)
    conv_big[...] = jnp.zeros_like(conv_big)
    for quarter in range(QUARTERS):
        for shift in range(3):
            conv_big[
                pl.ds(shift * LANES + quarter * QUARTER_LANES, QUARTER_LANES),
                pl.ds(quarter * LANES, LANES),
            ] = conv[shift * QUARTER_LANES : (shift + 1) * QUARTER_LANES]
    arrivals.wait()

    def place_frame(frame, carry):
        frames[frame + 1] = recv_ref[(frame // 16) * 16 + owner_ref[frame]]
        return carry

    lax.fori_loop(0, FRAMES, place_frame, 0, unroll=8)
    lane = iota((16, ROWS_HERE), 1)
    for slab_t in range(GRID):
        pooled = sum(
            dot(
                frames[pl.ds(slab_t * 16 + shift, 16)].reshape(ROWS_HERE, LANES),
                conv_big[pl.ds(shift * LANES, LANES), :],
            )
            for shift in range(3)
        ).astype(bf16)
        pieces = []
        for piece in range(GRID):
            slab = lax.rem(here_y + piece, GRID)
            block = recv_ref[slab_t * 16 + here_x * GRID + slab].astype(f32)
            for part in range(4):
                order = block[:, ORDER_LANE + part : ORDER_LANE + part + 1].astype(jnp.int32)
                target = (order // 4) * 16 + slab * 4 + lax.rem(order, 4)
                pieces.append(one_hot(lane == target))
        chosen = dot(jnp.concatenate(pieces, axis=0), pooled).astype(bf16)
        for piece in range(GRID):
            ordered[pl.ds(piece * ROWS_HERE + slab_t * 64, 64), :] = chosen[
                piece * 64 : (piece + 1) * 64
            ]


def token_kernel(owner_ref, conv_ref, *refs):
    recv_from, joint_from, picked_from = refs[:3]
    (
        dots_ref,
        grad_out,
        weight_out,
        frames,
        conv_big,
        ordered,
        recv_ref,
        joint_ref,
        picked_ref,
        weight_made,
        out_held,
        grad_made,
        first_arrived,
        out_arrived,
        grad_sent,
        weight_sent,
    ) = refs[GRID + 3 :]
    firsts = fetch(
        [recv_from, joint_from, picked_from], [recv_ref, joint_ref, picked_ref], first_arrived
    )
    out_copies = fetch_halves(refs[3 : GRID + 3], 1, out_held, out_arrived)
    token_part(owner_ref, conv_ref, recv_ref, firsts[0], frames, conv_big, ordered)
    firsts[1].wait()
    ones = jnp.ones((8, 2 * HDIM), bf16)
    sends = []
    dots_ref[...] = jnp.zeros_like(dots_ref)
    outer = jnp.zeros((QUARTERS * LANES, FEATS), f32)
    for piece in range(GRID):
        rows = ordered[pl.ds(piece * ROWS_HERE, ROWS_HERE), :]
        grads = dot(rows, joint_ref[...]).astype(bf16)
        grad_made[piece] = grads
        sends += fetch([grad_made.at[piece]], [grad_out.at[piece]], grad_sent.at[pl.ds(piece, 1)])
        out_copies[piece].wait()
        outs = out_held[piece]
        products = grads.astype(f32) * outs.astype(f32)
        high = products.astype(bf16)
        low = (products - high.astype(f32)).astype(bf16)
        for head in range(HEADS_HERE):
            columns = slice(head * HDIM, (head + 1) * HDIM)
            both = jnp.concatenate([high[:, columns], low[:, columns]], axis=1)
            dots_ref[pl.ds(head, 1), pl.ds(piece * ROWS_HERE, ROWS_HERE)] = dot(ones, both, NT)[
                0:1
            ]
        outer = outer + dot(rows, outs, TN)
    firsts[2].wait()
    weight_made[...] = (
        dot(picked_ref[...], outer.astype(bf16)) * (1.0 / math.sqrt(FRAMES * 64 * 4))
    ).astype(bf16)
    sends += fetch([weight_made], [weight_out], weight_sent)
    for send in sends:
        send.wait()


def grads_kernel(dots_ref, *refs):
    total_refs, grad_from = refs[:GRID], refs[GRID]
    query_refs, pair_refs = refs[GRID + 1 : 2 * GRID + 1], refs[2 * GRID + 1 : 3 * GRID + 1]
    rest = refs[3 * GRID + 1 :]
    query_out, pair_out = rest[:GRID], rest[GRID : 2 * GRID]
    (
        sums,
        query_held,
        key_held,
        value_held,
        grad_ref,
        query_made,
        pair_made,
        query_arrived,
        key_arrived,
        value_arrived,
        grad_arrived,
        query_sent,
        pair_sent,
    ) = rest[2 * GRID :]
    sends_order = (2, 1, 3, 0)
    query_copies = fetch_halves(query_refs, 0, query_held, query_arrived)
    query_copies += fetch([grad_from], [grad_ref], grad_arrived)
    key_copies, value_copies = (
        [
            pltpu.make_async_copy(
                pair_refs[other].at[:, pl.ds(half * FEATS, FEATS)],
                held.at[other],
                arrived.at[other],
            )
            for other in range(GRID)
        ]
        for half, held, arrived in ((0, key_held, key_arrived), (1, value_held, value_arrived))
    )
    start([key_copies[sends_order[0]], value_copies[sends_order[0]]])
    root = math.sqrt(FRAMES * 64)
    totals = []
    for piece in range(GRID):
        parts = [
            total_refs[step][:, pl.ds(((piece - step) % GRID) * ROWS_HERE, ROWS_HERE)]
            for step in range(GRID)
        ]
        top = functools.reduce(jnp.maximum, parts)
        totals.append(top + jnp.log2(sum(jnp.exp2(part - top) for part in parts)))
    totals = jnp.concatenate(totals, axis=1)
    for copy in query_copies:
        copy.wait()
    for other in sends_order[1:]:
        start([key_copies[other], value_copies[other]])
    sends = []
    for other in sends_order:
        key_copies[other].wait()
        value_copies[other].wait()
        for head in range(HEADS_HERE):
            columns = pl.ds(head * HDIM, HDIM)
            query = query_held[:, :, columns].reshape(BLOCK, HDIM)
            grad = grad_ref[:, :, columns].reshape(BLOCK, HDIM)
            key = key_held[other, :, columns]
            value = value_held[other, :, columns]
            weights = jnp.exp2(
                dot(key, query, NT) * (SCORE_SCALE * LOG2E) - totals[head : head + 1]
            )
            dscore = (weights * (dot(value, grad, NT) - dots_ref[pl.ds(head, 1), :])).astype(bf16)
            pair_made[other, 1, :, columns] = (dot(weights.astype(bf16), grad) * root).astype(bf16)
            pair_made[other, 0, :, columns] = (
                dot(dscore, query) * (root * SCORE_SCALE)
            ).astype(bf16)
            part = dot(key.T, dscore)
            if other == sends_order[0]:
                sums[head] = part
            else:
                sums[head] += part
        send = pltpu.make_async_copy(pair_made.at[other], pair_out[other], pair_sent.at[other])
        send.start()
        sends.append(send)
    for piece in sends_order:
        for head in range(HEADS_HERE):
            query_made[piece, :, pl.ds(head * HDIM, HDIM)] = (
                sums[head, :, pl.ds(piece * ROWS_HERE, ROWS_HERE)].T * (root * SCORE_SCALE)
            ).astype(bf16)
        send = pltpu.make_async_copy(query_made.at[piece], query_out[piece], query_sent.at[piece])
        send.start()
        sends.append(send)
    for send in sends:
        send.wait()


def sum_kernel(parts_ref, *refs):
    pair_refs, query_refs = refs[:GRID], refs[GRID : 2 * GRID]
    query_out, key_out, value_out, weight_out, query_held, pair_held, *arrived = refs[2 * GRID :]
    pair_copies = fetch(pair_refs, [pair_held.at[step] for step in range(GRID)], arrived[1])
    query_copies = fetch(query_refs, [query_held.at[step] for step in range(GRID)], arrived[0])
    weight_out[...] = sum(parts_ref[source].astype(f32) for source in range(4))
    for copy in query_copies:
        copy.wait()
    query_out[0] = sum(query_held[step].astype(f32) for step in range(GRID)).astype(bf16)
    for copy in pair_copies:
        copy.wait()
    for place, out_ref in enumerate((key_out, value_out)):
        out_ref[0] = sum(pair_held[step, place].astype(f32) for step in range(GRID)).astype(bf16)


def call(kernel, out_shape, in_specs, scratch=(), out_spec=None, limit=56):
    return pl.pallas_call(
        kernel,
        out_shape=out_shape,
        in_specs=in_specs,
        out_specs=out_spec or jax.tree.map(lambda _: VMEM, out_shape),
        scratch_shapes=list(scratch),
        compiler_params=pltpu.CompilerParams(vmem_limit_bytes=limit * MIB),
        cost_estimate=pl.CostEstimate(flops=10**6, bytes_accessed=10**5, transcendentals=0),
    )


VMEM = pl.BlockSpec(memory_space=pltpu.VMEM)
SMEM = pl.BlockSpec(memory_space=pltpu.SMEM)
ANY = pl.BlockSpec(memory_space=pl.ANY)
HBM = pl.BlockSpec(memory_space=pltpu.HBM)
HELD = [pltpu.VMEM((GRID, ROWS_HERE, FEATS), bf16)]
ARRIVED = [pltpu.SemaphoreType.DMA((GRID,))]


def shape(dims, dtype):
    return jax.ShapeDtypeStruct(dims, dtype)


def from_ahead(block, axis, step):
    return lax.ppermute(block, axis, [(i, (i - step) % GRID) for i in range(GRID)])


def to_ahead(block, axis, step):
    return lax.ppermute(block, axis, [(i, (i + step) % GRID) for i in range(GRID)])


def gather(block, axis):
    return [block] + [from_ahead(block, axis, step) for step in range(1, GRID)]


def per_device(
    vit_cot,
    vit_pre,
    ln_gain,
    patch_w,
    frame_owner,
    conv_w,
    join_w,
    token_order,
    queries,
    keys,
    values,
    attn_out,
    out_w,
):
    key_value = jnp.concatenate([keys[0], values[0]], axis=1)
    query_out = jnp.concatenate([queries[0], attn_out[0]], axis=1)
    sides = [from_ahead(key_value, "hx", step) for step in (1, 3)]
    sides += [from_ahead(query_out, "hy", step) for step in (1, 3)]
    windows = call(
        window_kernel,
        shape((FRAMES, 16, LANES), bf16),
        [VMEM] * 2 + [ANY] * 5,
        scratch=[
            pltpu.VMEM(vit_cot.shape[2:], bf16),
            pltpu.VMEM(vit_pre.shape[2:], bf16),
            pltpu.VMEM(patch_w.shape, bf16),
            pltpu.VMEM((LANES, patch_w.shape[0]), bf16),
            pltpu.VMEM((6 * LANES, LANES), bf16),
            pltpu.VMEM((SIDE * SIDE + 16, LANES), f32),
            pltpu.SemaphoreType.DMA((5,)),
        ],
    )(
        ln_gain,
        token_order,
        vit_pre[0, 0],
        vit_cot[0, 0],
        jnp.asarray(basis_matrix(), bf16),
        patch_w,
        jnp.asarray(spread_matrix(), bf16),
    )
    windows, join_w, key_value, query_out, sides = lax.optimization_barrier(
        (windows, join_w, key_value, query_out, sides)
    )
    key_values = [key_value, sides[0], from_ahead(key_value, "hx", 2), sides[1]]
    query_outs = [query_out, sides[2], from_ahead(query_out, "hy", 2), sides[3]]
    joint, picked = call(
        weights_kernel,
        (shape((QUARTERS * LANES, FEATS), bf16), shape((768, QUARTERS * LANES), bf16)),
        [ANY] * 2,
        scratch=[
            pltpu.VMEM(join_w.shape, bf16),
            pltpu.VMEM(out_w.shape, bf16),
            pltpu.SemaphoreType.DMA((2,)),
        ],
    )(join_w, out_w)
    windows, joint, picked, key_values, query_outs = lax.optimization_barrier(
        (windows, joint, picked, key_values, query_outs)
    )
    received = lax.all_to_all(
        windows, ("tm", "hx", "hy"), split_axis=0, concat_axis=0, tiled=True
    )
    totals = call(
        totals_kernel,
        shape((8, BLOCK), f32),
        [ANY] * (2 * GRID),
        scratch=HELD * 2 + ARRIVED * 2,
        limit=24,
    )(*query_outs, *key_values)
    totals, received = lax.optimization_barrier((totals, received))
    total_pieces = gather(totals, "hy")
    row_dots, grad_out, weight_part = call(
        token_kernel,
        (
            shape((8, BLOCK), f32),
            shape((GRID, ROWS_HERE, FEATS), bf16),
            shape((768, FEATS), bf16),
        ),
        [SMEM, VMEM] + [ANY] * (3 + GRID),
        scratch=[
            pltpu.VMEM((FRAMES + 2, 16, LANES), bf16),
            pltpu.VMEM((3 * LANES, QUARTERS * LANES), bf16),
            pltpu.VMEM((BLOCK, QUARTERS * LANES), bf16),
            pltpu.VMEM((FRAMES, 16, LANES), bf16),
            pltpu.VMEM((QUARTERS * LANES, FEATS), bf16),
            pltpu.VMEM((768, QUARTERS * LANES), bf16),
            pltpu.VMEM((768, FEATS), bf16),
        ]
        + HELD * 2
        + [pltpu.SemaphoreType.DMA((3,))]
        + ARRIVED * 2
        + [pltpu.SemaphoreType.DMA((1,))],
        out_spec=(VMEM, ANY, ANY),
    )(frame_owner, conv_w, received, joint, picked, *query_outs)
    outs = call(
        grads_kernel,
        tuple([shape((ROWS_HERE, FEATS), bf16)] * GRID)
        + tuple([shape((2, ROWS_HERE, FEATS), bf16)] * GRID),
        [VMEM] * (1 + GRID) + [ANY] * (1 + 2 * GRID),
        scratch=[pltpu.VMEM((HEADS_HERE, HDIM, BLOCK), f32)]
        + HELD * 5
        + [pltpu.VMEM((GRID, 2, ROWS_HERE, FEATS), bf16)]
        + ARRIVED * 3
        + [pltpu.SemaphoreType.DMA((1,))]
        + ARRIVED * 2,
        out_spec=tuple([ANY] * (2 * GRID)),
    )(row_dots, *total_pieces, grad_out, *query_outs, *key_values)
    query_parts, pair_parts = outs[:GRID], outs[GRID:]
    weight_part = lax.psum_scatter(weight_part, "hx", scatter_dimension=0, tiled=True)
    weight_parts = lax.all_to_all(
        weight_part.reshape(4, 48, FEATS),
        ("zh", "core"),
        split_axis=0,
        concat_axis=0,
        tiled=True,
    )
    pair_back = [pair_parts[0]] + [
        to_ahead(pair_parts[step], "hx", step) for step in range(1, GRID)
    ]
    query_back = [query_parts[0]] + [
        to_ahead(query_parts[step], "hy", step) for step in range(1, GRID)
    ]

    rows = shape((1, ROWS_HERE, FEATS), bf16)
    return call(
        sum_kernel,
        (rows, rows, rows, shape((48, FEATS), f32)),
        [VMEM] + ([HBM] + [ANY] * (GRID - 1)) * 2,
        scratch=HELD + [pltpu.VMEM((GRID, 2, ROWS_HERE, FEATS), bf16)] + ARRIVED * 2,
        limit=8,
    )(weight_parts, *pair_back, *query_back)


def solution(mesh):
    fine = Mesh(
        mesh.devices.reshape(2, 2, GRID, GRID, GRID), ("zh", "core", "tm", "hx", "hy")
    )
    dp, height = ("zh", "core"), ("hx", "hy")
    rows = P(dp, height, "tm")
    slots = P(dp, ("tm",) + height, None, None)
    placed = (
        slots,
        slots,
        P(),
        P(),
        P(),
        P(),
        P(),
        P(height, "tm"),
        rows,
        rows,
        rows,
        rows,
        P("tm", None),
    )
    return jax.shard_map(
        per_device,
        mesh=fine,
        in_specs=placed,
        out_specs=(rows, rows, rows, P(dp + height, "tm")),
        check_vma=False,
    )
```

```python
import functools
import math

import jax
import jax.numpy as jnp
import numpy as np
from jax import lax
from jax.experimental import pallas as pl
from jax.experimental.pallas import tpu as pltpu
from jax.sharding import Mesh
from jax.sharding import PartitionSpec as P

HDIM = 128
IMG = 224
PATCH = 14
SIDE = IMG // PATCH
GRID = 4
HEADS_HERE = 3
ROWS_HERE = 256
FEATS = HEADS_HERE * HDIM
BLOCK = GRID * ROWS_HERE
FRAMES = 64
LANES = 128
QUARTERS = 4
QUARTER_LANES = 32
TAPS = 27
ORDER_LANE = TAPS
QUARTER_CELLS = (PATCH // 2) * (2 * PATCH)

epsilon = 1e-05
pixel_std = (0.26862954, 0.26130258, 0.27577711)

f32 = jnp.float32
bf16 = jnp.bfloat16
MIB = 1024 * 1024
HIGHEST = lax.Precision.HIGHEST
LOG2E = math.log2(math.e)
SCORE_SCALE = HDIM ** (-0.5)


def row_masks():
    masks = np.zeros((8, PATCH), np.float32)
    for half in range(2):
        for shift in range(3):
            low = half * 7 + shift - 1
            masks[half * 3 + shift, max(low, 0) : min(low + 7, PATCH)] = 1
    masks[6, 0] = 1
    masks[7, PATCH - 1] = 1
    return masks


def basis_matrix():
    rows = row_masks()
    columns = np.zeros((3, PATCH), np.float32)
    columns[0] = 1
    columns[1, 0] = 1
    columns[2, PATCH - 1] = 1
    basis = np.zeros((LANES, 3, PATCH, PATCH), np.float32)
    for col in range(3):
        for row in range(8):
            for channel in range(3):
                basis[col * 24 + row * 3 + channel, channel] = np.outer(rows[row], columns[col])
    return basis.reshape(LANES, 3 * PATCH * PATCH)


def spread_matrix():
    spread = np.zeros((6, LANES, LANES), np.float32)
    for half in range(2):
        for side in range(2):
            first = 2 * side + 1
            terms = {
                0: [(first - 1, 2, 1), (first, 0, 1), (first + 1, 0, 1), (first + 1, 2, -1)],
                1: [(first, 0, 1), (first + 1, 0, 1)],
                2: [(first, 0, 1), (first, 1, -1), (first + 1, 0, 1), (first + 2, 1, 1)],
            }
            for shift in range(3):
                groups = [half * 3 + shift]
                if (half, shift) == (0, 0):
                    groups.append(7)
                if (half, shift) == (1, 2):
                    groups.append(6)
                for offset in range(3):
                    for channel in range(3):
                        lane = (half * 2 + side) * QUARTER_LANES + (shift * 3 + offset) * 3 + channel
                        for place, col, sign in terms[offset]:
                            for row in groups:
                                spread[place, col * 24 + row * 3 + channel, lane] += sign
    return spread.reshape(6 * LANES, LANES)


NN = (((1,), (0,)), ((), ()))
NT = (((1,), (1,)), ((), ()))
TN = (((0,), (0,)), ((), ()))


def dot(left, right, dims=NN):
    return lax.dot_general(left, right, dims, preferred_element_type=f32)


def one_hot(condition):
    return jnp.where(condition, 1.0, 0.0).astype(bf16)


def iota(dims, axis):
    return lax.broadcasted_iota(jnp.int32, dims, axis)


def start(copies):
    for copy in copies:
        copy.start()


def fetch(refs, held, arrived):
    copies = [
        pltpu.make_async_copy(ref, kept, arrived.at[place])
        for place, (ref, kept) in enumerate(zip(refs, held))
    ]
    start(copies)
    return copies


def fetch_halves(refs, column, held, arrived):
    return fetch(
        [ref.at[:, pl.ds(column * FEATS, FEATS)] for ref in refs],
        [held.at[place] for place in range(len(refs))],
        arrived,
    )


def window_kernel(gain_ref, order_ref, *refs):
    out_ref, cot_ref, pre_ref, patch_ref, basis_ref, spread_ref, sums, arrived = refs[5:]
    held = (pre_ref, cot_ref, basis_ref, patch_ref, spread_ref)
    copies = fetch(refs[:5], held, arrived)
    copies[0].wait()
    copies[1].wait()
    pre = pre_ref[...].astype(f32)
    centered = pre - jnp.mean(pre, axis=-1, keepdims=True)
    inverse = lax.rsqrt(jnp.mean(centered * centered, axis=-1, keepdims=True) + epsilon)
    normed = centered * inverse
    scaled = cot_ref[...].astype(f32) * gain_ref[...].astype(f32).reshape(1, -1)
    grad_rows = inverse * (
        scaled
        - jnp.mean(scaled, axis=-1, keepdims=True)
        - normed * jnp.mean(scaled * normed, axis=-1, keepdims=True)
    )
    grad_rows = grad_rows.astype(bf16)
    channel = iota((LANES, 1), 0) % 3
    scale = jnp.where(
        channel == 0, 1.0 / pixel_std[0], jnp.where(channel == 1, 1.0 / pixel_std[1], 1.0 / pixel_std[2])
    ) * (1.0 / QUARTER_CELLS)
    copies[2].wait()
    copies[3].wait()
    weights = dot(basis_ref[...], patch_ref[...]) * scale
    high = weights.astype(bf16)
    low = (weights - high.astype(f32)).astype(bf16)
    both = dot(grad_rows, jnp.concatenate([high, low], axis=0), NT)
    patch_sums = both[:, :LANES] + both[:, LANES:]
    group = (iota((SIDE * SIDE, LANES), 1) // 3) % 8
    edge = jnp.zeros((SIDE, LANES), f32)
    above = jnp.concatenate([edge, patch_sums[:-SIDE]], axis=0)
    below = jnp.concatenate([patch_sums[SIDE:], edge], axis=0)
    patch_sums = jnp.where(group == 7, above, jnp.where(group == 6, below, patch_sums))
    sums[pl.ds(0, 8), :] = jnp.zeros((8, LANES), f32)
    sums[pl.ds(8 + SIDE * SIDE, 8), :] = jnp.zeros((8, LANES), f32)
    sums[pl.ds(8, SIDE * SIDE), :] = patch_sums
    copies[4].wait()
    column = iota((SIDE * GRID, LANES), 0) % GRID
    total = jnp.zeros((SIDE * GRID, LANES), f32)
    for place in range(6):
        picked = sums[pl.ds(7 + place, SIDE * GRID, stride=GRID), :]
        if place == 0:
            picked = jnp.where(column == 0, 0.0, picked)
        if place == 5:
            picked = jnp.where(column == GRID - 1, 0.0, picked)
        high = picked.astype(bf16)
        low = (picked - high.astype(f32)).astype(bf16)
        both = dot(
            jnp.concatenate([high, low], axis=0), spread_ref[pl.ds(place * LANES, LANES), :]
        )
        total = total + (both[: SIDE * GRID] + both[SIDE * GRID :])
    windows = total.astype(bf16)
    entries = jnp.where(
        iota((16, 64), 1) % 16 == iota((16, 64), 0), order_ref[...].astype(f32), 0.0
    ).astype(bf16)
    order = dot(entries, one_hot(iota((64, LANES), 1) == ORDER_LANE + iota((64, LANES), 0) // 16))
    order = order.astype(bf16)
    for target_x in range(GRID):
        block = windows[target_x * 16 : (target_x + 1) * 16] + order
        for target_t in range(GRID):
            for target_y in range(GRID):
                out_ref[(target_t * GRID + target_x) * GRID + target_y] = block


def weights_kernel(join_from, out_w_from, joint_ref, picked_ref, join_ref, out_w_ref, arrived):
    here_y = lax.axis_index("hy")
    copies = fetch([join_from, out_w_from], [join_ref, out_w_ref], arrived)
    copies[0].wait()
    copies[1].wait()
    joint_ref[...] = dot(join_ref[...], out_w_ref[...], NT).astype(bf16)
    row, column = iota((96, 384), 0), iota((96, 384), 1)
    half = row // 48
    pick = one_hot(column == half * 192 + here_y * 48 + (row - half * 48))
    for pair in range(8):
        rows = dot(pick, join_ref[:, pl.ds(pair * 384, 384)], NT).astype(bf16)
        z, core, x = pair // 4, (pair % 4) // 2, (pair % 2) * 2
        for step in range(2):
            picked_ref[pl.ds((core * GRID + x + step) * 96 + z * 48, 48), :] = rows[
                step * 48 : (step + 1) * 48
            ]


def totals_kernel(*refs):
    query_refs, key_refs, out_ref = refs[:GRID], refs[GRID : 2 * GRID], refs[2 * GRID]
    for head in range(HEADS_HERE):
        columns = pl.ds(head * HDIM, HDIM)
        for piece in range(GRID):
            query = query_refs[piece][:, columns]
            scores = [dot(key_ref[:, columns], query, NT) for key_ref in key_refs]
            top = functools.reduce(
                jnp.maximum, [jnp.max(tile, axis=0, keepdims=True) for tile in scores]
            ) * (SCORE_SCALE * LOG2E)
            total = sum(
                jnp.sum(jnp.exp2(tile * (SCORE_SCALE * LOG2E) - top), axis=0, keepdims=True)
                for tile in scores
            )
            out_ref[pl.ds(head, 1), pl.ds(piece * ROWS_HERE, ROWS_HERE)] = top + jnp.log2(total)
    out_ref[pl.ds(HEADS_HERE, 8 - HEADS_HERE), :] = jnp.zeros((8 - HEADS_HERE, BLOCK), f32)


def token_part(owner_ref, conv_ref, recv_ref, arrivals, frames, conv_big, ordered):
    here_x = lax.axis_index("hx")
    here_y = lax.axis_index("hy")
    frames[0] = jnp.zeros((16, LANES), bf16)
    frames[FRAMES + 1] = jnp.zeros((16, LANES), bf16)
    row, column = iota((3 * QUARTER_LANES, 3 * TAPS), 0), iota((3 * QUARTER_LANES, 3 * TAPS), 1)
    tap = row % QUARTER_LANES
    conv = dot(
        one_hot((tap < TAPS) & (column == (row // QUARTER_LANES) * TAPS + tap)), conv_ref[...]
    ).astype(bf16)
    conv_big[...] = jnp.zeros_like(conv_big)
    for quarter in range(QUARTERS):
        for shift in range(3):
            conv_big[
                pl.ds(shift * LANES + quarter * QUARTER_LANES, QUARTER_LANES),
                pl.ds(quarter * LANES, LANES),
            ] = conv[shift * QUARTER_LANES : (shift + 1) * QUARTER_LANES]
    arrivals.wait()

    def place_frame(frame, carry):
        frames[frame + 1] = recv_ref[(frame // 16) * 16 + owner_ref[frame]]
        return carry

    lax.fori_loop(0, FRAMES, place_frame, 0, unroll=8)
    lane = iota((16, ROWS_HERE), 1)
    for slab_t in range(GRID):
        pooled = sum(
            dot(
                frames[pl.ds(slab_t * 16 + shift, 16)].reshape(ROWS_HERE, LANES),
                conv_big[pl.ds(shift * LANES, LANES), :],
            )
            for shift in range(3)
        ).astype(bf16)
        pieces = []
        for piece in range(GRID):
            slab = lax.rem(here_y + piece, GRID)
            block = recv_ref[slab_t * 16 + here_x * GRID + slab].astype(f32)
            for part in range(4):
                order = block[:, ORDER_LANE + part : ORDER_LANE + part + 1].astype(jnp.int32)
                target = (order // 4) * 16 + slab * 4 + lax.rem(order, 4)
                pieces.append(one_hot(lane == target))
        chosen = dot(jnp.concatenate(pieces, axis=0), pooled).astype(bf16)
        for piece in range(GRID):
            ordered[pl.ds(piece * ROWS_HERE + slab_t * 64, 64), :] = chosen[
                piece * 64 : (piece + 1) * 64
            ]


def block_grads(key, value, query, grad, totals, dots):
    weights = jnp.exp2(dot(key, query, NT) * (SCORE_SCALE * LOG2E) - totals)
    dscore = (weights * (dot(value, grad, NT) - dots)).astype(bf16)
    root = math.sqrt(FRAMES * 64)
    key_grad = (dot(dscore, query) * (root * SCORE_SCALE)).astype(bf16)
    value_grad = (dot(weights.astype(bf16), grad) * root).astype(bf16)
    return key_grad, value_grad, dot(key.T, dscore)


def others_kernel(owner_ref, conv_ref, *refs):
    total_refs, (recv_from, joint_from, picked_from) = refs[:GRID], refs[GRID : GRID + 3]
    query_refs, pair_refs = refs[GRID + 3 : 2 * GRID + 3], refs[2 * GRID + 3 : 3 * GRID + 2]
    (
        totals_ref,
        dots_ref,
        sums_out,
        grad_out,
        weight_out,
        *rest,
    ) = refs[3 * GRID + 2 :]
    pair_out = rest[: GRID - 1]
    (
        frames,
        conv_big,
        ordered,
        recv_ref,
        joint_ref,
        picked_ref,
        weight_made,
        sums,
        out_held,
        query_held,
        key_held,
        value_held,
        grad_ref,
        pair_made,
        first_arrived,
        out_arrived,
        query_arrived,
        key_arrived,
        value_arrived,
        pair_sent,
        weight_sent,
        sums_sent,
    ) = rest[GRID - 1 :]
    firsts = fetch(
        [recv_from, joint_from, picked_from], [recv_ref, joint_ref, picked_ref], first_arrived
    )
    out_copies = fetch_halves(query_refs, 1, out_held, out_arrived)
    query_copies = fetch_halves(query_refs, 0, query_held, query_arrived)
    key_copies = fetch_halves(pair_refs, 0, key_held, key_arrived)
    value_copies = fetch_halves(pair_refs, 1, value_held, value_arrived)
    dots_ref[...] = jnp.zeros_like(dots_ref)
    for piece in range(GRID):
        columns = pl.ds(piece * ROWS_HERE, ROWS_HERE)
        parts = [
            total_refs[step][:, pl.ds(((piece - step) % GRID) * ROWS_HERE, ROWS_HERE)]
            for step in range(GRID)
        ]
        top = functools.reduce(jnp.maximum, parts)
        totals_ref[:, columns] = top + jnp.log2(sum(jnp.exp2(part - top) for part in parts))
    token_part(owner_ref, conv_ref, recv_ref, firsts[0], frames, conv_big, ordered)
    firsts[1].wait()
    ones = jnp.ones((8, 2 * HDIM), bf16)
    outer = jnp.zeros((QUARTERS * LANES, FEATS), f32)
    for piece in range(GRID):
        rows = ordered[pl.ds(piece * ROWS_HERE, ROWS_HERE), :]
        grads = dot(rows, joint_ref[...]).astype(bf16)
        grad_ref[piece] = grads
        out_copies[piece].wait()
        outs = out_held[piece]
        products = grads.astype(f32) * outs.astype(f32)
        high = products.astype(bf16)
        low = (products - high.astype(f32)).astype(bf16)
        for head in range(HEADS_HERE):
            columns = slice(head * HDIM, (head + 1) * HDIM)
            both = jnp.concatenate([high[:, columns], low[:, columns]], axis=1)
            dots_ref[pl.ds(head, 1), pl.ds(piece * ROWS_HERE, ROWS_HERE)] = dot(ones, both, NT)[
                0:1
            ]
        outer = outer + dot(rows, outs, TN)
    firsts[2].wait()
    weight_made[...] = (
        dot(picked_ref[...], outer.astype(bf16)) * (1.0 / math.sqrt(FRAMES * 64 * 4))
    ).astype(bf16)
    sends = fetch([weight_made, grad_ref], [weight_out, grad_out], weight_sent)
    for copy in query_copies:
        copy.wait()
    for place in (1, 0, 2):
        key_copies[place].wait()
        value_copies[place].wait()
        for head in range(HEADS_HERE):
            columns = pl.ds(head * HDIM, HDIM)
            key_grad, value_grad, part = block_grads(
                key_held[place, :, columns],
                value_held[place, :, columns],
                query_held[:, :, columns].reshape(BLOCK, HDIM),
                grad_ref[:, :, columns].reshape(BLOCK, HDIM),
                totals_ref[pl.ds(head, 1), :],
                dots_ref[pl.ds(head, 1), :],
            )
            pair_made[place, 0, :, columns] = key_grad
            pair_made[place, 1, :, columns] = value_grad
            if place == 1:
                sums[head] = part
            else:
                sums[head] += part
            if place == 2:
                sends += fetch(
                    [sums.at[head]], [sums_out.at[head]], sums_sent.at[pl.ds(head, 1)]
                )
        sends += fetch([pair_made.at[place]], [pair_out[place]], pair_sent.at[pl.ds(place, 1)])
    for send in sends:
        send.wait()


def own_kernel(totals_ref, dots_ref, sums_from, grad_from, pair_from, *refs):
    query_refs, rest = refs[:GRID], refs[GRID:]
    query_out, rest = rest[:GRID], rest[GRID:]
    (
        pair_out,
        sums,
        query_held,
        grad_ref,
        query_made,
        pair_held,
        sums_arrived,
        grad_arrived,
        pair_arrived,
        query_arrived,
        query_sent,
    ) = rest
    (pair_copy,) = fetch([pair_from], [pair_held], pair_arrived)
    query_copies = fetch_halves(query_refs, 0, query_held, query_arrived)
    (grad_copy,) = fetch([grad_from], [grad_ref], grad_arrived)
    (sums_copy,) = fetch([sums_from], [sums], sums_arrived)
    for copy in query_copies + [pair_copy, grad_copy]:
        copy.wait()
    for head in range(HEADS_HERE):
        columns = pl.ds(head * HDIM, HDIM)
        key_grad, value_grad, part = block_grads(
            pair_held[:, columns],
            pair_held[:, pl.ds(FEATS + head * HDIM, HDIM)],
            query_held[:, :, columns].reshape(BLOCK, HDIM),
            grad_ref[:, :, columns].reshape(BLOCK, HDIM),
            totals_ref[pl.ds(head, 1), :],
            dots_ref[pl.ds(head, 1), :],
        )
        pair_out[0, :, columns] = key_grad
        pair_out[1, :, columns] = value_grad
        if head == 0:
            sums_copy.wait()
        part = (sums[head] + part) * (math.sqrt(FRAMES * 64) * SCORE_SCALE)
        for piece in range(GRID):
            query_made[piece, :, columns] = part[
                :, piece * ROWS_HERE : (piece + 1) * ROWS_HERE
            ].T.astype(bf16)
    for send in fetch([query_made.at[piece] for piece in range(GRID)], query_out, query_sent):
        send.wait()


def half_kernel(parts_ref, kept_ref, sent_ref):
    here_z = lax.axis_index("zh")
    for out_ref, half in ((kept_ref, here_z), (sent_ref, 1 - here_z)):
        out_ref[...] = sum(parts_ref[source, half].astype(f32) for source in range(2 * GRID))


def sum_kernel(kept_ref, other_ref, *refs):
    pair_refs, query_refs = refs[:GRID], refs[GRID : 2 * GRID]
    query_out, key_out, value_out, weight_out = refs[2 * GRID :]
    weight_out[...] = kept_ref[...] + other_ref[...]
    query_out[0] = sum(ref[...].astype(f32) for ref in query_refs).astype(bf16)
    for place, out_ref in enumerate((key_out, value_out)):
        out_ref[0] = sum(ref[place].astype(f32) for ref in pair_refs).astype(bf16)


def call(kernel, out_shape, in_specs, scratch=(), out_spec=None, limit=56, flops=10**6):
    return pl.pallas_call(
        kernel,
        out_shape=out_shape,
        in_specs=in_specs,
        out_specs=out_spec or jax.tree.map(lambda _: VMEM, out_shape),
        scratch_shapes=list(scratch),
        compiler_params=pltpu.CompilerParams(vmem_limit_bytes=limit * MIB),
        cost_estimate=pl.CostEstimate(flops=flops, bytes_accessed=10**5, transcendentals=0),
    )


VMEM = pl.BlockSpec(memory_space=pltpu.VMEM)
SMEM = pl.BlockSpec(memory_space=pltpu.SMEM)
ANY = pl.BlockSpec(memory_space=pl.ANY)
HELD = [pltpu.VMEM((GRID, ROWS_HERE, FEATS), bf16)]
ARRIVED = [pltpu.SemaphoreType.DMA((GRID,))]


def shape(dims, dtype):
    return jax.ShapeDtypeStruct(dims, dtype)


def from_ahead(block, axis, step):
    return lax.ppermute(block, axis, [(i, (i - step) % GRID) for i in range(GRID)])


def to_ahead(block, axis, step):
    return lax.ppermute(block, axis, [(i, (i + step) % GRID) for i in range(GRID)])


def gather(block, axis):
    return [block] + [from_ahead(block, axis, step) for step in range(1, GRID)]


def per_device(
    vit_cot,
    vit_pre,
    ln_gain,
    patch_w,
    frame_owner,
    conv_w,
    join_w,
    token_order,
    queries,
    keys,
    values,
    attn_out,
    out_w,
):
    key_value = jnp.concatenate([keys[0], values[0]], axis=1)
    query_out = jnp.concatenate([queries[0], attn_out[0]], axis=1)
    sides = [from_ahead(key_value, "hx", step) for step in (1, 3)]
    sides += [from_ahead(query_out, "hy", step) for step in (1, 3)]
    windows = call(
        window_kernel,
        shape((FRAMES, 16, LANES), bf16),
        [VMEM] * 2 + [ANY] * 5,
        scratch=[
            pltpu.VMEM(vit_cot.shape[2:], bf16),
            pltpu.VMEM(vit_pre.shape[2:], bf16),
            pltpu.VMEM(patch_w.shape, bf16),
            pltpu.VMEM((LANES, patch_w.shape[0]), bf16),
            pltpu.VMEM((6 * LANES, LANES), bf16),
            pltpu.VMEM((SIDE * SIDE + 16, LANES), f32),
            pltpu.SemaphoreType.DMA((5,)),
        ],
    )(
        ln_gain,
        token_order,
        vit_pre[0, 0],
        vit_cot[0, 0],
        jnp.asarray(basis_matrix(), bf16),
        patch_w,
        jnp.asarray(spread_matrix(), bf16),
    )
    windows, join_w, key_value, query_out, sides = lax.optimization_barrier(
        (windows, join_w, key_value, query_out, sides)
    )
    key_values = [key_value, sides[0], from_ahead(key_value, "hx", 2), sides[1]]
    query_outs = [query_out, sides[2], from_ahead(query_out, "hy", 2), sides[3]]
    joint, picked = call(
        weights_kernel,
        (shape((QUARTERS * LANES, FEATS), bf16), shape((768, QUARTERS * LANES), bf16)),
        [ANY] * 2,
        scratch=[
            pltpu.VMEM(join_w.shape, bf16),
            pltpu.VMEM(out_w.shape, bf16),
            pltpu.SemaphoreType.DMA((2,)),
        ],
    )(join_w, out_w)
    windows, joint, picked, key_values, query_outs = lax.optimization_barrier(
        (windows, joint, picked, key_values, query_outs)
    )
    received = lax.all_to_all(
        windows, ("tm", "hx", "hy"), split_axis=0, concat_axis=0, tiled=True
    )
    totals = call(
        totals_kernel,
        shape((8, BLOCK), f32),
        [VMEM] * (2 * GRID),
        limit=24,
    )(*query_outs, *key_values)
    total_pieces = gather(totals, "hy")
    pair_shape = shape((2, ROWS_HERE, FEATS), bf16)
    exact, row_dots, sums, grad_out, weight_part, *pair_others = call(
        others_kernel,
        (
            shape((8, BLOCK), f32),
            shape((8, BLOCK), f32),
            shape((HEADS_HERE, HDIM, BLOCK), f32),
            shape((GRID, ROWS_HERE, FEATS), bf16),
            shape((768, FEATS), bf16),
            pair_shape,
            pair_shape,
            pair_shape,
        ),
        [SMEM] + [VMEM] * (1 + GRID) + [ANY] * (2 + 2 * GRID),
        scratch=[
            pltpu.VMEM((FRAMES + 2, 16, LANES), bf16),
            pltpu.VMEM((3 * LANES, QUARTERS * LANES), bf16),
            pltpu.VMEM((BLOCK, QUARTERS * LANES), bf16),
            pltpu.VMEM((FRAMES, 16, LANES), bf16),
            pltpu.VMEM((QUARTERS * LANES, FEATS), bf16),
            pltpu.VMEM((768, QUARTERS * LANES), bf16),
            pltpu.VMEM((768, FEATS), bf16),
            pltpu.VMEM((HEADS_HERE, HDIM, BLOCK), f32),
        ]
        + HELD * 5
        + [pltpu.VMEM((GRID - 1, 2, ROWS_HERE, FEATS), bf16), pltpu.SemaphoreType.DMA((3,))]
        + ARRIVED * 5
        + [pltpu.SemaphoreType.DMA((2,)), pltpu.SemaphoreType.DMA((HEADS_HERE,))],
        out_spec=(VMEM, VMEM) + (ANY,) * 6,
    )(frame_owner, conv_w, *total_pieces, received, joint, picked, *query_outs, *key_values[1:])
    *query_parts, pair_own = call(
        own_kernel,
        tuple([shape((ROWS_HERE, FEATS), bf16)] * GRID) + (pair_shape,),
        [VMEM] * 2 + [ANY] * (3 + GRID),
        scratch=[pltpu.VMEM((HEADS_HERE, HDIM, BLOCK), f32)]
        + HELD * 3
        + [pltpu.VMEM((ROWS_HERE, 2 * FEATS), bf16)]
        + [pltpu.SemaphoreType.DMA((1,))] * 3
        + ARRIVED * 2,
        out_spec=(ANY,) * GRID + (VMEM,),
        flops=10**6,
    )(exact, row_dots, sums, grad_out, key_values[0], *query_outs)
    pair_parts = [pair_own] + pair_others
    weight_parts = lax.all_to_all(
        weight_part.reshape(8, 2, 48, FEATS),
        ("core", "hx"),
        split_axis=0,
        concat_axis=0,
        tiled=True,
    )
    weight_kept, weight_sent = call(
        half_kernel,
        (shape((48, FEATS), f32), shape((48, FEATS), f32)),
        [VMEM],
        limit=8,
    )(weight_parts)
    weight_other = lax.ppermute(weight_sent, "zh", [(0, 1), (1, 0)])
    pair_back = [pair_parts[0]] + [
        to_ahead(pair_parts[step], "hx", step) for step in range(1, GRID)
    ]
    query_back = [query_parts[0]] + [
        to_ahead(query_parts[step], "hy", step) for step in range(1, GRID)
    ]

    rows = shape((1, ROWS_HERE, FEATS), bf16)
    return call(
        sum_kernel,
        (rows, rows, rows, shape((48, FEATS), f32)),
        [VMEM] * (2 + 2 * GRID),
        limit=16,
    )(weight_kept, weight_other, *pair_back, *query_back)


def solution(mesh):
    fine = Mesh(
        mesh.devices.reshape(2, 2, GRID, GRID, GRID), ("zh", "core", "tm", "hx", "hy")
    )
    dp, height = ("zh", "core"), ("hx", "hy")
    rows = P(dp, height, "tm")
    slots = P(dp, ("tm",) + height, None, None)
    placed = (
        slots,
        slots,
        P(),
        P(),
        P(),
        P(),
        P(),
        P(height, "tm"),
        rows,
        rows,
        rows,
        rows,
        P("tm", None),
    )
    return jax.shard_map(
        per_device,
        mesh=fine,
        in_specs=placed,
        out_specs=(rows, rows, rows, P(dp + height, "tm")),
        check_vma=False,
    )
```

```python
import functools
import math

import jax
import jax.numpy as jnp
import numpy as np
from jax import lax
from jax.experimental import pallas as pl
from jax.experimental.pallas import tpu as pltpu
from jax.sharding import Mesh
from jax.sharding import PartitionSpec as P

HDIM = 128
IMG = 224
PATCH = 14
SIDE = IMG // PATCH
GRID = 4
HEADS_HERE = 3
ROWS_HERE = 256
FEATS = HEADS_HERE * HDIM
BLOCK = GRID * ROWS_HERE
FRAMES = 64
LANES = 128
QUARTERS = 4
QUARTER_LANES = 32
TAPS = 27
ORDER_LANE = TAPS
QUARTER_CELLS = (PATCH // 2) * (2 * PATCH)

epsilon = 1e-05
pixel_std = (0.26862954, 0.26130258, 0.27577711)

f32 = jnp.float32
bf16 = jnp.bfloat16
MIB = 1024 * 1024
HIGHEST = lax.Precision.HIGHEST
LOG2E = math.log2(math.e)
SCORE_SCALE = HDIM ** (-0.5)


def row_masks():
    masks = np.zeros((8, PATCH), np.float32)
    for half in range(2):
        for shift in range(3):
            low = half * 7 + shift - 1
            masks[half * 3 + shift, max(low, 0) : min(low + 7, PATCH)] = 1
    masks[6, 0] = 1
    masks[7, PATCH - 1] = 1
    return masks


def basis_matrix():
    rows = row_masks()
    columns = np.zeros((3, PATCH), np.float32)
    columns[0] = 1
    columns[1, 0] = 1
    columns[2, PATCH - 1] = 1
    basis = np.zeros((LANES, 3, PATCH, PATCH), np.float32)
    for col in range(3):
        for row in range(8):
            for channel in range(3):
                basis[col * 24 + row * 3 + channel, channel] = np.outer(rows[row], columns[col])
    return basis.reshape(LANES, 3 * PATCH * PATCH)


def spread_matrix():
    spread = np.zeros((6, LANES, LANES), np.float32)
    for half in range(2):
        for side in range(2):
            first = 2 * side + 1
            terms = {
                0: [(first - 1, 2, 1), (first, 0, 1), (first + 1, 0, 1), (first + 1, 2, -1)],
                1: [(first, 0, 1), (first + 1, 0, 1)],
                2: [(first, 0, 1), (first, 1, -1), (first + 1, 0, 1), (first + 2, 1, 1)],
            }
            for shift in range(3):
                groups = [half * 3 + shift]
                if (half, shift) == (0, 0):
                    groups.append(7)
                if (half, shift) == (1, 2):
                    groups.append(6)
                for offset in range(3):
                    for channel in range(3):
                        lane = (half * 2 + side) * QUARTER_LANES + (shift * 3 + offset) * 3 + channel
                        for place, col, sign in terms[offset]:
                            for row in groups:
                                spread[place, col * 24 + row * 3 + channel, lane] += sign
    return spread.reshape(6 * LANES, LANES)


NN = (((1,), (0,)), ((), ()))
NT = (((1,), (1,)), ((), ()))
TN = (((0,), (0,)), ((), ()))


def dot(left, right, dims=NN):
    return lax.dot_general(left, right, dims, preferred_element_type=f32)


def one_hot(condition):
    return jnp.where(condition, 1.0, 0.0).astype(bf16)


def iota(dims, axis):
    return lax.broadcasted_iota(jnp.int32, dims, axis)


def start(copies):
    for copy in copies:
        copy.start()


def fetch(refs, held, arrived):
    copies = [
        pltpu.make_async_copy(ref, kept, arrived.at[place])
        for place, (ref, kept) in enumerate(zip(refs, held))
    ]
    start(copies)
    return copies


def fetch_halves(refs, column, held, arrived):
    return fetch(
        [ref.at[:, pl.ds(column * FEATS, FEATS)] for ref in refs],
        [held.at[place] for place in range(len(refs))],
        arrived,
    )


def window_kernel(gain_ref, order_ref, *refs):
    out_ref, cot_ref, pre_ref, patch_ref, basis_ref, spread_ref, sums, arrived = refs[5:]
    held = (pre_ref, cot_ref, basis_ref, patch_ref, spread_ref)
    copies = fetch(refs[:5], held, arrived)
    copies[0].wait()
    copies[1].wait()
    pre = pre_ref[...].astype(f32)
    centered = pre - jnp.mean(pre, axis=-1, keepdims=True)
    inverse = lax.rsqrt(jnp.mean(centered * centered, axis=-1, keepdims=True) + epsilon)
    normed = centered * inverse
    scaled = cot_ref[...].astype(f32) * gain_ref[...].astype(f32).reshape(1, -1)
    grad_rows = inverse * (
        scaled
        - jnp.mean(scaled, axis=-1, keepdims=True)
        - normed * jnp.mean(scaled * normed, axis=-1, keepdims=True)
    )
    grad_rows = grad_rows.astype(bf16)
    channel = iota((LANES, 1), 0) % 3
    scale = jnp.where(
        channel == 0, 1.0 / pixel_std[0], jnp.where(channel == 1, 1.0 / pixel_std[1], 1.0 / pixel_std[2])
    ) * (1.0 / QUARTER_CELLS)
    copies[2].wait()
    copies[3].wait()
    weights = dot(basis_ref[...], patch_ref[...]) * scale
    high = weights.astype(bf16)
    low = (weights - high.astype(f32)).astype(bf16)
    both = dot(grad_rows, jnp.concatenate([high, low], axis=0), NT)
    patch_sums = both[:, :LANES] + both[:, LANES:]
    group = (iota((SIDE * SIDE, LANES), 1) // 3) % 8
    edge = jnp.zeros((SIDE, LANES), f32)
    above = jnp.concatenate([edge, patch_sums[:-SIDE]], axis=0)
    below = jnp.concatenate([patch_sums[SIDE:], edge], axis=0)
    patch_sums = jnp.where(group == 7, above, jnp.where(group == 6, below, patch_sums))
    sums[pl.ds(0, 8), :] = jnp.zeros((8, LANES), f32)
    sums[pl.ds(8 + SIDE * SIDE, 8), :] = jnp.zeros((8, LANES), f32)
    sums[pl.ds(8, SIDE * SIDE), :] = patch_sums
    copies[4].wait()
    column = iota((SIDE * GRID, LANES), 0) % GRID
    total = jnp.zeros((SIDE * GRID, LANES), f32)
    for place in range(6):
        picked = sums[pl.ds(7 + place, SIDE * GRID, stride=GRID), :]
        if place == 0:
            picked = jnp.where(column == 0, 0.0, picked)
        if place == 5:
            picked = jnp.where(column == GRID - 1, 0.0, picked)
        high = picked.astype(bf16)
        low = (picked - high.astype(f32)).astype(bf16)
        both = dot(
            jnp.concatenate([high, low], axis=0), spread_ref[pl.ds(place * LANES, LANES), :]
        )
        total = total + (both[: SIDE * GRID] + both[SIDE * GRID :])
    windows = total.astype(bf16)
    entries = jnp.where(
        iota((16, 64), 1) % 16 == iota((16, 64), 0), order_ref[...].astype(f32), 0.0
    ).astype(bf16)
    order = dot(entries, one_hot(iota((64, LANES), 1) == ORDER_LANE + iota((64, LANES), 0) // 16))
    order = order.astype(bf16)
    for target_x in range(GRID):
        block = windows[target_x * 16 : (target_x + 1) * 16] + order
        for target_t in range(GRID):
            for target_y in range(GRID):
                out_ref[(target_t * GRID + target_x) * GRID + target_y] = block


def weights_kernel(join_from, out_w_from, joint_ref, picked_ref, join_ref, out_w_ref, arrived):
    here_y = lax.axis_index("hy")
    copies = fetch([join_from, out_w_from], [join_ref, out_w_ref], arrived)
    copies[0].wait()
    copies[1].wait()
    joint_ref[...] = dot(join_ref[...], out_w_ref[...], NT).astype(bf16)
    row, column = iota((96, 384), 0), iota((96, 384), 1)
    half = row // 48
    pick = one_hot(column == half * 192 + here_y * 48 + (row - half * 48))
    for pair in range(8):
        rows = dot(pick, join_ref[:, pl.ds(pair * 384, 384)], NT).astype(bf16)
        z, core, x = pair // 4, (pair % 4) // 2, (pair % 2) * 2
        for step in range(2):
            picked_ref[pl.ds((z * 2 + core) * 192 + (x + step) * 48, 48), :] = rows[
                step * 48 : (step + 1) * 48
            ]


def totals_kernel(*refs):
    query_refs, key_refs, out_ref = refs[:GRID], refs[GRID : 2 * GRID], refs[2 * GRID]
    for head in range(HEADS_HERE):
        columns = pl.ds(head * HDIM, HDIM)
        for piece in range(GRID):
            query = query_refs[piece][:, columns]
            scores = [dot(key_ref[:, columns], query, NT) for key_ref in key_refs]
            top = functools.reduce(
                jnp.maximum, [jnp.max(tile, axis=0, keepdims=True) for tile in scores]
            ) * (SCORE_SCALE * LOG2E)
            total = sum(
                jnp.sum(jnp.exp2(tile * (SCORE_SCALE * LOG2E) - top), axis=0, keepdims=True)
                for tile in scores
            )
            out_ref[pl.ds(head, 1), pl.ds(piece * ROWS_HERE, ROWS_HERE)] = top + jnp.log2(total)
    out_ref[pl.ds(HEADS_HERE, 8 - HEADS_HERE), :] = jnp.zeros((8 - HEADS_HERE, BLOCK), f32)


def token_part(owner_ref, conv_ref, recv_ref, arrivals, frames, conv_big, ordered):
    here_x = lax.axis_index("hx")
    here_y = lax.axis_index("hy")
    frames[0] = jnp.zeros((16, LANES), bf16)
    frames[FRAMES + 1] = jnp.zeros((16, LANES), bf16)
    row, column = iota((3 * QUARTER_LANES, 3 * TAPS), 0), iota((3 * QUARTER_LANES, 3 * TAPS), 1)
    tap = row % QUARTER_LANES
    conv = dot(
        one_hot((tap < TAPS) & (column == (row // QUARTER_LANES) * TAPS + tap)), conv_ref[...]
    ).astype(bf16)
    conv_big[...] = jnp.zeros_like(conv_big)
    for quarter in range(QUARTERS):
        for shift in range(3):
            conv_big[
                pl.ds(shift * LANES + quarter * QUARTER_LANES, QUARTER_LANES),
                pl.ds(quarter * LANES, LANES),
            ] = conv[shift * QUARTER_LANES : (shift + 1) * QUARTER_LANES]
    arrivals.wait()

    def place_frame(frame, carry):
        frames[frame + 1] = recv_ref[(frame // 16) * 16 + owner_ref[frame]]
        return carry

    lax.fori_loop(0, FRAMES, place_frame, 0, unroll=8)
    lane = iota((16, ROWS_HERE), 1)
    for slab_t in range(GRID):
        pooled = sum(
            dot(
                frames[pl.ds(slab_t * 16 + shift, 16)].reshape(ROWS_HERE, LANES),
                conv_big[pl.ds(shift * LANES, LANES), :],
            )
            for shift in range(3)
        ).astype(bf16)
        pieces = []
        for piece in range(GRID):
            slab = lax.rem(here_y + piece, GRID)
            block = recv_ref[slab_t * 16 + here_x * GRID + slab].astype(f32)
            for part in range(4):
                order = block[:, ORDER_LANE + part : ORDER_LANE + part + 1].astype(jnp.int32)
                target = (order // 4) * 16 + slab * 4 + lax.rem(order, 4)
                pieces.append(one_hot(lane == target))
        chosen = dot(jnp.concatenate(pieces, axis=0), pooled).astype(bf16)
        for piece in range(GRID):
            ordered[pl.ds(piece * ROWS_HERE + slab_t * 64, 64), :] = chosen[
                piece * 64 : (piece + 1) * 64
            ]


def grads_kernel(owner_ref, conv_ref, *refs):
    total_refs, (recv_from, joint_from, picked_from) = refs[:GRID], refs[GRID : GRID + 3]
    query_refs, pair_refs = refs[GRID + 3 : 2 * GRID + 3], refs[2 * GRID + 3 : 3 * GRID + 3]
    rest = refs[3 * GRID + 3 :]
    query_out, pair_out, weight_out = rest[:GRID], rest[GRID : 2 * GRID], rest[2 * GRID]
    (
        frames,
        conv_big,
        ordered,
        recv_ref,
        joint_ref,
        picked_ref,
        weight_made,
        dots_ref,
        sums,
        out_held,
        query_held,
        key_held,
        value_held,
        grad_ref,
        query_made,
        pair_made,
        first_arrived,
        out_arrived,
        query_arrived,
        key_arrived,
        value_arrived,
        query_sent,
        pair_sent,
        weight_sent,
    ) = rest[2 * GRID + 1 :]
    sends_order = (2, 1, 3, 0)
    firsts = fetch(
        [recv_from, joint_from, picked_from], [recv_ref, joint_ref, picked_ref], first_arrived
    )
    out_copies = fetch_halves(query_refs, 1, out_held, out_arrived)
    query_copies = fetch_halves(query_refs, 0, query_held, query_arrived)
    key_copies = fetch_halves(pair_refs, 0, key_held, key_arrived)
    value_copies = fetch_halves(pair_refs, 1, value_held, value_arrived)
    token_part(owner_ref, conv_ref, recv_ref, firsts[0], frames, conv_big, ordered)
    firsts[1].wait()
    ones = jnp.ones((8, 2 * HDIM), bf16)
    outer = jnp.zeros((QUARTERS * LANES, FEATS), f32)
    for piece in range(GRID):
        rows = ordered[pl.ds(piece * ROWS_HERE, ROWS_HERE), :]
        grads = dot(rows, joint_ref[...]).astype(bf16)
        grad_ref[piece] = grads
        out_copies[piece].wait()
        outs = out_held[piece]
        products = grads.astype(f32) * outs.astype(f32)
        high = products.astype(bf16)
        low = (products - high.astype(f32)).astype(bf16)
        for head in range(HEADS_HERE):
            columns = slice(head * HDIM, (head + 1) * HDIM)
            both = jnp.concatenate([high[:, columns], low[:, columns]], axis=1)
            dots_ref[head, :, pl.ds(piece * ROWS_HERE, ROWS_HERE)] = dot(ones, both, NT)
        outer = outer + dot(rows, outs, TN)
    firsts[2].wait()
    weight_made[...] = (
        dot(picked_ref[...], outer.astype(bf16)) * (1.0 / math.sqrt(FRAMES * 64 * 4))
    ).astype(bf16)
    sends = fetch([weight_made], [weight_out], weight_sent)
    root = math.sqrt(FRAMES * 64)
    totals = []
    for piece in range(GRID):
        parts = [
            total_refs[step][:, pl.ds(((piece - step) % GRID) * ROWS_HERE, ROWS_HERE)]
            for step in range(GRID)
        ]
        top = functools.reduce(jnp.maximum, parts)
        totals.append(top + jnp.log2(sum(jnp.exp2(part - top) for part in parts)))
    totals = jnp.concatenate(totals, axis=1)
    for copy in query_copies:
        copy.wait()
    for other in sends_order:
        key_copies[other].wait()
        value_copies[other].wait()
        for head in range(HEADS_HERE):
            columns = pl.ds(head * HDIM, HDIM)
            query = query_held[:, :, columns].reshape(BLOCK, HDIM)
            grad = grad_ref[:, :, columns].reshape(BLOCK, HDIM)
            key = key_held[other, :, columns]
            value = value_held[other, :, columns]
            weights = jnp.exp2(
                dot(key, query, NT) * (SCORE_SCALE * LOG2E) - totals[head : head + 1]
            )
            dscore = (weights * (dot(value, grad, NT) - dots_ref[head, 0:1, :])).astype(bf16)
            pair_made[other, 1, :, columns] = (dot(weights.astype(bf16), grad) * root).astype(bf16)
            pair_made[other, 0, :, columns] = (
                dot(dscore, query) * (root * SCORE_SCALE)
            ).astype(bf16)
            part = dot(key.T, dscore)
            if other == sends_order[0]:
                sums[head] = part
            else:
                sums[head] += part
        send = pltpu.make_async_copy(pair_made.at[other], pair_out[other], pair_sent.at[other])
        send.start()
        sends.append(send)
    for piece in sends_order:
        for head in range(HEADS_HERE):
            query_made[piece, :, pl.ds(head * HDIM, HDIM)] = (
                sums[head, :, pl.ds(piece * ROWS_HERE, ROWS_HERE)].T * (root * SCORE_SCALE)
            ).astype(bf16)
        send = pltpu.make_async_copy(query_made.at[piece], query_out[piece], query_sent.at[piece])
        send.start()
        sends.append(send)
    for send in sends:
        send.wait()


def weight_kernel(parts_ref, out_ref):
    out_ref[...] = sum(parts_ref[source].astype(f32) for source in range(4)).astype(bf16)


def sum_kernel(parts_ref, *refs):
    pair_refs, query_refs = refs[:GRID], refs[GRID : 2 * GRID]
    query_out, key_out, value_out, weight_out = refs[2 * GRID :]
    weight_out[...] = sum(parts_ref[source].astype(f32) for source in range(GRID))
    query_out[0] = sum(ref[...].astype(f32) for ref in query_refs).astype(bf16)
    for place, out_ref in enumerate((key_out, value_out)):
        out_ref[0] = sum(ref[place].astype(f32) for ref in pair_refs).astype(bf16)


def call(kernel, out_shape, in_specs, scratch=(), out_spec=None, limit=56):
    return pl.pallas_call(
        kernel,
        out_shape=out_shape,
        in_specs=in_specs,
        out_specs=jax.tree.map(lambda _: out_spec or VMEM, out_shape),
        scratch_shapes=list(scratch),
        compiler_params=pltpu.CompilerParams(vmem_limit_bytes=limit * MIB),
        cost_estimate=pl.CostEstimate(flops=10**6, bytes_accessed=10**5, transcendentals=0),
    )


VMEM = pl.BlockSpec(memory_space=pltpu.VMEM)
SMEM = pl.BlockSpec(memory_space=pltpu.SMEM)
ANY = pl.BlockSpec(memory_space=pl.ANY)
HELD = [pltpu.VMEM((GRID, ROWS_HERE, FEATS), bf16)]
ARRIVED = [pltpu.SemaphoreType.DMA((GRID,))]


def shape(dims, dtype):
    return jax.ShapeDtypeStruct(dims, dtype)


def from_ahead(block, axis, step):
    return lax.ppermute(block, axis, [(i, (i - step) % GRID) for i in range(GRID)])


def to_ahead(block, axis, step):
    return lax.ppermute(block, axis, [(i, (i + step) % GRID) for i in range(GRID)])


def gather(block, axis):
    return [block] + [from_ahead(block, axis, step) for step in range(1, GRID)]


def per_device(
    vit_cot,
    vit_pre,
    ln_gain,
    patch_w,
    frame_owner,
    conv_w,
    join_w,
    token_order,
    queries,
    keys,
    values,
    attn_out,
    out_w,
):
    key_value = jnp.concatenate([keys[0], values[0]], axis=1)
    query_out = jnp.concatenate([queries[0], attn_out[0]], axis=1)
    sides = [from_ahead(key_value, "hx", step) for step in (1, 3)]
    sides += [from_ahead(query_out, "hy", step) for step in (1, 3)]
    windows = call(
        window_kernel,
        shape((FRAMES, 16, LANES), bf16),
        [VMEM] * 2 + [ANY] * 5,
        scratch=[
            pltpu.VMEM(vit_cot.shape[2:], bf16),
            pltpu.VMEM(vit_pre.shape[2:], bf16),
            pltpu.VMEM(patch_w.shape, bf16),
            pltpu.VMEM((LANES, patch_w.shape[0]), bf16),
            pltpu.VMEM((6 * LANES, LANES), bf16),
            pltpu.VMEM((SIDE * SIDE + 16, LANES), f32),
            pltpu.SemaphoreType.DMA((5,)),
        ],
    )(
        ln_gain,
        token_order,
        vit_pre[0, 0],
        vit_cot[0, 0],
        jnp.asarray(basis_matrix(), bf16),
        patch_w,
        jnp.asarray(spread_matrix(), bf16),
    )
    windows, join_w, key_value, query_out, sides = lax.optimization_barrier(
        (windows, join_w, key_value, query_out, sides)
    )
    key_values = [key_value, sides[0], from_ahead(key_value, "hx", 2), sides[1]]
    query_outs = [query_out, sides[2], from_ahead(query_out, "hy", 2), sides[3]]
    joint, picked = call(
        weights_kernel,
        (shape((QUARTERS * LANES, FEATS), bf16), shape((768, QUARTERS * LANES), bf16)),
        [ANY] * 2,
        scratch=[
            pltpu.VMEM(join_w.shape, bf16),
            pltpu.VMEM(out_w.shape, bf16),
            pltpu.SemaphoreType.DMA((2,)),
        ],
    )(join_w, out_w)
    windows, joint, picked, key_values, query_outs = lax.optimization_barrier(
        (windows, joint, picked, key_values, query_outs)
    )
    received = lax.all_to_all(
        windows, ("tm", "hx", "hy"), split_axis=0, concat_axis=0, tiled=True
    )
    totals = call(
        totals_kernel,
        shape((8, BLOCK), f32),
        [VMEM] * (2 * GRID),
        limit=24,
    )(*query_outs, *key_values)
    total_pieces = gather(totals, "hy")
    outs = call(
        grads_kernel,
        tuple([shape((ROWS_HERE, FEATS), bf16)] * GRID)
        + tuple([shape((2, ROWS_HERE, FEATS), bf16)] * GRID)
        + (shape((768, FEATS), bf16),),
        [SMEM] + [VMEM] * (1 + GRID) + [ANY] * (3 + 2 * GRID),
        scratch=[
            pltpu.VMEM((FRAMES + 2, 16, LANES), bf16),
            pltpu.VMEM((3 * LANES, QUARTERS * LANES), bf16),
            pltpu.VMEM((BLOCK, QUARTERS * LANES), bf16),
            pltpu.VMEM((FRAMES, 16, LANES), bf16),
            pltpu.VMEM((QUARTERS * LANES, FEATS), bf16),
            pltpu.VMEM((768, QUARTERS * LANES), bf16),
            pltpu.VMEM((768, FEATS), bf16),
            pltpu.VMEM((HEADS_HERE, 8, BLOCK), f32),
            pltpu.VMEM((HEADS_HERE, HDIM, BLOCK), f32),
        ]
        + HELD * 6
        + [pltpu.VMEM((GRID, 2, ROWS_HERE, FEATS), bf16), pltpu.SemaphoreType.DMA((3,))]
        + ARRIVED * 6
        + [pltpu.SemaphoreType.DMA((1,))],
        out_spec=ANY,
        limit=56,
    )(frame_owner, conv_w, *total_pieces, received, joint, picked, *query_outs, *key_values)
    query_parts, pair_parts, weight_part = outs[:GRID], outs[GRID : 2 * GRID], outs[2 * GRID]
    weight_parts = lax.all_to_all(
        weight_part.reshape(4, 4 * 48, FEATS),
        ("zh", "core"),
        split_axis=0,
        concat_axis=0,
        tiled=True,
    )
    weight_blocks = call(weight_kernel, shape((4 * 48, FEATS), bf16), [VMEM], limit=8)(weight_parts)
    weight_parts = lax.all_to_all(
        weight_blocks.reshape(4, 48, FEATS), "hx", split_axis=0, concat_axis=0, tiled=True
    )
    pair_back = [pair_parts[0]] + [
        to_ahead(pair_parts[step], "hx", step) for step in range(1, GRID)
    ]
    query_back = [query_parts[0]] + [
        to_ahead(query_parts[step], "hy", step) for step in range(1, GRID)
    ]

    rows = shape((1, ROWS_HERE, FEATS), bf16)
    return call(
        sum_kernel,
        (rows, rows, rows, shape((48, FEATS), f32)),
        [VMEM] * (1 + 2 * GRID),
        limit=16,
    )(weight_parts, *pair_back, *query_back)


def solution(mesh):
    fine = Mesh(
        mesh.devices.reshape(2, 2, GRID, GRID, GRID), ("zh", "core", "tm", "hx", "hy")
    )
    dp, height = ("zh", "core"), ("hx", "hy")
    rows = P(dp, height, "tm")
    slots = P(dp, ("tm",) + height, None, None)
    placed = (
        slots,
        slots,
        P(),
        P(),
        P(),
        P(),
        P(),
        P(height, "tm"),
        rows,
        rows,
        rows,
        rows,
        P("tm", None),
    )
    return jax.shard_map(
        per_device,
        mesh=fine,
        in_specs=placed,
        out_specs=(rows, rows, rows, P(dp + height, "tm")),
        check_vma=False,
    )
```

```python
import functools
import math

import jax
import jax.numpy as jnp
import numpy as np
from jax import lax
from jax.experimental import pallas as pl
from jax.experimental.pallas import tpu as pltpu
from jax.sharding import Mesh
from jax.sharding import PartitionSpec as P

HDIM = 128
IMG = 224
PATCH = 14
SIDE = IMG // PATCH
GRID = 4
HEADS_HERE = 3
ROWS_HERE = 256
FEATS = HEADS_HERE * HDIM
BLOCK = GRID * ROWS_HERE
FRAMES = 64
LANES = 128
QUARTERS = 4
QUARTER_LANES = 32
TAPS = 27
ORDER_LANE = TAPS
QUARTER_CELLS = (PATCH // 2) * (2 * PATCH)

epsilon = 1e-05
pixel_std = (0.26862954, 0.26130258, 0.27577711)

f32 = jnp.float32
bf16 = jnp.bfloat16
MIB = 1024 * 1024
HIGHEST = lax.Precision.HIGHEST
LOG2E = math.log2(math.e)
SCORE_SCALE = HDIM ** (-0.5)


def row_masks():
    masks = np.zeros((8, PATCH), np.float32)
    for half in range(2):
        for shift in range(3):
            low = half * 7 + shift - 1
            masks[half * 3 + shift, max(low, 0) : min(low + 7, PATCH)] = 1
    masks[6, 0] = 1
    masks[7, PATCH - 1] = 1
    return masks


def basis_matrix():
    rows = row_masks()
    columns = np.zeros((3, PATCH), np.float32)
    columns[0] = 1
    columns[1, 0] = 1
    columns[2, PATCH - 1] = 1
    basis = np.zeros((LANES, 3, PATCH, PATCH), np.float32)
    for col in range(3):
        for row in range(8):
            for channel in range(3):
                basis[col * 24 + row * 3 + channel, channel] = np.outer(rows[row], columns[col])
    return basis.reshape(LANES, 3 * PATCH * PATCH)


def spread_matrix():
    spread = np.zeros((6, LANES, LANES), np.float32)
    for half in range(2):
        for side in range(2):
            first = 2 * side + 1
            terms = {
                0: [(first - 1, 2, 1), (first, 0, 1), (first + 1, 0, 1), (first + 1, 2, -1)],
                1: [(first, 0, 1), (first + 1, 0, 1)],
                2: [(first, 0, 1), (first, 1, -1), (first + 1, 0, 1), (first + 2, 1, 1)],
            }
            for shift in range(3):
                groups = [half * 3 + shift]
                if (half, shift) == (0, 0):
                    groups.append(7)
                if (half, shift) == (1, 2):
                    groups.append(6)
                for offset in range(3):
                    for channel in range(3):
                        lane = (half * 2 + side) * QUARTER_LANES + (shift * 3 + offset) * 3 + channel
                        for place, col, sign in terms[offset]:
                            for row in groups:
                                spread[place, col * 24 + row * 3 + channel, lane] += sign
    return spread.reshape(6 * LANES, LANES)


NN = (((1,), (0,)), ((), ()))
NT = (((1,), (1,)), ((), ()))
TN = (((0,), (0,)), ((), ()))


def dot(left, right, dims=NN):
    return lax.dot_general(left, right, dims, preferred_element_type=f32)


def one_hot(condition):
    return jnp.where(condition, 1.0, 0.0).astype(bf16)


def iota(dims, axis):
    return lax.broadcasted_iota(jnp.int32, dims, axis)


def start(copies):
    for copy in copies:
        copy.start()


def fetch(refs, held, arrived):
    copies = [
        pltpu.make_async_copy(ref, kept, arrived.at[place])
        for place, (ref, kept) in enumerate(zip(refs, held))
    ]
    start(copies)
    return copies


def fetch_halves(refs, column, held, arrived):
    return fetch(
        [ref.at[:, pl.ds(column * FEATS, FEATS)] for ref in refs],
        [held.at[place] for place in range(len(refs))],
        arrived,
    )


def window_kernel(gain_ref, order_ref, *refs):
    out_ref, cot_ref, pre_ref, patch_ref, basis_ref, spread_ref, sums, arrived = refs[5:]
    held = (pre_ref, cot_ref, basis_ref, patch_ref, spread_ref)
    copies = fetch(refs[:5], held, arrived)
    copies[0].wait()
    copies[1].wait()
    pre = pre_ref[...].astype(f32)
    centered = pre - jnp.mean(pre, axis=-1, keepdims=True)
    inverse = lax.rsqrt(jnp.mean(centered * centered, axis=-1, keepdims=True) + epsilon)
    normed = centered * inverse
    scaled = cot_ref[...].astype(f32) * gain_ref[...].astype(f32).reshape(1, -1)
    grad_rows = inverse * (
        scaled
        - jnp.mean(scaled, axis=-1, keepdims=True)
        - normed * jnp.mean(scaled * normed, axis=-1, keepdims=True)
    )
    grad_rows = grad_rows.astype(bf16)
    channel = iota((LANES, 1), 0) % 3
    scale = jnp.where(
        channel == 0, 1.0 / pixel_std[0], jnp.where(channel == 1, 1.0 / pixel_std[1], 1.0 / pixel_std[2])
    ) * (1.0 / QUARTER_CELLS)
    copies[2].wait()
    copies[3].wait()
    weights = dot(basis_ref[...], patch_ref[...]) * scale
    high = weights.astype(bf16)
    low = (weights - high.astype(f32)).astype(bf16)
    both = dot(grad_rows, jnp.concatenate([high, low], axis=0), NT)
    patch_sums = both[:, :LANES] + both[:, LANES:]
    group = (iota((SIDE * SIDE, LANES), 1) // 3) % 8
    edge = jnp.zeros((SIDE, LANES), f32)
    above = jnp.concatenate([edge, patch_sums[:-SIDE]], axis=0)
    below = jnp.concatenate([patch_sums[SIDE:], edge], axis=0)
    patch_sums = jnp.where(group == 7, above, jnp.where(group == 6, below, patch_sums))
    sums[pl.ds(0, 8), :] = jnp.zeros((8, LANES), f32)
    sums[pl.ds(8 + SIDE * SIDE, 8), :] = jnp.zeros((8, LANES), f32)
    sums[pl.ds(8, SIDE * SIDE), :] = patch_sums
    copies[4].wait()
    column = iota((SIDE * GRID, LANES), 0) % GRID
    total = jnp.zeros((SIDE * GRID, LANES), f32)
    for place in range(6):
        picked = sums[pl.ds(7 + place, SIDE * GRID, stride=GRID), :]
        if place == 0:
            picked = jnp.where(column == 0, 0.0, picked)
        if place == 5:
            picked = jnp.where(column == GRID - 1, 0.0, picked)
        high = picked.astype(bf16)
        low = (picked - high.astype(f32)).astype(bf16)
        both = dot(
            jnp.concatenate([high, low], axis=0), spread_ref[pl.ds(place * LANES, LANES), :]
        )
        total = total + (both[: SIDE * GRID] + both[SIDE * GRID :])
    windows = total.astype(bf16)
    entries = jnp.where(
        iota((16, 64), 1) % 16 == iota((16, 64), 0), order_ref[...].astype(f32), 0.0
    ).astype(bf16)
    order = dot(entries, one_hot(iota((64, LANES), 1) == ORDER_LANE + iota((64, LANES), 0) // 16))
    order = order.astype(bf16)
    for target_x in range(GRID):
        block = windows[target_x * 16 : (target_x + 1) * 16] + order
        for target_t in range(GRID):
            for target_y in range(GRID):
                out_ref[(target_t * GRID + target_x) * GRID + target_y] = block


def weights_kernel(join_from, out_w_from, joint_ref, picked_ref, join_ref, out_w_ref, arrived):
    here_y = lax.axis_index("hy")
    copies = fetch([join_from, out_w_from], [join_ref, out_w_ref], arrived)
    copies[0].wait()
    copies[1].wait()
    joint_ref[...] = dot(join_ref[...], out_w_ref[...], NT).astype(bf16)
    row, column = iota((96, 384), 0), iota((96, 384), 1)
    half = row // 48
    pick = one_hot(column == half * 192 + here_y * 48 + (row - half * 48))
    for pair in range(8):
        rows = dot(pick, join_ref[:, pl.ds(pair * 384, 384)], NT).astype(bf16)
        z, core, x = pair // 4, (pair % 4) // 2, (pair % 2) * 2
        for step in range(2):
            picked_ref[pl.ds((z * 2 + core) * 192 + (x + step) * 48, 48), :] = rows[
                step * 48 : (step + 1) * 48
            ]


def totals_kernel(*refs):
    query_refs, key_refs, out_ref = refs[:GRID], refs[GRID : 2 * GRID], refs[2 * GRID]
    for head in range(HEADS_HERE):
        columns = pl.ds(head * HDIM, HDIM)
        for piece in range(GRID):
            query = query_refs[piece][:, columns]
            scores = [dot(key_ref[:, columns], query, NT) for key_ref in key_refs]
            top = functools.reduce(
                jnp.maximum, [jnp.max(tile, axis=0, keepdims=True) for tile in scores]
            ) * (SCORE_SCALE * LOG2E)
            total = sum(
                jnp.sum(jnp.exp2(tile * (SCORE_SCALE * LOG2E) - top), axis=0, keepdims=True)
                for tile in scores
            )
            out_ref[pl.ds(head, 1), pl.ds(piece * ROWS_HERE, ROWS_HERE)] = top + jnp.log2(total)
    out_ref[pl.ds(HEADS_HERE, 8 - HEADS_HERE), :] = jnp.zeros((8 - HEADS_HERE, BLOCK), f32)


def token_part(owner_ref, conv_ref, recv_ref, arrivals, frames, conv_big, ordered):
    here_x = lax.axis_index("hx")
    here_y = lax.axis_index("hy")
    frames[0] = jnp.zeros((16, LANES), bf16)
    frames[FRAMES + 1] = jnp.zeros((16, LANES), bf16)
    row, column = iota((3 * QUARTER_LANES, 3 * TAPS), 0), iota((3 * QUARTER_LANES, 3 * TAPS), 1)
    tap = row % QUARTER_LANES
    conv = dot(
        one_hot((tap < TAPS) & (column == (row // QUARTER_LANES) * TAPS + tap)), conv_ref[...]
    ).astype(bf16)
    conv_big[...] = jnp.zeros_like(conv_big)
    for quarter in range(QUARTERS):
        for shift in range(3):
            conv_big[
                pl.ds(shift * LANES + quarter * QUARTER_LANES, QUARTER_LANES),
                pl.ds(quarter * LANES, LANES),
            ] = conv[shift * QUARTER_LANES : (shift + 1) * QUARTER_LANES]
    arrivals.wait()

    def place_frame(frame, carry):
        frames[frame + 1] = recv_ref[(frame // 16) * 16 + owner_ref[frame]]
        return carry

    lax.fori_loop(0, FRAMES, place_frame, 0, unroll=8)
    lane = iota((16, ROWS_HERE), 1)
    for slab_t in range(GRID):
        pooled = sum(
            dot(
                frames[pl.ds(slab_t * 16 + shift, 16)].reshape(ROWS_HERE, LANES),
                conv_big[pl.ds(shift * LANES, LANES), :],
            )
            for shift in range(3)
        ).astype(bf16)
        pieces = []
        for piece in range(GRID):
            slab = lax.rem(here_y + piece, GRID)
            block = recv_ref[slab_t * 16 + here_x * GRID + slab].astype(f32)
            for part in range(4):
                order = block[:, ORDER_LANE + part : ORDER_LANE + part + 1].astype(jnp.int32)
                target = (order // 4) * 16 + slab * 4 + lax.rem(order, 4)
                pieces.append(one_hot(lane == target))
        chosen = dot(jnp.concatenate(pieces, axis=0), pooled).astype(bf16)
        for piece in range(GRID):
            ordered[pl.ds(piece * ROWS_HERE + slab_t * 64, 64), :] = chosen[
                piece * 64 : (piece + 1) * 64
            ]


def token_kernel(owner_ref, conv_ref, *refs):
    recv_from, joint_from, picked_from = refs[:3]
    (
        dots_ref,
        grad_out,
        weight_out,
        frames,
        conv_big,
        ordered,
        recv_ref,
        joint_ref,
        picked_ref,
        weight_made,
        out_held,
        grad_made,
        first_arrived,
        out_arrived,
        grad_sent,
        weight_sent,
    ) = refs[GRID + 3 :]
    firsts = fetch(
        [recv_from, joint_from, picked_from], [recv_ref, joint_ref, picked_ref], first_arrived
    )
    out_copies = fetch_halves(refs[3 : GRID + 3], 1, out_held, out_arrived)
    token_part(owner_ref, conv_ref, recv_ref, firsts[0], frames, conv_big, ordered)
    firsts[1].wait()
    ones = jnp.ones((8, 2 * HDIM), bf16)
    sends = []
    dots_ref[...] = jnp.zeros_like(dots_ref)
    outer = jnp.zeros((QUARTERS * LANES, FEATS), f32)
    for piece in range(GRID):
        rows = ordered[pl.ds(piece * ROWS_HERE, ROWS_HERE), :]
        grads = dot(rows, joint_ref[...]).astype(bf16)
        grad_made[piece] = grads
        sends += fetch([grad_made.at[piece]], [grad_out.at[piece]], grad_sent.at[pl.ds(piece, 1)])
        out_copies[piece].wait()
        outs = out_held[piece]
        products = grads.astype(f32) * outs.astype(f32)
        high = products.astype(bf16)
        low = (products - high.astype(f32)).astype(bf16)
        for head in range(HEADS_HERE):
            columns = slice(head * HDIM, (head + 1) * HDIM)
            both = jnp.concatenate([high[:, columns], low[:, columns]], axis=1)
            dots_ref[pl.ds(head, 1), pl.ds(piece * ROWS_HERE, ROWS_HERE)] = dot(ones, both, NT)[
                0:1
            ]
        outer = outer + dot(rows, outs, TN)
    firsts[2].wait()
    weight_made[...] = (
        dot(picked_ref[...], outer.astype(bf16)) * (1.0 / math.sqrt(FRAMES * 64 * 4))
    ).astype(bf16)
    sends += fetch([weight_made], [weight_out], weight_sent)
    for send in sends:
        send.wait()


def grads_kernel(dots_ref, *refs):
    total_refs, grad_from = refs[:GRID], refs[GRID]
    query_refs, pair_refs = refs[GRID + 1 : 2 * GRID + 1], refs[2 * GRID + 1 : 3 * GRID + 1]
    rest = refs[3 * GRID + 1 :]
    query_out, pair_out = rest[:GRID], rest[GRID : 2 * GRID]
    (
        sums,
        query_held,
        key_held,
        value_held,
        grad_ref,
        query_made,
        pair_made,
        query_arrived,
        key_arrived,
        value_arrived,
        grad_arrived,
        query_sent,
        pair_sent,
    ) = rest[2 * GRID :]
    sends_order = (2, 1, 3, 0)
    query_copies = fetch_halves(query_refs, 0, query_held, query_arrived)
    query_copies += fetch([grad_from], [grad_ref], grad_arrived)
    key_copies = fetch_halves(pair_refs, 0, key_held, key_arrived)
    value_copies = fetch_halves(pair_refs, 1, value_held, value_arrived)
    root = math.sqrt(FRAMES * 64)
    totals = []
    for piece in range(GRID):
        parts = [
            total_refs[step][:, pl.ds(((piece - step) % GRID) * ROWS_HERE, ROWS_HERE)]
            for step in range(GRID)
        ]
        top = functools.reduce(jnp.maximum, parts)
        totals.append(top + jnp.log2(sum(jnp.exp2(part - top) for part in parts)))
    totals = jnp.concatenate(totals, axis=1)
    for copy in query_copies:
        copy.wait()
    sends = []
    for other in sends_order:
        key_copies[other].wait()
        value_copies[other].wait()
        for head in range(HEADS_HERE):
            columns = pl.ds(head * HDIM, HDIM)
            query = query_held[:, :, columns].reshape(BLOCK, HDIM)
            grad = grad_ref[:, :, columns].reshape(BLOCK, HDIM)
            key = key_held[other, :, columns]
            value = value_held[other, :, columns]
            weights = jnp.exp2(
                dot(key, query, NT) * (SCORE_SCALE * LOG2E) - totals[head : head + 1]
            )
            dscore = (weights * (dot(value, grad, NT) - dots_ref[pl.ds(head, 1), :])).astype(bf16)
            pair_made[other, 1, :, columns] = (dot(weights.astype(bf16), grad) * root).astype(bf16)
            pair_made[other, 0, :, columns] = (
                dot(dscore, query) * (root * SCORE_SCALE)
            ).astype(bf16)
            part = dot(key.T, dscore)
            if other == sends_order[0]:
                sums[head] = part
            else:
                sums[head] += part
        send = pltpu.make_async_copy(pair_made.at[other], pair_out[other], pair_sent.at[other])
        send.start()
        sends.append(send)
    for piece in sends_order:
        for head in range(HEADS_HERE):
            query_made[piece, :, pl.ds(head * HDIM, HDIM)] = (
                sums[head, :, pl.ds(piece * ROWS_HERE, ROWS_HERE)].T * (root * SCORE_SCALE)
            ).astype(bf16)
        send = pltpu.make_async_copy(query_made.at[piece], query_out[piece], query_sent.at[piece])
        send.start()
        sends.append(send)
    for send in sends:
        send.wait()


def weight_kernel(parts_ref, out_ref):
    out_ref[...] = sum(parts_ref[source].astype(f32) for source in range(4)).astype(bf16)


def sum_kernel(parts_ref, *refs):
    pair_refs, query_refs = refs[:GRID], refs[GRID : 2 * GRID]
    query_out, key_out, value_out, weight_out = refs[2 * GRID :]
    weight_out[...] = sum(parts_ref[source].astype(f32) for source in range(GRID))
    query_out[0] = sum(ref[...].astype(f32) for ref in query_refs).astype(bf16)
    for place, out_ref in enumerate((key_out, value_out)):
        out_ref[0] = sum(ref[place].astype(f32) for ref in pair_refs).astype(bf16)


def call(kernel, out_shape, in_specs, scratch=(), out_spec=None, limit=56):
    return pl.pallas_call(
        kernel,
        out_shape=out_shape,
        in_specs=in_specs,
        out_specs=out_spec or jax.tree.map(lambda _: VMEM, out_shape),
        scratch_shapes=list(scratch),
        compiler_params=pltpu.CompilerParams(vmem_limit_bytes=limit * MIB),
        cost_estimate=pl.CostEstimate(flops=10**6, bytes_accessed=10**5, transcendentals=0),
    )


VMEM = pl.BlockSpec(memory_space=pltpu.VMEM)
SMEM = pl.BlockSpec(memory_space=pltpu.SMEM)
ANY = pl.BlockSpec(memory_space=pl.ANY)
HELD = [pltpu.VMEM((GRID, ROWS_HERE, FEATS), bf16)]
ARRIVED = [pltpu.SemaphoreType.DMA((GRID,))]


def shape(dims, dtype):
    return jax.ShapeDtypeStruct(dims, dtype)


def from_ahead(block, axis, step):
    return lax.ppermute(block, axis, [(i, (i - step) % GRID) for i in range(GRID)])


def to_ahead(block, axis, step):
    return lax.ppermute(block, axis, [(i, (i + step) % GRID) for i in range(GRID)])


def gather(block, axis):
    return [block] + [from_ahead(block, axis, step) for step in range(1, GRID)]


def per_device(
    vit_cot,
    vit_pre,
    ln_gain,
    patch_w,
    frame_owner,
    conv_w,
    join_w,
    token_order,
    queries,
    keys,
    values,
    attn_out,
    out_w,
):
    key_value = jnp.concatenate([keys[0], values[0]], axis=1)
    query_out = jnp.concatenate([queries[0], attn_out[0]], axis=1)
    sides = [from_ahead(key_value, "hx", step) for step in (1, 3)]
    sides += [from_ahead(query_out, "hy", step) for step in (1, 3)]
    windows = call(
        window_kernel,
        shape((FRAMES, 16, LANES), bf16),
        [VMEM] * 2 + [ANY] * 5,
        scratch=[
            pltpu.VMEM(vit_cot.shape[2:], bf16),
            pltpu.VMEM(vit_pre.shape[2:], bf16),
            pltpu.VMEM(patch_w.shape, bf16),
            pltpu.VMEM((LANES, patch_w.shape[0]), bf16),
            pltpu.VMEM((6 * LANES, LANES), bf16),
            pltpu.VMEM((SIDE * SIDE + 16, LANES), f32),
            pltpu.SemaphoreType.DMA((5,)),
        ],
    )(
        ln_gain,
        token_order,
        vit_pre[0, 0],
        vit_cot[0, 0],
        jnp.asarray(basis_matrix(), bf16),
        patch_w,
        jnp.asarray(spread_matrix(), bf16),
    )
    windows, join_w, key_value, query_out, sides = lax.optimization_barrier(
        (windows, join_w, key_value, query_out, sides)
    )
    key_values = [key_value, sides[0], from_ahead(key_value, "hx", 2), sides[1]]
    query_outs = [query_out, sides[2], from_ahead(query_out, "hy", 2), sides[3]]
    joint, picked = call(
        weights_kernel,
        (shape((QUARTERS * LANES, FEATS), bf16), shape((768, QUARTERS * LANES), bf16)),
        [ANY] * 2,
        scratch=[
            pltpu.VMEM(join_w.shape, bf16),
            pltpu.VMEM(out_w.shape, bf16),
            pltpu.SemaphoreType.DMA((2,)),
        ],
    )(join_w, out_w)
    windows, joint, picked, key_values, query_outs = lax.optimization_barrier(
        (windows, joint, picked, key_values, query_outs)
    )
    received = lax.all_to_all(
        windows, ("tm", "hx", "hy"), split_axis=0, concat_axis=0, tiled=True
    )
    totals = call(
        totals_kernel,
        shape((8, BLOCK), f32),
        [VMEM] * (2 * GRID),
        limit=24,
    )(*query_outs, *key_values)
    total_pieces = gather(totals, "hy")
    total_pieces, received = lax.optimization_barrier((total_pieces, received))
    row_dots, grad_out, weight_part = call(
        token_kernel,
        (
            shape((8, BLOCK), f32),
            shape((GRID, ROWS_HERE, FEATS), bf16),
            shape((768, FEATS), bf16),
        ),
        [SMEM, VMEM] + [ANY] * (3 + GRID),
        scratch=[
            pltpu.VMEM((FRAMES + 2, 16, LANES), bf16),
            pltpu.VMEM((3 * LANES, QUARTERS * LANES), bf16),
            pltpu.VMEM((BLOCK, QUARTERS * LANES), bf16),
            pltpu.VMEM((FRAMES, 16, LANES), bf16),
            pltpu.VMEM((QUARTERS * LANES, FEATS), bf16),
            pltpu.VMEM((768, QUARTERS * LANES), bf16),
            pltpu.VMEM((768, FEATS), bf16),
        ]
        + HELD * 2
        + [pltpu.SemaphoreType.DMA((3,))]
        + ARRIVED * 2
        + [pltpu.SemaphoreType.DMA((1,))],
        out_spec=(VMEM, ANY, ANY),
        limit=56,
    )(frame_owner, conv_w, received, joint, picked, *query_outs)
    outs = call(
        grads_kernel,
        tuple([shape((ROWS_HERE, FEATS), bf16)] * GRID)
        + tuple([shape((2, ROWS_HERE, FEATS), bf16)] * GRID),
        [VMEM] * (1 + GRID) + [ANY] * (1 + 2 * GRID),
        scratch=[pltpu.VMEM((HEADS_HERE, HDIM, BLOCK), f32)]
        + HELD * 5
        + [pltpu.VMEM((GRID, 2, ROWS_HERE, FEATS), bf16)]
        + ARRIVED * 3
        + [pltpu.SemaphoreType.DMA((1,))]
        + ARRIVED * 2,
        out_spec=tuple([ANY] * (2 * GRID)),
        limit=56,
    )(row_dots, *total_pieces, grad_out, *query_outs, *key_values)
    query_parts, pair_parts = outs[:GRID], outs[GRID:]
    weight_parts = lax.all_to_all(
        weight_part.reshape(4, 4 * 48, FEATS),
        ("zh", "core"),
        split_axis=0,
        concat_axis=0,
        tiled=True,
    )
    weight_blocks = call(weight_kernel, shape((4 * 48, FEATS), bf16), [VMEM], limit=8)(weight_parts)
    weight_parts = lax.all_to_all(
        weight_blocks.reshape(4, 48, FEATS), "hx", split_axis=0, concat_axis=0, tiled=True
    )
    pair_back = [pair_parts[0]] + [
        to_ahead(pair_parts[step], "hx", step) for step in range(1, GRID)
    ]
    query_back = [query_parts[0]] + [
        to_ahead(query_parts[step], "hy", step) for step in range(1, GRID)
    ]

    rows = shape((1, ROWS_HERE, FEATS), bf16)
    return call(
        sum_kernel,
        (rows, rows, rows, shape((48, FEATS), f32)),
        [VMEM] * (1 + 2 * GRID),
        limit=16,
    )(weight_parts, *pair_back, *query_back)


def solution(mesh):
    fine = Mesh(
        mesh.devices.reshape(2, 2, GRID, GRID, GRID), ("zh", "core", "tm", "hx", "hy")
    )
    dp, height = ("zh", "core"), ("hx", "hy")
    rows = P(dp, height, "tm")
    slots = P(dp, ("tm",) + height, None, None)
    placed = (
        slots,
        slots,
        P(),
        P(),
        P(),
        P(),
        P(),
        P(height, "tm"),
        rows,
        rows,
        rows,
        rows,
        P("tm", None),
    )
    return jax.shard_map(
        per_device,
        mesh=fine,
        in_specs=placed,
        out_specs=(rows, rows, rows, P(dp + height, "tm")),
        check_vma=False,
    )
```

```python
import functools
import math

import jax
import jax.numpy as jnp
import numpy as np
from jax import lax
from jax.experimental import pallas as pl
from jax.experimental.pallas import tpu as pltpu
from jax.sharding import Mesh
from jax.sharding import PartitionSpec as P

HDIM = 128
IMG = 224
PATCH = 14
SIDE = IMG // PATCH
GRID = 4
HEADS_HERE = 3
ROWS_HERE = 256
FEATS = HEADS_HERE * HDIM
BLOCK = GRID * ROWS_HERE
FRAMES = 64
LANES = 128
QUARTERS = 4
QUARTER_LANES = 32
TAPS = 27
ORDER_LANE = TAPS
QUARTER_CELLS = (PATCH // 2) * (2 * PATCH)

epsilon = 1e-05
pixel_std = (0.26862954, 0.26130258, 0.27577711)

f32 = jnp.float32
bf16 = jnp.bfloat16
MIB = 1024 * 1024
HIGHEST = lax.Precision.HIGHEST
LOG2E = math.log2(math.e)
SCORE_SCALE = HDIM ** (-0.5)


def row_masks():
    masks = np.zeros((8, PATCH), np.float32)
    for half in range(2):
        for shift in range(3):
            low = half * 7 + shift - 1
            masks[half * 3 + shift, max(low, 0) : min(low + 7, PATCH)] = 1
    masks[6, 0] = 1
    masks[7, PATCH - 1] = 1
    return masks


def basis_matrix():
    rows = row_masks()
    columns = np.zeros((3, PATCH), np.float32)
    columns[0] = 1
    columns[1, 0] = 1
    columns[2, PATCH - 1] = 1
    basis = np.zeros((LANES, 3, PATCH, PATCH), np.float32)
    for col in range(3):
        for row in range(8):
            for channel in range(3):
                basis[col * 24 + row * 3 + channel, channel] = np.outer(rows[row], columns[col])
    return basis.reshape(LANES, 3 * PATCH * PATCH)


def spread_matrix():
    spread = np.zeros((6, LANES, LANES), np.float32)
    for half in range(2):
        for side in range(2):
            first = 2 * side + 1
            terms = {
                0: [(first - 1, 2, 1), (first, 0, 1), (first + 1, 0, 1), (first + 1, 2, -1)],
                1: [(first, 0, 1), (first + 1, 0, 1)],
                2: [(first, 0, 1), (first, 1, -1), (first + 1, 0, 1), (first + 2, 1, 1)],
            }
            for shift in range(3):
                groups = [half * 3 + shift]
                if (half, shift) == (0, 0):
                    groups.append(7)
                if (half, shift) == (1, 2):
                    groups.append(6)
                for offset in range(3):
                    for channel in range(3):
                        lane = (half * 2 + side) * QUARTER_LANES + (shift * 3 + offset) * 3 + channel
                        for place, col, sign in terms[offset]:
                            for row in groups:
                                spread[place, col * 24 + row * 3 + channel, lane] += sign
    return spread.reshape(6 * LANES, LANES)


NN = (((1,), (0,)), ((), ()))
NT = (((1,), (1,)), ((), ()))
TN = (((0,), (0,)), ((), ()))


def dot(left, right, dims=NN):
    return lax.dot_general(left, right, dims, preferred_element_type=f32)


def one_hot(condition):
    return jnp.where(condition, 1.0, 0.0).astype(bf16)


def iota(dims, axis):
    return lax.broadcasted_iota(jnp.int32, dims, axis)


def start(copies):
    for copy in copies:
        copy.start()


def fetch(refs, held, arrived):
    copies = [
        pltpu.make_async_copy(ref, kept, arrived.at[place])
        for place, (ref, kept) in enumerate(zip(refs, held))
    ]
    start(copies)
    return copies


def fetch_halves(refs, column, held, arrived):
    return fetch(
        [ref.at[:, pl.ds(column * FEATS, FEATS)] for ref in refs],
        [held.at[place] for place in range(len(refs))],
        arrived,
    )


def window_kernel(gain_ref, order_ref, *refs):
    out_ref, cot_ref, pre_ref, patch_ref, basis_ref, spread_ref, sums, arrived = refs[5:]
    held = (pre_ref, cot_ref, basis_ref, patch_ref, spread_ref)
    copies = fetch(refs[:5], held, arrived)
    copies[0].wait()
    copies[1].wait()
    pre = pre_ref[...].astype(f32)
    centered = pre - jnp.mean(pre, axis=-1, keepdims=True)
    inverse = lax.rsqrt(jnp.mean(centered * centered, axis=-1, keepdims=True) + epsilon)
    normed = centered * inverse
    scaled = cot_ref[...].astype(f32) * gain_ref[...].astype(f32).reshape(1, -1)
    grad_rows = inverse * (
        scaled
        - jnp.mean(scaled, axis=-1, keepdims=True)
        - normed * jnp.mean(scaled * normed, axis=-1, keepdims=True)
    )
    grad_rows = grad_rows.astype(bf16)
    channel = iota((LANES, 1), 0) % 3
    scale = jnp.where(
        channel == 0, 1.0 / pixel_std[0], jnp.where(channel == 1, 1.0 / pixel_std[1], 1.0 / pixel_std[2])
    ) * (1.0 / QUARTER_CELLS)
    copies[2].wait()
    copies[3].wait()
    weights = dot(basis_ref[...], patch_ref[...]) * scale
    high = weights.astype(bf16)
    low = (weights - high.astype(f32)).astype(bf16)
    both = dot(grad_rows, jnp.concatenate([high, low], axis=0), NT)
    patch_sums = both[:, :LANES] + both[:, LANES:]
    group = (iota((SIDE * SIDE, LANES), 1) // 3) % 8
    edge = jnp.zeros((SIDE, LANES), f32)
    above = jnp.concatenate([edge, patch_sums[:-SIDE]], axis=0)
    below = jnp.concatenate([patch_sums[SIDE:], edge], axis=0)
    patch_sums = jnp.where(group == 7, above, jnp.where(group == 6, below, patch_sums))
    sums[pl.ds(0, 8), :] = jnp.zeros((8, LANES), f32)
    sums[pl.ds(8 + SIDE * SIDE, 8), :] = jnp.zeros((8, LANES), f32)
    sums[pl.ds(8, SIDE * SIDE), :] = patch_sums
    copies[4].wait()
    column = iota((SIDE * GRID, LANES), 0) % GRID
    total = jnp.zeros((SIDE * GRID, LANES), f32)
    for place in range(6):
        picked = sums[pl.ds(7 + place, SIDE * GRID, stride=GRID), :]
        if place == 0:
            picked = jnp.where(column == 0, 0.0, picked)
        if place == 5:
            picked = jnp.where(column == GRID - 1, 0.0, picked)
        high = picked.astype(bf16)
        low = (picked - high.astype(f32)).astype(bf16)
        both = dot(
            jnp.concatenate([high, low], axis=0), spread_ref[pl.ds(place * LANES, LANES), :]
        )
        total = total + (both[: SIDE * GRID] + both[SIDE * GRID :])
    windows = total.astype(bf16)
    entries = jnp.where(
        iota((16, 64), 1) % 16 == iota((16, 64), 0), order_ref[...].astype(f32), 0.0
    ).astype(bf16)
    order = dot(entries, one_hot(iota((64, LANES), 1) == ORDER_LANE + iota((64, LANES), 0) // 16))
    order = order.astype(bf16)
    for target_x in range(GRID):
        block = windows[target_x * 16 : (target_x + 1) * 16] + order
        for target_t in range(GRID):
            for target_y in range(GRID):
                out_ref[(target_t * GRID + target_x) * GRID + target_y] = block


def weights_kernel(join_from, out_w_from, joint_ref, picked_ref, join_ref, out_w_ref, arrived):
    here_y = lax.axis_index("hy")
    copies = fetch([join_from, out_w_from], [join_ref, out_w_ref], arrived)
    copies[0].wait()
    copies[1].wait()
    joint_ref[...] = dot(join_ref[...], out_w_ref[...], NT).astype(bf16)
    row, column = iota((96, 384), 0), iota((96, 384), 1)
    half = row // 48
    pick = one_hot(column == half * 192 + here_y * 48 + (row - half * 48))
    for pair in range(8):
        rows = dot(pick, join_ref[:, pl.ds(pair * 384, 384)], NT).astype(bf16)
        z, core, x = pair // 4, (pair % 4) // 2, (pair % 2) * 2
        for step in range(2):
            picked_ref[pl.ds((core * 2 + z) * 192 + (x + step) * 48, 48), :] = rows[
                step * 48 : (step + 1) * 48
            ]


def totals_kernel(*refs):
    query_refs, key_refs, out_ref = refs[:GRID], refs[GRID : 2 * GRID], refs[2 * GRID]
    for head in range(HEADS_HERE):
        columns = pl.ds(head * HDIM, HDIM)
        for piece in range(GRID):
            query = query_refs[piece][:, columns]
            scores = [dot(key_ref[:, columns], query, NT) for key_ref in key_refs]
            top = functools.reduce(
                jnp.maximum, [jnp.max(tile, axis=0, keepdims=True) for tile in scores]
            ) * (SCORE_SCALE * LOG2E)
            total = sum(
                jnp.sum(jnp.exp2(tile * (SCORE_SCALE * LOG2E) - top), axis=0, keepdims=True)
                for tile in scores
            )
            out_ref[pl.ds(head, 1), pl.ds(piece * ROWS_HERE, ROWS_HERE)] = top + jnp.log2(total)
    out_ref[pl.ds(HEADS_HERE, 8 - HEADS_HERE), :] = jnp.zeros((8 - HEADS_HERE, BLOCK), f32)


def token_part(owner_ref, conv_ref, recv_ref, arrivals, frames, conv_big, ordered):
    here_x = lax.axis_index("hx")
    here_y = lax.axis_index("hy")
    frames[0] = jnp.zeros((16, LANES), bf16)
    frames[FRAMES + 1] = jnp.zeros((16, LANES), bf16)
    row, column = iota((3 * QUARTER_LANES, 3 * TAPS), 0), iota((3 * QUARTER_LANES, 3 * TAPS), 1)
    tap = row % QUARTER_LANES
    conv = dot(
        one_hot((tap < TAPS) & (column == (row // QUARTER_LANES) * TAPS + tap)), conv_ref[...]
    ).astype(bf16)
    conv_big[...] = jnp.zeros_like(conv_big)
    for quarter in range(QUARTERS):
        for shift in range(3):
            conv_big[
                pl.ds(shift * LANES + quarter * QUARTER_LANES, QUARTER_LANES),
                pl.ds(quarter * LANES, LANES),
            ] = conv[shift * QUARTER_LANES : (shift + 1) * QUARTER_LANES]
    arrivals.wait()

    def place_frame(frame, carry):
        frames[frame + 1] = recv_ref[(frame // 16) * 16 + owner_ref[frame]]
        return carry

    lax.fori_loop(0, FRAMES, place_frame, 0, unroll=8)
    lane = iota((16, ROWS_HERE), 1)
    for slab_t in range(GRID):
        pooled = sum(
            dot(
                frames[pl.ds(slab_t * 16 + shift, 16)].reshape(ROWS_HERE, LANES),
                conv_big[pl.ds(shift * LANES, LANES), :],
            )
            for shift in range(3)
        ).astype(bf16)
        pieces = []
        for piece in range(GRID):
            slab = lax.rem(here_y + piece, GRID)
            block = recv_ref[slab_t * 16 + here_x * GRID + slab].astype(f32)
            for part in range(4):
                order = block[:, ORDER_LANE + part : ORDER_LANE + part + 1].astype(jnp.int32)
                target = (order // 4) * 16 + slab * 4 + lax.rem(order, 4)
                pieces.append(one_hot(lane == target))
        chosen = dot(jnp.concatenate(pieces, axis=0), pooled).astype(bf16)
        for piece in range(GRID):
            ordered[pl.ds(piece * ROWS_HERE + slab_t * 64, 64), :] = chosen[
                piece * 64 : (piece + 1) * 64
            ]


def grads_kernel(owner_ref, conv_ref, *refs):
    total_refs, (recv_from, joint_from, picked_from) = refs[:GRID], refs[GRID : GRID + 3]
    query_refs, pair_refs = refs[GRID + 3 : 2 * GRID + 3], refs[2 * GRID + 3 : 3 * GRID + 3]
    rest = refs[3 * GRID + 3 :]
    query_out, pair_out = rest[:GRID], rest[GRID : 2 * GRID]
    weight_outs = rest[2 * GRID : 2 * GRID + 2]
    (
        frames,
        conv_big,
        ordered,
        recv_ref,
        joint_ref,
        picked_ref,
        weight_made,
        dots_ref,
        sums,
        out_held,
        query_held,
        key_held,
        value_held,
        grad_ref,
        query_made,
        pair_made,
        first_arrived,
        out_arrived,
        query_arrived,
        key_arrived,
        value_arrived,
        query_sent,
        pair_sent,
        weight_sent,
    ) = rest[2 * GRID + 2 :]
    sends_order = (2, 1, 3, 0)
    firsts = fetch(
        [recv_from, joint_from, picked_from], [recv_ref, joint_ref, picked_ref], first_arrived
    )
    out_copies = fetch_halves(query_refs, 1, out_held, out_arrived)
    query_copies = fetch_halves(query_refs, 0, query_held, query_arrived)
    key_copies = fetch_halves(pair_refs, 0, key_held, key_arrived)
    value_copies = fetch_halves(pair_refs, 1, value_held, value_arrived)
    token_part(owner_ref, conv_ref, recv_ref, firsts[0], frames, conv_big, ordered)
    firsts[1].wait()
    ones = jnp.ones((8, 2 * HDIM), bf16)
    outer = jnp.zeros((QUARTERS * LANES, FEATS), f32)
    for piece in range(GRID):
        rows = ordered[pl.ds(piece * ROWS_HERE, ROWS_HERE), :]
        grads = dot(rows, joint_ref[...]).astype(bf16)
        grad_ref[piece] = grads
        out_copies[piece].wait()
        outs = out_held[piece]
        products = grads.astype(f32) * outs.astype(f32)
        high = products.astype(bf16)
        low = (products - high.astype(f32)).astype(bf16)
        for head in range(HEADS_HERE):
            columns = slice(head * HDIM, (head + 1) * HDIM)
            both = jnp.concatenate([high[:, columns], low[:, columns]], axis=1)
            dots_ref[head, :, pl.ds(piece * ROWS_HERE, ROWS_HERE)] = dot(ones, both, NT)
        outer = outer + dot(rows, outs, TN)
    firsts[2].wait()
    weight_made[...] = (
        dot(picked_ref[...], outer.astype(bf16)) * (1.0 / math.sqrt(FRAMES * 64 * 4))
    ).astype(bf16)
    here_core = lax.axis_index("core")
    sends = fetch(
        [
            weight_made.at[pl.ds(pl.multiple_of(half * 384, 384), 384)]
            for half in (here_core, 1 - here_core)
        ],
        weight_outs,
        weight_sent,
    )
    root = math.sqrt(FRAMES * 64)
    totals = []
    for piece in range(GRID):
        parts = [
            total_refs[step][:, pl.ds(((piece - step) % GRID) * ROWS_HERE, ROWS_HERE)]
            for step in range(GRID)
        ]
        top = functools.reduce(jnp.maximum, parts)
        totals.append(top + jnp.log2(sum(jnp.exp2(part - top) for part in parts)))
    totals = jnp.concatenate(totals, axis=1)
    for copy in query_copies:
        copy.wait()
    for other in sends_order:
        key_copies[other].wait()
        value_copies[other].wait()
        for head in range(HEADS_HERE):
            columns = pl.ds(head * HDIM, HDIM)
            query = query_held[:, :, columns].reshape(BLOCK, HDIM)
            grad = grad_ref[:, :, columns].reshape(BLOCK, HDIM)
            key = key_held[other, :, columns]
            value = value_held[other, :, columns]
            weights = jnp.exp2(
                dot(key, query, NT) * (SCORE_SCALE * LOG2E) - totals[head : head + 1]
            )
            dscore = (weights * (dot(value, grad, NT) - dots_ref[head, 0:1, :])).astype(bf16)
            pair_made[other, 1, :, columns] = (dot(weights.astype(bf16), grad) * root).astype(bf16)
            pair_made[other, 0, :, columns] = (
                dot(dscore, query) * (root * SCORE_SCALE)
            ).astype(bf16)
            part = dot(key.T, dscore)
            if other == sends_order[0]:
                sums[head] = part
            else:
                sums[head] += part
        send = pltpu.make_async_copy(pair_made.at[other], pair_out[other], pair_sent.at[other])
        send.start()
        sends.append(send)
    for piece in sends_order:
        for head in range(HEADS_HERE):
            query_made[piece, :, pl.ds(head * HDIM, HDIM)] = (
                sums[head, :, pl.ds(piece * ROWS_HERE, ROWS_HERE)].T * (root * SCORE_SCALE)
            ).astype(bf16)
        send = pltpu.make_async_copy(query_made.at[piece], query_out[piece], query_sent.at[piece])
        send.start()
        sends.append(send)
    for send in sends:
        send.wait()


def half_kernel(kept_ref, got_ref, kept_out, sent_out):
    here_z = lax.axis_index("zh")
    for out_ref, half in ((kept_out, here_z), (sent_out, 1 - here_z)):
        rows = pl.ds(pl.multiple_of(half * 192, 192), 192)
        out_ref[...] = (kept_ref[rows, :].astype(f32) + got_ref[rows, :].astype(f32)).astype(
            out_ref.dtype
        )


def weight_kernel(kept_ref, got_ref, out_ref):
    out_ref[...] = (kept_ref[...] + got_ref[...].astype(f32)).astype(bf16)


def sum_kernel(parts_ref, *refs):
    pair_refs, query_refs = refs[:GRID], refs[GRID : 2 * GRID]
    query_out, key_out, value_out, weight_out = refs[2 * GRID :]
    weight_out[...] = sum(parts_ref[source].astype(f32) for source in range(GRID))
    query_out[0] = sum(ref[...].astype(f32) for ref in query_refs).astype(bf16)
    for place, out_ref in enumerate((key_out, value_out)):
        out_ref[0] = sum(ref[place].astype(f32) for ref in pair_refs).astype(bf16)


def call(kernel, out_shape, in_specs, scratch=(), out_spec=None, limit=56):
    return pl.pallas_call(
        kernel,
        out_shape=out_shape,
        in_specs=in_specs,
        out_specs=jax.tree.map(lambda _: out_spec or VMEM, out_shape),
        scratch_shapes=list(scratch),
        compiler_params=pltpu.CompilerParams(vmem_limit_bytes=limit * MIB),
        cost_estimate=pl.CostEstimate(flops=10**6, bytes_accessed=10**5, transcendentals=0),
    )


VMEM = pl.BlockSpec(memory_space=pltpu.VMEM)
SMEM = pl.BlockSpec(memory_space=pltpu.SMEM)
ANY = pl.BlockSpec(memory_space=pl.ANY)
HELD = [pltpu.VMEM((GRID, ROWS_HERE, FEATS), bf16)]
ARRIVED = [pltpu.SemaphoreType.DMA((GRID,))]


def shape(dims, dtype):
    return jax.ShapeDtypeStruct(dims, dtype)


def from_ahead(block, axis, step):
    return lax.ppermute(block, axis, [(i, (i - step) % GRID) for i in range(GRID)])


def to_ahead(block, axis, step):
    return lax.ppermute(block, axis, [(i, (i + step) % GRID) for i in range(GRID)])


def gather(block, axis):
    return [block] + [from_ahead(block, axis, step) for step in range(1, GRID)]


def per_device(
    vit_cot,
    vit_pre,
    ln_gain,
    patch_w,
    frame_owner,
    conv_w,
    join_w,
    token_order,
    queries,
    keys,
    values,
    attn_out,
    out_w,
):
    key_value = jnp.concatenate([keys[0], values[0]], axis=1)
    query_out = jnp.concatenate([queries[0], attn_out[0]], axis=1)
    sides = [from_ahead(key_value, "hx", step) for step in (1, 3)]
    sides += [from_ahead(query_out, "hy", step) for step in (1, 3)]
    windows = call(
        window_kernel,
        shape((FRAMES, 16, LANES), bf16),
        [VMEM] * 2 + [ANY] * 5,
        scratch=[
            pltpu.VMEM(vit_cot.shape[2:], bf16),
            pltpu.VMEM(vit_pre.shape[2:], bf16),
            pltpu.VMEM(patch_w.shape, bf16),
            pltpu.VMEM((LANES, patch_w.shape[0]), bf16),
            pltpu.VMEM((6 * LANES, LANES), bf16),
            pltpu.VMEM((SIDE * SIDE + 16, LANES), f32),
            pltpu.SemaphoreType.DMA((5,)),
        ],
    )(
        ln_gain,
        token_order,
        vit_pre[0, 0],
        vit_cot[0, 0],
        jnp.asarray(basis_matrix(), bf16),
        patch_w,
        jnp.asarray(spread_matrix(), bf16),
    )
    windows, join_w, key_value, query_out, sides = lax.optimization_barrier(
        (windows, join_w, key_value, query_out, sides)
    )
    key_values = [key_value, sides[0], from_ahead(key_value, "hx", 2), sides[1]]
    query_outs = [query_out, sides[2], from_ahead(query_out, "hy", 2), sides[3]]
    joint, picked = call(
        weights_kernel,
        (shape((QUARTERS * LANES, FEATS), bf16), shape((768, QUARTERS * LANES), bf16)),
        [ANY] * 2,
        scratch=[
            pltpu.VMEM(join_w.shape, bf16),
            pltpu.VMEM(out_w.shape, bf16),
            pltpu.SemaphoreType.DMA((2,)),
        ],
    )(join_w, out_w)
    windows, joint, picked, key_values, query_outs = lax.optimization_barrier(
        (windows, joint, picked, key_values, query_outs)
    )
    received = lax.all_to_all(
        windows, ("tm", "hx", "hy"), split_axis=0, concat_axis=0, tiled=True
    )
    totals = call(
        totals_kernel,
        shape((8, BLOCK), f32),
        [VMEM] * (2 * GRID),
        limit=24,
    )(*query_outs, *key_values)
    total_pieces = gather(totals, "hy")
    outs = call(
        grads_kernel,
        tuple([shape((ROWS_HERE, FEATS), bf16)] * GRID)
        + tuple([shape((2, ROWS_HERE, FEATS), bf16)] * GRID)
        + (shape((384, FEATS), bf16),) * 2,
        [SMEM] + [VMEM] * (1 + GRID) + [ANY] * (3 + 2 * GRID),
        scratch=[
            pltpu.VMEM((FRAMES + 2, 16, LANES), bf16),
            pltpu.VMEM((3 * LANES, QUARTERS * LANES), bf16),
            pltpu.VMEM((BLOCK, QUARTERS * LANES), bf16),
            pltpu.VMEM((FRAMES, 16, LANES), bf16),
            pltpu.VMEM((QUARTERS * LANES, FEATS), bf16),
            pltpu.VMEM((768, QUARTERS * LANES), bf16),
            pltpu.VMEM((768, FEATS), bf16),
            pltpu.VMEM((HEADS_HERE, 8, BLOCK), f32),
            pltpu.VMEM((HEADS_HERE, HDIM, BLOCK), f32),
        ]
        + HELD * 6
        + [pltpu.VMEM((GRID, 2, ROWS_HERE, FEATS), bf16), pltpu.SemaphoreType.DMA((3,))]
        + ARRIVED * 6
        + [pltpu.SemaphoreType.DMA((2,))],
        out_spec=ANY,
        limit=56,
    )(frame_owner, conv_w, *total_pieces, received, joint, picked, *query_outs, *key_values)
    query_parts, pair_parts = outs[:GRID], outs[GRID : 2 * GRID]
    weight_kept, weight_sent = outs[2 * GRID :]
    weight_got = lax.ppermute(weight_sent, "core", [(0, 1), (1, 0)])
    weight_kept, weight_sent = call(
        half_kernel, (shape((192, FEATS), f32), shape((192, FEATS), bf16)), [VMEM] * 2, limit=8
    )(weight_kept, weight_got)
    weight_got = lax.ppermute(weight_sent, "zh", [(0, 1), (1, 0)])
    weight_blocks = call(weight_kernel, shape((192, FEATS), bf16), [VMEM] * 2, limit=8)(
        weight_kept, weight_got
    )
    weight_parts = lax.all_to_all(
        weight_blocks.reshape(4, 48, FEATS), "hx", split_axis=0, concat_axis=0, tiled=True
    )
    pair_back = [pair_parts[0]] + [
        to_ahead(pair_parts[step], "hx", step) for step in range(1, GRID)
    ]
    query_back = [query_parts[0]] + [
        to_ahead(query_parts[step], "hy", step) for step in range(1, GRID)
    ]

    rows = shape((1, ROWS_HERE, FEATS), bf16)
    return call(
        sum_kernel,
        (rows, rows, rows, shape((48, FEATS), f32)),
        [VMEM] * (1 + 2 * GRID),
        limit=16,
    )(weight_parts, *pair_back, *query_back)


def solution(mesh):
    fine = Mesh(
        mesh.devices.reshape(2, 2, GRID, GRID, GRID), ("zh", "core", "tm", "hx", "hy")
    )
    dp, height = ("zh", "core"), ("hx", "hy")
    rows = P(dp, height, "tm")
    slots = P(dp, ("tm",) + height, None, None)
    placed = (
        slots,
        slots,
        P(),
        P(),
        P(),
        P(),
        P(),
        P(height, "tm"),
        rows,
        rows,
        rows,
        rows,
        P("tm", None),
    )
    return jax.shard_map(
        per_device,
        mesh=fine,
        in_specs=placed,
        out_specs=(rows, rows, rows, P(dp + height, "tm")),
        check_vma=False,
    )
```

```python
import functools
import math

import jax
import jax.numpy as jnp
import numpy as np
from jax import lax
from jax.experimental import pallas as pl
from jax.experimental.pallas import tpu as pltpu
from jax.sharding import Mesh
from jax.sharding import PartitionSpec as P

HDIM = 128
IMG = 224
PATCH = 14
SIDE = IMG // PATCH
GRID = 4
HEADS_HERE = 3
ROWS_HERE = 256
FEATS = HEADS_HERE * HDIM
BLOCK = GRID * ROWS_HERE
FRAMES = 64
LANES = 128
QUARTERS = 4
QUARTER_LANES = 32
TAPS = 27
ORDER_LANE = TAPS
QUARTER_CELLS = (PATCH // 2) * (2 * PATCH)

epsilon = 1e-05
pixel_std = (0.26862954, 0.26130258, 0.27577711)

f32 = jnp.float32
bf16 = jnp.bfloat16
MIB = 1024 * 1024
HIGHEST = lax.Precision.HIGHEST
LOG2E = math.log2(math.e)
SCORE_SCALE = HDIM ** (-0.5)


def row_masks():
    masks = np.zeros((8, PATCH), np.float32)
    for half in range(2):
        for shift in range(3):
            low = half * 7 + shift - 1
            masks[half * 3 + shift, max(low, 0) : min(low + 7, PATCH)] = 1
    masks[6, 0] = 1
    masks[7, PATCH - 1] = 1
    return masks


def basis_matrix():
    rows = row_masks()
    columns = np.zeros((3, PATCH), np.float32)
    columns[0] = 1
    columns[1, 0] = 1
    columns[2, PATCH - 1] = 1
    basis = np.zeros((LANES, 3, PATCH, PATCH), np.float32)
    for col in range(3):
        for row in range(8):
            for channel in range(3):
                basis[col * 24 + row * 3 + channel, channel] = np.outer(rows[row], columns[col])
    return basis.reshape(LANES, 3 * PATCH * PATCH)


def spread_matrix():
    spread = np.zeros((6, LANES, LANES), np.float32)
    for half in range(2):
        for side in range(2):
            first = 2 * side + 1
            terms = {
                0: [(first - 1, 2, 1), (first, 0, 1), (first + 1, 0, 1), (first + 1, 2, -1)],
                1: [(first, 0, 1), (first + 1, 0, 1)],
                2: [(first, 0, 1), (first, 1, -1), (first + 1, 0, 1), (first + 2, 1, 1)],
            }
            for shift in range(3):
                groups = [half * 3 + shift]
                if (half, shift) == (0, 0):
                    groups.append(7)
                if (half, shift) == (1, 2):
                    groups.append(6)
                for offset in range(3):
                    for channel in range(3):
                        lane = (half * 2 + side) * QUARTER_LANES + (shift * 3 + offset) * 3 + channel
                        for place, col, sign in terms[offset]:
                            for row in groups:
                                spread[place, col * 24 + row * 3 + channel, lane] += sign
    return spread.reshape(6 * LANES, LANES)


NN = (((1,), (0,)), ((), ()))
NT = (((1,), (1,)), ((), ()))
TN = (((0,), (0,)), ((), ()))


def dot(left, right, dims=NN):
    return lax.dot_general(left, right, dims, preferred_element_type=f32)


def one_hot(condition):
    return jnp.where(condition, 1.0, 0.0).astype(bf16)


def iota(dims, axis):
    return lax.broadcasted_iota(jnp.int32, dims, axis)


def start(copies):
    for copy in copies:
        copy.start()


def fetch(refs, held, arrived):
    copies = [
        pltpu.make_async_copy(ref, kept, arrived.at[place])
        for place, (ref, kept) in enumerate(zip(refs, held))
    ]
    start(copies)
    return copies


def fetch_halves(refs, column, held, arrived):
    return fetch(
        [ref.at[:, pl.ds(column * FEATS, FEATS)] for ref in refs],
        [held.at[place] for place in range(len(refs))],
        arrived,
    )


def window_kernel(gain_ref, order_ref, *refs):
    out_ref, cot_ref, pre_ref, patch_ref, basis_ref, spread_ref, sums, arrived = refs[5:]
    held = (pre_ref, cot_ref, basis_ref, patch_ref, spread_ref)
    copies = fetch(refs[:5], held, arrived)
    copies[0].wait()
    copies[1].wait()
    pre = pre_ref[...].astype(f32)
    centered = pre - jnp.mean(pre, axis=-1, keepdims=True)
    inverse = lax.rsqrt(jnp.mean(centered * centered, axis=-1, keepdims=True) + epsilon)
    normed = centered * inverse
    scaled = cot_ref[...].astype(f32) * gain_ref[...].astype(f32).reshape(1, -1)
    grad_rows = inverse * (
        scaled
        - jnp.mean(scaled, axis=-1, keepdims=True)
        - normed * jnp.mean(scaled * normed, axis=-1, keepdims=True)
    )
    grad_rows = grad_rows.astype(bf16)
    channel = iota((LANES, 1), 0) % 3
    scale = jnp.where(
        channel == 0, 1.0 / pixel_std[0], jnp.where(channel == 1, 1.0 / pixel_std[1], 1.0 / pixel_std[2])
    ) * (1.0 / QUARTER_CELLS)
    copies[2].wait()
    copies[3].wait()
    weights = dot(basis_ref[...], patch_ref[...]) * scale
    high = weights.astype(bf16)
    low = (weights - high.astype(f32)).astype(bf16)
    both = dot(grad_rows, jnp.concatenate([high, low], axis=0), NT)
    patch_sums = both[:, :LANES] + both[:, LANES:]
    group = (iota((SIDE * SIDE, LANES), 1) // 3) % 8
    edge = jnp.zeros((SIDE, LANES), f32)
    above = jnp.concatenate([edge, patch_sums[:-SIDE]], axis=0)
    below = jnp.concatenate([patch_sums[SIDE:], edge], axis=0)
    patch_sums = jnp.where(group == 7, above, jnp.where(group == 6, below, patch_sums))
    sums[pl.ds(0, 8), :] = jnp.zeros((8, LANES), f32)
    sums[pl.ds(8 + SIDE * SIDE, 8), :] = jnp.zeros((8, LANES), f32)
    sums[pl.ds(8, SIDE * SIDE), :] = patch_sums
    copies[4].wait()
    column = iota((SIDE * GRID, LANES), 0) % GRID
    total = jnp.zeros((SIDE * GRID, LANES), f32)
    for place in range(6):
        picked = sums[pl.ds(7 + place, SIDE * GRID, stride=GRID), :]
        if place == 0:
            picked = jnp.where(column == 0, 0.0, picked)
        if place == 5:
            picked = jnp.where(column == GRID - 1, 0.0, picked)
        high = picked.astype(bf16)
        low = (picked - high.astype(f32)).astype(bf16)
        both = dot(
            jnp.concatenate([high, low], axis=0), spread_ref[pl.ds(place * LANES, LANES), :]
        )
        total = total + (both[: SIDE * GRID] + both[SIDE * GRID :])
    windows = total.astype(bf16)
    entries = jnp.where(
        iota((16, 64), 1) % 16 == iota((16, 64), 0), order_ref[...].astype(f32), 0.0
    ).astype(bf16)
    order = dot(entries, one_hot(iota((64, LANES), 1) == ORDER_LANE + iota((64, LANES), 0) // 16))
    order = order.astype(bf16)
    for target_x in range(GRID):
        block = windows[target_x * 16 : (target_x + 1) * 16] + order
        for target_t in range(GRID):
            for target_y in range(GRID):
                out_ref[(target_t * GRID + target_x) * GRID + target_y] = block


def weights_kernel(join_from, out_w_from, joint_ref, picked_ref, join_ref, out_w_ref, arrived):
    here_y = lax.axis_index("hy")
    copies = fetch([join_from, out_w_from], [join_ref, out_w_ref], arrived)
    copies[0].wait()
    copies[1].wait()
    joint_ref[...] = dot(join_ref[...], out_w_ref[...], NT).astype(bf16)
    row, column = iota((96, 384), 0), iota((96, 384), 1)
    half = row // 48
    pick = one_hot(column == half * 192 + here_y * 48 + (row - half * 48))
    for pair in range(8):
        rows = dot(pick, join_ref[:, pl.ds(pair * 384, 384)], NT).astype(bf16)
        z, core, x = pair // 4, (pair % 4) // 2, (pair % 2) * 2
        for step in range(2):
            picked_ref[pl.ds((core * 2 + z) * 192 + (x + step) * 48, 48), :] = rows[
                step * 48 : (step + 1) * 48
            ]


def totals_kernel(*refs):
    query_refs, key_refs, out_ref = refs[:GRID], refs[GRID : 2 * GRID], refs[2 * GRID]
    for head in range(HEADS_HERE):
        columns = pl.ds(head * HDIM, HDIM)
        for piece in range(GRID):
            query = query_refs[piece][:, columns]
            scores = [dot(key_ref[:, columns], query, NT) for key_ref in key_refs]
            top = functools.reduce(
                jnp.maximum, [jnp.max(tile, axis=0, keepdims=True) for tile in scores]
            ) * (SCORE_SCALE * LOG2E)
            total = sum(
                jnp.sum(jnp.exp2(tile * (SCORE_SCALE * LOG2E) - top), axis=0, keepdims=True)
                for tile in scores
            )
            out_ref[pl.ds(head, 1), pl.ds(piece * ROWS_HERE, ROWS_HERE)] = top + jnp.log2(total)
    out_ref[pl.ds(HEADS_HERE, 8 - HEADS_HERE), :] = jnp.zeros((8 - HEADS_HERE, BLOCK), f32)


def token_part(owner_ref, conv_ref, recv_ref, arrivals, frames, conv_big, ordered):
    here_x = lax.axis_index("hx")
    here_y = lax.axis_index("hy")
    frames[0] = jnp.zeros((16, LANES), bf16)
    frames[FRAMES + 1] = jnp.zeros((16, LANES), bf16)
    row, column = iota((3 * QUARTER_LANES, 3 * TAPS), 0), iota((3 * QUARTER_LANES, 3 * TAPS), 1)
    tap = row % QUARTER_LANES
    conv = dot(
        one_hot((tap < TAPS) & (column == (row // QUARTER_LANES) * TAPS + tap)), conv_ref[...]
    ).astype(bf16)
    conv_big[...] = jnp.zeros_like(conv_big)
    for quarter in range(QUARTERS):
        for shift in range(3):
            conv_big[
                pl.ds(shift * LANES + quarter * QUARTER_LANES, QUARTER_LANES),
                pl.ds(quarter * LANES, LANES),
            ] = conv[shift * QUARTER_LANES : (shift + 1) * QUARTER_LANES]
    arrivals.wait()

    def place_frame(frame, carry):
        frames[frame + 1] = recv_ref[(frame // 16) * 16 + owner_ref[frame]]
        return carry

    lax.fori_loop(0, FRAMES, place_frame, 0, unroll=8)
    lane = iota((16, ROWS_HERE), 1)
    for slab_t in range(GRID):
        pooled = sum(
            dot(
                frames[pl.ds(slab_t * 16 + shift, 16)].reshape(ROWS_HERE, LANES),
                conv_big[pl.ds(shift * LANES, LANES), :],
            )
            for shift in range(3)
        ).astype(bf16)
        pieces = []
        for piece in range(GRID):
            slab = lax.rem(here_y + piece, GRID)
            block = recv_ref[slab_t * 16 + here_x * GRID + slab].astype(f32)
            for part in range(4):
                order = block[:, ORDER_LANE + part : ORDER_LANE + part + 1].astype(jnp.int32)
                target = (order // 4) * 16 + slab * 4 + lax.rem(order, 4)
                pieces.append(one_hot(lane == target))
        chosen = dot(jnp.concatenate(pieces, axis=0), pooled).astype(bf16)
        for piece in range(GRID):
            ordered[pl.ds(piece * ROWS_HERE + slab_t * 64, 64), :] = chosen[
                piece * 64 : (piece + 1) * 64
            ]


def grads_kernel(owner_ref, conv_ref, *refs):
    total_refs, (recv_from, joint_from, picked_from) = refs[:GRID], refs[GRID : GRID + 3]
    query_refs, pair_refs = refs[GRID + 3 : 2 * GRID + 3], refs[2 * GRID + 3 : 3 * GRID + 3]
    rest = refs[3 * GRID + 3 :]
    query_out, pair_out = rest[:GRID], rest[GRID : 2 * GRID]
    weight_outs = rest[2 * GRID : 2 * GRID + 2]
    (
        frames,
        conv_big,
        ordered,
        recv_ref,
        joint_ref,
        picked_ref,
        weight_made,
        dots_ref,
        sums,
        out_held,
        query_held,
        key_held,
        value_held,
        grad_ref,
        query_made,
        pair_made,
        first_arrived,
        out_arrived,
        query_arrived,
        key_arrived,
        value_arrived,
        query_sent,
        pair_sent,
        weight_sent,
    ) = rest[2 * GRID + 2 :]
    sends_order = (2, 1, 3, 0)
    firsts = fetch(
        [recv_from, joint_from, picked_from], [recv_ref, joint_ref, picked_ref], first_arrived
    )
    out_copies = fetch_halves(query_refs, 1, out_held, out_arrived)
    query_copies = fetch_halves(query_refs, 0, query_held, query_arrived)
    key_copies = fetch_halves(pair_refs, 0, key_held, key_arrived)
    value_copies = fetch_halves(pair_refs, 1, value_held, value_arrived)
    token_part(owner_ref, conv_ref, recv_ref, firsts[0], frames, conv_big, ordered)
    firsts[1].wait()
    ones = jnp.ones((8, 2 * HDIM), bf16)
    outer = jnp.zeros((QUARTERS * LANES, FEATS), f32)
    for piece in range(GRID):
        rows = ordered[pl.ds(piece * ROWS_HERE, ROWS_HERE), :]
        grads = dot(rows, joint_ref[...]).astype(bf16)
        grad_ref[piece] = grads
        out_copies[piece].wait()
        outs = out_held[piece]
        products = grads.astype(f32) * outs.astype(f32)
        high = products.astype(bf16)
        low = (products - high.astype(f32)).astype(bf16)
        for head in range(HEADS_HERE):
            columns = slice(head * HDIM, (head + 1) * HDIM)
            both = jnp.concatenate([high[:, columns], low[:, columns]], axis=1)
            dots_ref[head, :, pl.ds(piece * ROWS_HERE, ROWS_HERE)] = dot(ones, both, NT)
        outer = outer + dot(rows, outs, TN)
    firsts[2].wait()
    weight_made[...] = (
        dot(picked_ref[...], outer.astype(bf16)) * (1.0 / math.sqrt(FRAMES * 64 * 4))
    ).astype(bf16)
    here_core = lax.axis_index("core")
    sends = fetch(
        [
            weight_made.at[pl.ds(pl.multiple_of(half * 384, 384), 384)]
            for half in (here_core, 1 - here_core)
        ],
        weight_outs,
        weight_sent,
    )
    root = math.sqrt(FRAMES * 64)
    totals = []
    for piece in range(GRID):
        parts = [
            total_refs[step][:, pl.ds(((piece - step) % GRID) * ROWS_HERE, ROWS_HERE)]
            for step in range(GRID)
        ]
        top = functools.reduce(jnp.maximum, parts)
        totals.append(top + jnp.log2(sum(jnp.exp2(part - top) for part in parts)))
    totals = jnp.concatenate(totals, axis=1)
    for copy in query_copies:
        copy.wait()
    for other in sends_order:
        key_copies[other].wait()
        value_copies[other].wait()
        for head in range(HEADS_HERE):
            columns = pl.ds(head * HDIM, HDIM)
            query = query_held[:, :, columns].reshape(BLOCK, HDIM)
            grad = grad_ref[:, :, columns].reshape(BLOCK, HDIM)
            key = key_held[other, :, columns]
            value = value_held[other, :, columns]
            weights = jnp.exp2(
                dot(key, query, NT) * (SCORE_SCALE * LOG2E) - totals[head : head + 1]
            )
            dscore = (weights * (dot(value, grad, NT) - dots_ref[head, 0:1, :])).astype(bf16)
            pair_made[other, 1, :, columns] = (dot(weights.astype(bf16), grad) * root).astype(bf16)
            pair_made[other, 0, :, columns] = (
                dot(dscore, query) * (root * SCORE_SCALE)
            ).astype(bf16)
            part = dot(key.T, dscore)
            if other == sends_order[0]:
                sums[head] = part
            else:
                sums[head] += part
        send = pltpu.make_async_copy(pair_made.at[other], pair_out[other], pair_sent.at[other])
        send.start()
        sends.append(send)
    for piece in sends_order:
        for head in range(HEADS_HERE):
            query_made[piece, :, pl.ds(head * HDIM, HDIM)] = (
                sums[head, :, pl.ds(piece * ROWS_HERE, ROWS_HERE)].T * (root * SCORE_SCALE)
            ).astype(bf16)
        send = pltpu.make_async_copy(query_made.at[piece], query_out[piece], query_sent.at[piece])
        send.start()
        sends.append(send)
    for send in sends:
        send.wait()


def half_kernel(kept_ref, got_ref, kept_out, sent_out):
    here_z = lax.axis_index("zh")
    for out_ref, half in ((kept_out, here_z), (sent_out, 1 - here_z)):
        rows = pl.ds(pl.multiple_of(half * 192, 192), 192)
        out_ref[...] = (kept_ref[rows, :].astype(f32) + got_ref[rows, :].astype(f32)).astype(
            out_ref.dtype
        )


def weight_kernel(kept_ref, got_ref, out_ref):
    out_ref[...] = (kept_ref[...] + got_ref[...].astype(f32)).astype(bf16)


def last_kernel(parts_ref, out_ref):
    out_ref[...] = sum(parts_ref[source].astype(f32) for source in range(GRID))


def sum_kernel(*refs):
    pair_refs, query_refs = refs[:GRID], refs[GRID : 2 * GRID]
    query_out, key_out, value_out = refs[2 * GRID :]
    query_out[0] = sum(ref[...].astype(f32) for ref in query_refs).astype(bf16)
    for place, out_ref in enumerate((key_out, value_out)):
        out_ref[0] = sum(ref[place].astype(f32) for ref in pair_refs).astype(bf16)


def call(kernel, out_shape, in_specs, scratch=(), out_spec=None, limit=56):
    return pl.pallas_call(
        kernel,
        out_shape=out_shape,
        in_specs=in_specs,
        out_specs=jax.tree.map(lambda _: out_spec or VMEM, out_shape),
        scratch_shapes=list(scratch),
        compiler_params=pltpu.CompilerParams(vmem_limit_bytes=limit * MIB),
        cost_estimate=pl.CostEstimate(flops=10**6, bytes_accessed=10**5, transcendentals=0),
    )


VMEM = pl.BlockSpec(memory_space=pltpu.VMEM)
SMEM = pl.BlockSpec(memory_space=pltpu.SMEM)
ANY = pl.BlockSpec(memory_space=pl.ANY)
HELD = [pltpu.VMEM((GRID, ROWS_HERE, FEATS), bf16)]
ARRIVED = [pltpu.SemaphoreType.DMA((GRID,))]


def shape(dims, dtype):
    return jax.ShapeDtypeStruct(dims, dtype)


def from_ahead(block, axis, step):
    return lax.ppermute(block, axis, [(i, (i - step) % GRID) for i in range(GRID)])


def to_ahead(block, axis, step):
    return lax.ppermute(block, axis, [(i, (i + step) % GRID) for i in range(GRID)])


def gather(block, axis):
    return [block] + [from_ahead(block, axis, step) for step in range(1, GRID)]


def per_device(
    vit_cot,
    vit_pre,
    ln_gain,
    patch_w,
    frame_owner,
    conv_w,
    join_w,
    token_order,
    queries,
    keys,
    values,
    attn_out,
    out_w,
):
    key_value = jnp.concatenate([keys[0], values[0]], axis=1)
    query_out = jnp.concatenate([queries[0], attn_out[0]], axis=1)
    sides = [from_ahead(key_value, "hx", step) for step in (1, 3)]
    sides += [from_ahead(query_out, "hy", step) for step in (1, 3)]
    windows = call(
        window_kernel,
        shape((FRAMES, 16, LANES), bf16),
        [VMEM] * 2 + [ANY] * 5,
        scratch=[
            pltpu.VMEM(vit_cot.shape[2:], bf16),
            pltpu.VMEM(vit_pre.shape[2:], bf16),
            pltpu.VMEM(patch_w.shape, bf16),
            pltpu.VMEM((LANES, patch_w.shape[0]), bf16),
            pltpu.VMEM((6 * LANES, LANES), bf16),
            pltpu.VMEM((SIDE * SIDE + 16, LANES), f32),
            pltpu.SemaphoreType.DMA((5,)),
        ],
    )(
        ln_gain,
        token_order,
        vit_pre[0, 0],
        vit_cot[0, 0],
        jnp.asarray(basis_matrix(), bf16),
        patch_w,
        jnp.asarray(spread_matrix(), bf16),
    )
    windows, join_w, key_value, query_out, sides = lax.optimization_barrier(
        (windows, join_w, key_value, query_out, sides)
    )
    key_values = [key_value, sides[0], from_ahead(key_value, "hx", 2), sides[1]]
    query_outs = [query_out, sides[2], from_ahead(query_out, "hy", 2), sides[3]]
    joint, picked = call(
        weights_kernel,
        (shape((QUARTERS * LANES, FEATS), bf16), shape((768, QUARTERS * LANES), bf16)),
        [ANY] * 2,
        scratch=[
            pltpu.VMEM(join_w.shape, bf16),
            pltpu.VMEM(out_w.shape, bf16),
            pltpu.SemaphoreType.DMA((2,)),
        ],
    )(join_w, out_w)
    windows, joint, picked, key_values, query_outs = lax.optimization_barrier(
        (windows, joint, picked, key_values, query_outs)
    )
    received = lax.all_to_all(
        windows, ("tm", "hx", "hy"), split_axis=0, concat_axis=0, tiled=True
    )
    totals = call(
        totals_kernel,
        shape((8, BLOCK), f32),
        [VMEM] * (2 * GRID),
        limit=24,
    )(*query_outs, *key_values)
    total_pieces = gather(totals, "hy")
    outs = call(
        grads_kernel,
        tuple([shape((ROWS_HERE, FEATS), bf16)] * GRID)
        + tuple([shape((2, ROWS_HERE, FEATS), bf16)] * GRID)
        + (shape((384, FEATS), bf16),) * 2,
        [SMEM] + [VMEM] * (1 + GRID) + [ANY] * (3 + 2 * GRID),
        scratch=[
            pltpu.VMEM((FRAMES + 2, 16, LANES), bf16),
            pltpu.VMEM((3 * LANES, QUARTERS * LANES), bf16),
            pltpu.VMEM((BLOCK, QUARTERS * LANES), bf16),
            pltpu.VMEM((FRAMES, 16, LANES), bf16),
            pltpu.VMEM((QUARTERS * LANES, FEATS), bf16),
            pltpu.VMEM((768, QUARTERS * LANES), bf16),
            pltpu.VMEM((768, FEATS), bf16),
            pltpu.VMEM((HEADS_HERE, 8, BLOCK), f32),
            pltpu.VMEM((HEADS_HERE, HDIM, BLOCK), f32),
        ]
        + HELD * 6
        + [pltpu.VMEM((GRID, 2, ROWS_HERE, FEATS), bf16), pltpu.SemaphoreType.DMA((3,))]
        + ARRIVED * 6
        + [pltpu.SemaphoreType.DMA((2,))],
        out_spec=ANY,
        limit=56,
    )(frame_owner, conv_w, *total_pieces, received, joint, picked, *query_outs, *key_values)
    query_parts, pair_parts = outs[:GRID], outs[GRID : 2 * GRID]
    weight_kept, weight_sent = outs[2 * GRID :]
    weight_got = lax.ppermute(weight_sent, "core", [(0, 1), (1, 0)])
    weight_kept, weight_sent = call(
        half_kernel, (shape((192, FEATS), f32), shape((192, FEATS), bf16)), [VMEM] * 2, limit=8
    )(weight_kept, weight_got)
    weight_got = lax.ppermute(weight_sent, "zh", [(0, 1), (1, 0)])
    weight_blocks = call(weight_kernel, shape((192, FEATS), bf16), [VMEM] * 2, limit=8)(
        weight_kept, weight_got
    )
    weight_parts = lax.all_to_all(
        weight_blocks.reshape(4, 48, FEATS), "hx", split_axis=0, concat_axis=0, tiled=True
    )
    pair_back = [pair_parts[0]] + [
        to_ahead(pair_parts[step], "hx", step) for step in range(1, GRID)
    ]
    query_back = [query_parts[0]] + [
        to_ahead(query_parts[step], "hy", step) for step in range(1, GRID)
    ]

    rows = shape((1, ROWS_HERE, FEATS), bf16)
    query_grad, key_grad, value_grad = call(
        sum_kernel, (rows, rows, rows), [VMEM] * (2 * GRID), limit=16
    )(*pair_back, *query_back)
    weight_grad = call(last_kernel, shape((48, FEATS), f32), [VMEM], limit=8)(weight_parts)
    return query_grad, key_grad, value_grad, weight_grad


def solution(mesh):
    fine = Mesh(
        mesh.devices.reshape(2, 2, GRID, GRID, GRID), ("zh", "core", "tm", "hx", "hy")
    )
    dp, height = ("zh", "core"), ("hx", "hy")
    rows = P(dp, height, "tm")
    slots = P(dp, ("tm",) + height, None, None)
    placed = (
        slots,
        slots,
        P(),
        P(),
        P(),
        P(),
        P(),
        P(height, "tm"),
        rows,
        rows,
        rows,
        rows,
        P("tm", None),
    )
    return jax.shard_map(
        per_device,
        mesh=fine,
        in_specs=placed,
        out_specs=(rows, rows, rows, P(dp + height, "tm")),
        check_vma=False,
    )
```
